32 devices in a mesh: seq: 4 (over y, core), dp: 8 (over z, x).
Axes of the slice: x: 2, y: 2, z: 4, core: 2. Of those that a mesh axis runs over, the one named last changes fastest.
Arguments:
- tokens: bfloat16 [8, 1024, 768], P('dp', 'seq'), may hold values from -6 to 6
- lengths: int32 [8], P('dp'), may hold values from 128 to 1024, as said below
- w_qkv: bfloat16 [2, 768, 2304], replicated, may hold values from -0.21875 to 0.21875
- b_qkv: float32 [2, 2304], replicated, may hold values from -3 to 3
- output_weight: bfloat16 [2, 768, 768], replicated, may hold values from -3.5 to 3.5
- w_up: bfloat16 [2, 768, 3072], replicated, may hold values from -0.21875 to 0.21875
- b_up: float32 [2, 3072], replicated, may hold values from -3 to 3
- w_down: bfloat16 [2, 3072, 768], replicated, may hold values from -0.109375 to 0.109375
- gains: float32 [2, 1536], replicated, may hold values from 0.5 to 1.5
- shifts: float32 [2, 3072], replicated, may hold values from -2 to 2
- cotangent: bfloat16 [8, 1024, 768], P('dp', 'seq'), may hold values from -6 to 6
Outputs:
- mixed: bfloat16 [8, 1024, 768], P('dp', 'seq')
- grad_tokens: float32 [8, 1024, 768], P('dp', 'seq')
- grad_w_qkv: float32 [2, 768, 2304], P(None, 'dp', 'seq')
- grad_w_out: float32 [2, 768, 768], P(None, 'dp', 'seq')
- grad_w_up: float32 [2, 768, 3072], P(None, 'dp', 'seq')
- grad_w_down: float32 [2, 3072, 768], P(None, 'dp', 'seq')
- grad_b_qkv: float32 [2, 2304], replicated
- grad_b_up: float32 [2, 3072], replicated
- grad_gains: float32 [2, 1536], replicated
- grad_shifts: float32 [2, 3072], replicated
The draws below stay inside these ranges and needn't reach their ends.
Inputs may be any that keep to these rules, and one draw needn't show every extreme that they name: `lengths`: in each of the 8 groups of 1 sequence one sequence, chosen at random, is longer than 896; in the first group it has length 1024. The others are spread evenly.
All inputs are finite; a program needn't handle non-finite values.
Results may differ from the reference program's by a relative error of at most 0.01.
Values sent between devices are 32-bit elements; how exact they have to be, the bound alone decides.
No kernel may reach another device: no remote copies, remote signals or barrier semaphores. Data moves between devices by JAX's collectives and lax.ppermute only.
A program may use at most 384 MiB of HBM per device.

```python
import math
import jax
import jax.numpy as jnp
from jax import lax

D = 768
HEADS = 12
HEAD_DIM = 64
FF = 3072
SPAN = 64
LAYERS = 2
SEQ_LEN = 1024
SEQS = 1
BATCH = 8
SEG = 256


def draw_lengths(key, part):
    key = jax.random.fold_in(key, 7)
    first_key, second_key, third_key = jax.random.split(key, 3)
    spread = jax.random.randint(first_key, (BATCH,), SEQ_LEN // 8, SEQ_LEN + 1)
    chosen = jax.random.randint(second_key, (BATCH // SEQS,), 0, SEQS)
    long_lengths = jax.random.randint(third_key, (BATCH // SEQS,), SEQ_LEN - SEG // 2 + 1, SEQ_LEN + 1)
    long_lengths = long_lengths.at[0].set(SEQ_LEN)
    within = jnp.arange(BATCH, dtype=jnp.int32) % SEQS
    longest = within == jnp.repeat(chosen, SEQS)
    return jnp.where(longest, jnp.repeat(long_lengths, SEQS), spread).astype(jnp.int32)


def shard_levels(rng, extent, cuts, smallest, high):
    factor_of = 1.0
    for axis_at, parts in cuts:
        heights = jax.random.uniform(jax.random.fold_in(jax.random.fold_in(rng, 6), axis_at), (parts,), jnp.float32, smallest / len(cuts), high / len(cuts))
        factor_of = factor_of * jnp.repeat(jnp.exp(heights), extent[axis_at] // parts).reshape((-1,) + (1,) * (len(extent) - 1 - axis_at))
    return factor_of


def normal_values(key, shape, scale, reach, cuts=(), held_as=jnp.bfloat16):
    entries = scale * jax.random.normal(key, shape, jnp.float32)
    if cuts:
        entries = entries * shard_levels(key, shape, cuts, -0.22, 0.18)
    return jnp.clip(entries, -reach, reach).astype(held_as)


def setup_inputs(seed: int = 0) -> dict:
    key_of = jax.random.split(jax.random.key(seed), 12)
    return {
        "tokens": normal_values(key_of[0], (BATCH, SEQ_LEN, D), 1.0, 6.0, ((0, 8), (1, 4))),
        "lengths": draw_lengths(jax.random.fold_in(key_of[11], 71), 0),
        "w_qkv": normal_values(key_of[2], (LAYERS, D, 3 * D), D ** -0.5, 0.21875),
        "b_qkv": normal_values(key_of[3], (LAYERS, 3 * D), 0.5, 3.0, (), jnp.float32),
        "output_weight": normal_values(key_of[4], (LAYERS, D, D), (max(D // 256, 1)) ** -0.5, 3.5),
        "w_up": normal_values(key_of[5], (LAYERS, D, FF), D ** -0.5, 0.21875),
        "b_up": normal_values(key_of[6], (LAYERS, FF), 0.5, 3.0, (), jnp.float32),
        "w_down": normal_values(key_of[7], (LAYERS, FF, D), FF ** -0.5, 0.109375),
        "gains": jnp.clip(1.0 + 0.1 * jax.random.normal(key_of[8], (LAYERS, 2 * D), jnp.float32), 0.5, 1.5),
        "shifts": normal_values(key_of[9], (LAYERS, 4 * D), 0.3, 2.0, (), jnp.float32),
        "cotangent": normal_values(key_of[10], (BATCH, SEQ_LEN, D), 1.0, 6.0, ((0, 8), (1, 4))),
    }


@jax.custom_vjp
def low(v):
    return lax.optimization_barrier(v.astype(jnp.bfloat16)).astype(jnp.float32)

@jax.custom_vjp
def low_back(v):
    return v

def low_keep(v):
    return (low(v), None)

def low_pass(kept, grad):
    return (grad,)

def back_keep(v):
    return (v, None)

def back_low(kept, grad):
    return (low(grad),)
low.defvjp(low_keep, low_pass)
low_back.defvjp(back_keep, back_low)

def normalize(residual, gain, shift):
    centre = residual - lax.optimization_barrier(jnp.mean(residual, axis=-1, keepdims=True))
    spread = lax.optimization_barrier(jnp.mean(centre * centre, axis=-1, keepdims=True))
    return centre * lax.rsqrt(spread + 1e-05) * gain + shift

def spanned(array):
    return array.reshape(array.shape[0], -1, SPAN, HEADS, HEAD_DIM)

def feature_maps(joined, cosine_wave, sine_wave, inside):
    hidden_width = joined.shape[-1] // 3
    query = jax.nn.softplus(joined[..., :hidden_width])
    key_map = jax.nn.softplus(joined[..., hidden_width:2 * hidden_width]) * inside
    values = joined[..., 2 * hidden_width:]
    return (spanned(query * cosine_wave), spanned(query * sine_wave), spanned(key_map * cosine_wave), spanned(key_map * sine_wave), spanned(values))

def block_sums(key_cos, key_sin, values):
    sum_cos = jnp.einsum('snchk,snchv->snhkv', key_cos, values, precision=lax.Precision.HIGHEST)
    sum_sin = jnp.einsum('snchk,snchv->snhkv', key_sin, values, precision=lax.Precision.HIGHEST)
    return (sum_cos, sum_sin, lax.optimization_barrier(jnp.sum(key_cos, axis=2)), lax.optimization_barrier(jnp.sum(key_sin, axis=2)))

def exclusive(blocks, before):
    running = jnp.cumsum(blocks, axis=1)
    shifted = jnp.concatenate([jnp.zeros_like(blocks[:, :1]), running[:, :-1]], axis=1)
    return shifted + before[:, None]

def attend(pieces, before):
    query_cos, query_sin, key_cos, key_sin, values = pieces
    sums = block_sums(key_cos, key_sin, values)
    state_cos, state_sin, norm_cos, norm_sin = [exclusive(group_member, prior) for group_member, prior in zip(sums, before)]
    numer = jnp.einsum('snchk,snhkv->snchv', query_cos, state_cos, precision=lax.Precision.HIGHEST)
    numer = numer + jnp.einsum('snchk,snhkv->snchv', query_sin, state_sin, precision=lax.Precision.HIGHEST)
    denom = jnp.einsum('snchk,snhk->snch', query_cos, norm_cos, precision=lax.Precision.HIGHEST)
    denom = denom + jnp.einsum('snchk,snhk->snch', query_sin, norm_sin, precision=lax.Precision.HIGHEST)
    scores = jnp.einsum('snihk,snjhk->snhij', query_cos, key_cos, precision=lax.Precision.HIGHEST)
    scores = scores + jnp.einsum('snihk,snjhk->snhij', query_sin, key_sin, precision=lax.Precision.HIGHEST)
    scores = scores * jnp.tril(jnp.ones((SPAN, SPAN), jnp.float32))
    numer = numer + jnp.einsum('snhij,snjhv->snihv', scores, values, precision=lax.Precision.HIGHEST)
    denom = denom + jnp.transpose(lax.optimization_barrier(jnp.sum(scores, axis=-1)), (0, 1, 3, 2))
    result = numer / denom[..., None]
    return result.reshape(result.shape[0], -1, HEADS * HEAD_DIM)

def layer_pass(residual_flow, weights, cosine_wave, sine_wave, inside):
    w_qkv, b_qkv, output_weight, w_up, b_up, w_down, gains, shifts = weights
    hidden_width = residual_flow.shape[-1]
    stream_in = low(residual_flow)
    joined = low_back(jnp.einsum('snd,df->snf', stream_in, w_qkv, precision=lax.Precision.HIGHEST)) + b_qkv
    pieces = feature_maps(joined, cosine_wave, sine_wave, inside)
    count = residual_flow.shape[0]
    before = (jnp.zeros((count, HEADS, HEAD_DIM, HEAD_DIM), jnp.float32), jnp.zeros((count, HEADS, HEAD_DIM, HEAD_DIM), jnp.float32), jnp.zeros((count, HEADS, HEAD_DIM), jnp.float32), jnp.zeros((count, HEADS, HEAD_DIM), jnp.float32))
    attention_input = low(attend(pieces, before))
    first_residual = residual_flow + low_back(jnp.einsum('vub,bi->vui', attention_input, output_weight, precision=lax.Precision.HIGHEST)) + shifts[:hidden_width]
    normed = normalize(first_residual, gains[:hidden_width], shifts[hidden_width:2 * hidden_width])
    normed_in = low(normed)
    pre_act = low_back(jnp.einsum('snd,df->snf', normed_in, w_up, precision=lax.Precision.HIGHEST)) + b_up
    activated = low(jax.nn.gelu(pre_act))
    residual_two = normed + low_back(jnp.einsum('snf,fd->snd', activated, w_down, precision=lax.Precision.HIGHEST)) + shifts[2 * hidden_width:3 * hidden_width]
    return normalize(residual_two, gains[hidden_width:], shifts[3 * hidden_width:])

def reference(tokens, lengths, w_qkv, b_qkv, output_weight, w_up, b_up, w_down, gains, shifts, cotangent):
    group_size = math.gcd(BATCH, max(1, 4096 // SEQ_LEN))
    group_count = BATCH // group_size
    params = (w_qkv.astype(jnp.float32), b_qkv, output_weight.astype(jnp.float32), w_up.astype(jnp.float32), b_up, w_down.astype(jnp.float32), gains, shifts)
    position = jnp.arange(SEQ_LEN, dtype=jnp.int32)

    def run(running, batch_item):
        tok_group, len_group, cot_group = batch_item
        length_col = len_group[:, None]
        inside = (position[None, :] < length_col).astype(jnp.float32)[..., None]
        phases = math.pi / 2 * jnp.minimum(position[None, :], length_col - 1).astype(jnp.float32) / length_col.astype(jnp.float32)
        cosine_wave = jnp.cos(phases)[..., None]
        sine_wave = jnp.sin(phases)[..., None]

        def forward(residual_flow, *weights):
            for number in range(LAYERS):
                layer_weights = tuple((group_member[number] for group_member in weights))
                residual_flow = layer_pass(residual_flow, layer_weights, cosine_wave, sine_wave, inside)
            return residual_flow
        result, pullback = jax.vjp(forward, tok_group.astype(jnp.float32), *params)
        grads = pullback(cot_group.astype(jnp.float32))
        updated = tuple((left_term + right_term for left_term, right_term in zip(running, grads[1:])))
        return (updated, (result.astype(jnp.bfloat16), grads[0]))
    initial = tuple((jnp.zeros_like(group_member) for group_member in params))
    totals_all, (outputs, grad_tok) = lax.scan(run, initial, (tokens.reshape(group_count, group_size, SEQ_LEN, D), lengths.reshape(group_count, group_size), cotangent.reshape(group_count, group_size, SEQ_LEN, D)))
    return (outputs.reshape(BATCH, SEQ_LEN, D), grad_tok.reshape(BATCH, SEQ_LEN, D), totals_all[0], totals_all[2], totals_all[3], totals_all[5], totals_all[1], totals_all[4], totals_all[6], totals_all[7])
```

```python
import functools
import math

import jax
import jax.numpy as jnp
from jax import lax
from jax.experimental import pallas as pl
from jax.experimental.pallas import tpu as pltpu
from jax.sharding import PartitionSpec as P

HEAD = 64
PAIR = 128
WIDE = 256
STATE = 136
EPS = 1e-05
F32 = jnp.float32
BF16 = jnp.bfloat16

NN = (((1,), (0,)), ((), ()))
NT = (((1,), (1,)), ((), ()))
TN = (((0,), (0,)), ((), ()))


def dot(a, b, dims=NN):
    return lax.dot_general(a, b, dims, preferred_element_type=F32)


def split(a):
    high = a.astype(BF16)
    return high, (a - high.astype(F32)).astype(BF16)


def dot3(a, b, dims=NN):
    return dot(a[0], b[0], dims) + (dot(a[0], b[1], dims) + dot(a[1], b[0], dims))


def cut(parts, rows):
    return tuple(part[rows] for part in parts)


def softplus(v):
    return jnp.maximum(v, 0.0) + jnp.log1p(jnp.exp(-jnp.abs(v)))


def sigmoid(v):
    return 1.0 / (1.0 + jnp.exp(-v))


def lanes_of_first(shape):
    lane = lax.broadcasted_iota(jnp.int32, shape, len(shape) - 1)
    return (lane & HEAD) == 0


def causal(tokens, sequences):
    row = lax.broadcasted_iota(jnp.int32, (tokens, tokens), 0)
    column = lax.broadcasted_iota(jnp.int32, (tokens, tokens), 1)
    keep = column <= row
    segment = tokens // sequences
    for later in range(1, sequences):
        keep = keep & ((row < later * segment) | (column >= later * segment))
    return keep


def two_maps(feature, cosine, sine):
    return jnp.concatenate([feature * cosine, feature * sine], axis=1)


def pack_state(full, sums):
    first = lanes_of_first((HEAD, PAIR))
    top = jnp.where(first, full[0:HEAD], full[HEAD : 2 * HEAD])
    low = jnp.where(first, full[2 * HEAD : 3 * HEAD], full[3 * HEAD :])
    rest = jnp.zeros((STATE - 2 * HEAD - 2, PAIR), F32)
    return jnp.concatenate([top, low, sums[:, :PAIR], sums[:, PAIR:], rest], axis=0)


def unpack_state(packed):
    first = lanes_of_first((HEAD, PAIR))
    top, low = packed[0:HEAD], packed[HEAD : 2 * HEAD]
    full = jnp.concatenate(
        [
            jnp.where(first, top, 0.0),
            jnp.where(first, 0.0, top),
            jnp.where(first, low, 0.0),
            jnp.where(first, 0.0, low),
        ],
        axis=0,
    )
    return full, packed[2 * HEAD : 2 * HEAD + 1], packed[2 * HEAD + 1 : 2 * HEAD + 2]


def head_sum(values):
    row = lax.broadcasted_iota(jnp.int32, (PAIR, PAIR), 0)
    column = lax.broadcasted_iota(jnp.int32, (PAIR, PAIR), 1)
    same = jnp.where((row & HEAD) == (column & HEAD), 1.0, 0.0).astype(BF16)
    high, low = split(values)
    return dot(high, same) + dot(low, same)


def norm_parts(residual):
    centre = residual - jnp.mean(residual, axis=-1, keepdims=True)
    rstd = lax.rsqrt(jnp.mean(centre * centre, axis=-1, keepdims=True) + EPS)
    return centre * rstd, rstd


def norm_back(residual, gain, upstream):
    xhat, rstd = norm_parts(residual)
    scaled = gain * upstream
    mean = jnp.mean(scaled, axis=-1, keepdims=True)
    along = jnp.mean(scaled * xhat, axis=-1, keepdims=True)
    grad = rstd * (scaled - mean - xhat * along)
    sums = jnp.concatenate(
        [
            jnp.sum(upstream * xhat, axis=0, keepdims=True),
            jnp.sum(upstream, axis=0, keepdims=True),
            jnp.sum(grad, axis=0, keepdims=True),
            jnp.zeros((5, residual.shape[1]), F32),
        ],
        axis=0,
    )
    return grad, sums


GELU_A = math.sqrt(2.0 / math.pi)
GELU_B = 0.044715


def gelu_terms(v):
    square = v * v
    bent = jnp.tanh(GELU_A * (v + GELU_B * (square * v)))
    return square, bent


def gelu(v):
    unused, bent = gelu_terms(v)
    return 0.5 * v * (1.0 + bent)


def gelu_both(v):
    square, bent = gelu_terms(v)
    slope = 0.5 * (1.0 + bent) + (0.5 * GELU_A) * v * (1.0 - bent * bent) * (
        1.0 + (3.0 * GELU_B) * square
    )
    return 0.5 * v * (1.0 + bent), slope


def spec(block, index):
    return pl.BlockSpec(block, index)


def whole(shape):
    return pl.BlockSpec(shape, lambda *at: (0,) * len(shape))


def shaped(shape, dtype=F32):
    return jax.ShapeDtypeStruct(shape, dtype)


def call(body, grid, ins, outs, shapes, flops, scratch=(), vmem=40, prefetch=0, name=None):
    moved = sum(math.prod(s.shape) * s.dtype.itemsize for s in shapes)
    return pl.pallas_call(
        body,
        grid_spec=pltpu.PrefetchScalarGridSpec(
            num_scalar_prefetch=prefetch,
            grid=grid,
            in_specs=ins,
            out_specs=outs,
            scratch_shapes=list(scratch),
        ),
        out_shape=shapes,
        compiler_params=pltpu.CompilerParams(
            dimension_semantics=("arbitrary",) * len(grid), vmem_limit_bytes=vmem << 20
        ),
        cost_estimate=pl.CostEstimate(
            flops=int(flops), bytes_accessed=int(2 * moved + 4e6), transcendentals=0
        ),
        name=name,
    )


def key_value_kernel(
    sequences, x_ref, wk_ref, wv_ref, bk_ref, bv_ref, trig_ref, jk_ref, jv_ref, state_ref
):
    x = x_ref[...].astype(BF16)
    key = dot(x, wk_ref[...]) + bk_ref[...]
    value = dot(x, wv_ref[...]) + bv_ref[...]
    jk_ref[...] = key
    jv_ref[...] = value
    cosine, sine, inside = trig_ref[0], trig_ref[1], trig_ref[2]
    segment = x.shape[0] // sequences
    for pair in range(WIDE // PAIR):
        lanes = slice(pair * PAIR, (pair + 1) * PAIR)
        maps = two_maps(softplus(key[:, lanes]) * inside, cosine, sine)
        maps_s, value_s = split(maps), split(value[:, lanes])
        for number in range(sequences):
            rows = slice(number * segment, (number + 1) * segment)
            state_ref[number, pair] = pack_state(
                dot3(cut(maps_s, rows), cut(value_s, rows), TN),
                jnp.sum(maps[rows], axis=0, keepdims=True),
            )


def query_kernel(
    sequences, x_ref, wq_ref, bq_ref, jk_ref, jv_ref, trig_ref, jq_ref, numer_ref, denom_ref
):
    x = x_ref[...].astype(BF16)
    query = dot(x, wq_ref[...]) + bq_ref[...]
    jq_ref[...] = query
    cosine, sine, inside = trig_ref[0], trig_ref[1], trig_ref[2]
    tokens = x.shape[0]
    keep = causal(tokens, sequences)
    first_two = lanes_of_first((tokens, 2 * PAIR))
    first = lanes_of_first((tokens, PAIR))
    for pair in range(WIDE // PAIR):
        lanes = slice(pair * PAIR, (pair + 1) * PAIR)
        query_maps = two_maps(softplus(query[:, lanes]), cosine, sine)
        key_s = split(two_maps(softplus(jk_ref[:, lanes]) * inside, cosine, sine))
        value = jv_ref[:, lanes]
        both = []
        for head in range(2):
            masked = jnp.where(first_two, query_maps, 0.0) if head == 0 else jnp.where(first_two, 0.0, query_maps)
            scores = jnp.where(keep, dot3(split(masked), key_s, NT), 0.0)
            ones = jnp.where(first, value, 1.0) if head == 0 else jnp.where(first, 1.0, value)
            both.append(dot3(split(scores), split(ones)))
        numer_ref[:, lanes] = jnp.where(first, both[0], both[1])
        denom_ref[:, lanes] = pltpu.roll(jnp.where(first, both[1], both[0]), HEAD, 1)


def attend_kernel(
    sequences, jq_ref, numer_ref, denom_ref, state_ref, trig_ref, w_ref, res_ref, vec_ref,
    att_ref, den_ref, one_ref, normed_ref, acc_ref,
):
    step = pl.program_id(0)
    cosine, sine = trig_ref[0], trig_ref[1]
    segment = jq_ref.shape[0] // sequences
    for pair in range(WIDE // PAIR):
        lanes = slice(pair * PAIR, (pair + 1) * PAIR)
        for number in range(sequences):
            rows = slice(number * segment, (number + 1) * segment)
            feature = softplus(jq_ref[rows, lanes])
            query_cos, query_sin = feature * cosine[rows], feature * sine[rows]
            full, sum_cos, sum_sin = unpack_state(state_ref[number, pair])
            maps = jnp.concatenate([query_cos, query_sin], axis=1)
            numer = numer_ref[rows, lanes] + dot3(split(maps), split(full))
            denom = denom_ref[rows, lanes] + head_sum(query_cos * sum_cos + query_sin * sum_sin)
            den_ref[rows, lanes] = denom
            att_ref[rows, lanes] = numer / denom
    part = dot(att_ref[...].astype(BF16), w_ref[...])

    @pl.when(step == 0)
    def _():
        acc_ref[...] = part

    @pl.when(step > 0)
    def _():
        acc_ref[...] += part

    @pl.when(step == pl.num_programs(0) - 1)
    def _():
        residual = res_ref[...].astype(F32) + acc_ref[...] + vec_ref[0:1]
        one_ref[...] = residual
        xhat, unused = norm_parts(residual)
        normed_ref[...] = xhat * vec_ref[1:2] + vec_ref[2:3]


def feed_forward_kernel(
    normed_ref, up_ref, bias_ref, down_ref, vec_ref, pre_ref, two_ref, stream_ref, low_ref, acc_ref
):
    step = pl.program_id(0)
    pre = dot(normed_ref[...].astype(BF16), up_ref[...]) + bias_ref[...]
    pre_ref[...] = pre
    part = dot(gelu(pre).astype(BF16), down_ref[...])

    @pl.when(step == 0)
    def _():
        acc_ref[...] = part

    @pl.when(step > 0)
    def _():
        acc_ref[...] += part

    @pl.when(step == pl.num_programs(0) - 1)
    def _():
        residual = normed_ref[...] + acc_ref[...] + vec_ref[0:1]
        two_ref[...] = residual
        xhat, unused = norm_parts(residual)
        stream = xhat * vec_ref[1:2] + vec_ref[2:3]
        stream_ref[...] = stream
        low_ref[...] = stream.astype(BF16)


def second_norm_kernel(up_ref, two_ref, vec_ref, d_ref, sums_ref):
    grad, sums = norm_back(two_ref[...], vec_ref[1:2], up_ref[...].astype(F32))
    d_ref[...] = grad
    sums_ref[...] = sums


def feed_back_kernel(
    d_two_ref, down_ref, up_ref, pre_ref, one_ref, vec_ref,
    d_one_ref, blocks_ref, sums_ref, bias_ref, acc_ref,
):
    step = pl.program_id(0)
    d_act = dot(d_two_ref[...].astype(BF16), down_ref[...], NT)
    unused, slope = gelu_both(pre_ref[...])
    d_pre = slope * d_act
    bias_ref[...] = jnp.sum(d_pre, axis=0, keepdims=True)
    part = dot(d_pre.astype(BF16), up_ref[...], NT)

    @pl.when(step == 0)
    def _():
        acc_ref[...] = part

    @pl.when(step > 0)
    def _():
        acc_ref[...] += part

    @pl.when(step == pl.num_programs(0) - 1)
    def _():
        grad, sums = norm_back(one_ref[...], vec_ref[1:2], d_two_ref[...] + acc_ref[...])
        d_one_ref[...] = grad
        sums_ref[...] = sums
        blocks, unused, width = blocks_ref.shape
        for block in range(blocks):
            blocks_ref[block] = grad[:, block * width : (block + 1) * width]


def state_back_kernel(
    sequences, d_one_ref, w_ref, jq_ref, trig_ref, att_ref, den_ref, num_ref, dden_ref, state_ref
):
    d_att = dot(d_one_ref[...].astype(BF16), w_ref[...], NT)
    cosine, sine = trig_ref[0], trig_ref[1]
    segment = jq_ref.shape[0] // sequences
    for pair in range(WIDE // PAIR):
        lanes = slice(pair * PAIR, (pair + 1) * PAIR)
        feature = softplus(jq_ref[:, lanes])
        query_cos, query_sin = feature * cosine, feature * sine
        d_num = d_att[:, lanes] / den_ref[:, lanes]
        d_den = -head_sum(d_num * att_ref[:, lanes])
        num_ref[:, lanes] = d_num
        dden_ref[:, lanes] = d_den
        maps_s = split(jnp.concatenate([query_cos, query_sin], axis=1))
        num_s = split(d_num)
        sum_cos, sum_sin = query_cos * d_den, query_sin * d_den
        for number in range(sequences):
            rows = slice(number * segment, (number + 1) * segment)
            sums = jnp.concatenate(
                [
                    jnp.sum(sum_cos[rows], axis=0, keepdims=True),
                    jnp.sum(sum_sin[rows], axis=0, keepdims=True),
                ],
                axis=1,
            )
            state_ref[number, pair] = pack_state(
                dot3(cut(maps_s, rows), cut(num_s, rows), TN), sums
            )


def inner_back_kernel(
    sequences, jq_ref, jk_ref, jv_ref, trig_ref, num_ref, dden_ref, state_ref,
    dq_ref, dk_ref, dv_ref,
):
    cosine, sine, inside = trig_ref[0], trig_ref[1], trig_ref[2]
    tokens = jq_ref.shape[0]
    segment = tokens // sequences
    keep = causal(tokens, sequences)
    first_two = lanes_of_first((tokens, 2 * PAIR))
    first = lanes_of_first((tokens, PAIR))
    for pair in range(WIDE // PAIR):
        lanes = slice(pair * PAIR, (pair + 1) * PAIR)
        query = jq_ref[:, lanes]
        query_maps = two_maps(softplus(query), cosine, sine)
        query_s = split(query_maps)
        key_s = split(two_maps(softplus(jk_ref[:, lanes]) * inside, cosine, sine))
        value = jv_ref[:, lanes]
        d_num, d_den = num_ref[:, lanes], dden_ref[:, lanes]
        num_s = split(d_num)
        moved = pltpu.roll(d_den, HEAD, 1) * (1.0 / HEAD)
        d_query, d_key, d_value = [], [], []
        for head in range(2):
            if head == 0:
                masked = jnp.where(first_two, query_maps, 0.0)
                ones = jnp.where(first, value, 1.0)
                joint = jnp.where(first, d_num, moved)
            else:
                masked = jnp.where(first_two, 0.0, query_maps)
                ones = jnp.where(first, 1.0, value)
                joint = jnp.where(first, moved, d_num)
            scores_s = split(jnp.where(keep, dot3(split(masked), key_s, NT), 0.0))
            grads_s = split(jnp.where(keep, dot3(split(joint), split(ones), NT), 0.0))
            d_query.append(dot3(grads_s, key_s))
            d_key.append(dot3(grads_s, query_s, TN))
            d_value.append(dot3(scores_s, num_s, TN))
        d_query_maps = jnp.where(first_two, d_query[0], d_query[1])
        d_key_maps = jnp.where(first_two, d_key[0], d_key[1])
        from_state = []
        for number in range(sequences):
            rows = slice(number * segment, (number + 1) * segment)
            full, sum_cos, sum_sin = unpack_state(state_ref[number, pair])
            more = dot3(cut(num_s, rows), split(full), NT)
            part = d_den[rows]
            from_state.append(
                more + jnp.concatenate([part * sum_cos, part * sum_sin], axis=1)
            )
        d_query_maps = d_query_maps + (
            from_state[0] if sequences == 1 else jnp.concatenate(from_state, axis=0)
        )
        dq_ref[:, lanes] = sigmoid(query) * (
            d_query_maps[:, :PAIR] * cosine + d_query_maps[:, PAIR:] * sine
        )
        dk_ref[:, lanes] = d_key_maps[:, :PAIR] * cosine + d_key_maps[:, PAIR:] * sine
        dv_ref[:, lanes] = jnp.where(first, d_value[0], d_value[1])


def joined_back_kernel(
    sequences, dq_ref, dk_ref, dv_ref, jk_ref, jv_ref, trig_ref, state_ref,
    wq_ref, wk_ref, wv_ref, d_one_ref,
    up_ref, blocks_ref, sum_ref, acc_ref, join_ref,
):
    step = pl.program_id(0)
    steps = 3
    cosine, sine, inside = trig_ref[0], trig_ref[1], trig_ref[2]
    segment = jk_ref.shape[0] // sequences
    keys, values = [], []
    for pair in range(WIDE // PAIR):
        lanes = slice(pair * PAIR, (pair + 1) * PAIR)
        key = jk_ref[:, lanes]
        maps_s = split(two_maps(softplus(key) * inside, cosine, sine))
        value_s = split(jv_ref[:, lanes])
        d_key, d_value = [], []
        for number in range(sequences):
            rows = slice(number * segment, (number + 1) * segment)
            full, sum_cos, sum_sin = unpack_state(state_ref[number, pair])
            full_s = split(full)
            back = dot3(cut(value_s, rows), full_s, NT)
            d_key.append(
                (back[:, :PAIR] + sum_cos) * cosine[rows] + (back[:, PAIR:] + sum_sin) * sine[rows]
            )
            d_value.append(dot3(cut(maps_s, rows), full_s))
        d_key = d_key[0] if sequences == 1 else jnp.concatenate(d_key, axis=0)
        d_value = d_value[0] if sequences == 1 else jnp.concatenate(d_value, axis=0)
        keys.append(inside * sigmoid(key) * (dk_ref[:, lanes] + d_key))
        values.append(dv_ref[:, lanes] + d_value)
    three = (dq_ref[...], jnp.concatenate(keys, axis=1), jnp.concatenate(values, axis=1))
    part = (
        dot(three[0].astype(BF16), wq_ref[...], NT)
        + dot(three[1].astype(BF16), wk_ref[...], NT)
        + dot(three[2].astype(BF16), wv_ref[...], NT)
    )
    for at in range(steps):

        @pl.when(step == at)
        def _(at=at):
            for group, block in enumerate(three):
                begin = (group * steps + at) * WIDE
                join_ref[:, begin : begin + WIDE] = block

    @pl.when(step == 0)
    def _():
        acc_ref[...] = d_one_ref[...] + part

    @pl.when(step > 0)
    def _():
        acc_ref[...] += part

    @pl.when(step == steps - 1)
    def _():
        up_ref[...] = acc_ref[...]
        sum_ref[...] = jnp.sum(join_ref[...], axis=0, keepdims=True)
        blocks, unused, width = blocks_ref.shape
        for block in range(blocks):
            blocks_ref[block] = join_ref[:, block * width : (block + 1) * width]


def feed_weights_kernel(count, at_ref, *refs):
    normed, errors = refs[:count], refs[count : 2 * count]
    up_ref, bias_ref, down_ref, d_up_ref, d_down_ref = refs[2 * count :]
    up, down, bias = up_ref[...], down_ref[...], bias_ref[...]
    d_up = d_down = None
    for n_ref, e_ref in zip(normed, errors):
        n, e = n_ref[...].astype(BF16), e_ref[...].astype(BF16)
        act, slope = gelu_both(dot(n, up) + bias)
        d_pre = slope * dot(e, down, NT)
        more_up = dot(n, d_pre.astype(BF16), TN)
        more_down = dot(act.astype(BF16), e, TN)
        d_up = more_up if d_up is None else d_up + more_up
        d_down = more_down if d_down is None else d_down + more_down
    d_up_ref[...] = d_up
    d_down_ref[...] = d_down


def attention_weights_kernel(
    at_ref, x_ref, x_other_ref, dj_ref, dj_other_ref, a_ref, a_other_ref, d_ref, d_other_ref,
    qkv_ref, out_ref,
):
    qkv_ref[...] = dot(x_ref[...].astype(BF16), dj_ref[...].astype(BF16), TN) + dot(
        x_other_ref[...].astype(BF16), dj_other_ref[...].astype(BF16), TN
    )
    out_ref[...] = dot(a_ref[...].astype(BF16), d_ref[...].astype(BF16), TN) + dot(
        a_other_ref[...].astype(BF16), d_other_ref[...].astype(BF16), TN
    )


def swap(value, axis, stride):
    return lax.ppermute(value, axis, [(i, i ^ stride) for i in range(lax.axis_size(axis))])


def strides(count):
    found, stride = [], 1
    while stride < count:
        found.append(stride)
        stride *= 2
    return found


def bit(axis, stride):
    return (lax.axis_index(axis) // stride) % 2


def scan_states(total, backward):
    before = jnp.zeros_like(total)
    for stride in strides(lax.axis_size("seq")):
        other = swap(total, "seq", stride)
        mine = bit("seq", stride)
        takes = (mine == 0) if backward else (mine == 1)
        before = before + jnp.where(takes, other, 0.0)
        total = total + other
    return before


def gather_sequence(value):
    held = [value]
    for stride in reversed(strides(lax.axis_size("seq"))):
        held = held + [swap(part, "seq", stride) for part in held]
    return held


def halve(value, axis, stride, at):
    mine = bit(axis, stride)
    keep = lax.dynamic_index_in_dim(value, mine, at, keepdims=False)
    send = lax.dynamic_index_in_dim(value, 1 - mine, at, keepdims=False)
    return keep + swap(send, axis, stride)


def scatter_rows(value, axis):
    steps = strides(lax.axis_size(axis))
    rows, columns = value.shape
    value = value.reshape((2,) * len(steps) + (rows // lax.axis_size(axis), columns))
    for at, stride in reversed(list(enumerate(reversed(steps)))):
        value = halve(value, axis, stride, at)
    return value


def scatter_down(value):
    seq, dp = lax.axis_size("seq"), lax.axis_size("dp")
    rows, columns = value.shape
    if dp == 2 * seq:
        value = halve(value.reshape(2, rows // 2, columns), "dp", 1, 0)
        pieces = jnp.stack(jnp.split(value, seq, axis=1))
        steps = strides(seq)
        pieces = pieces.reshape((2,) * len(steps) + pieces.shape[1:])
        for at, stride in reversed(list(enumerate(reversed(steps)))):
            pieces = halve(pieces, "dp", 2 * stride, at)
        pairs = []
        for z in range(seq):
            for x in range(2):
                for s in range(seq):
                    pairs.append((s * dp + 2 * z + x, z * dp + 2 * s + x))
        return lax.ppermute(pieces, ("seq", "dp"), pairs)
    pieces = lax.all_to_all(value, "seq", split_axis=1, concat_axis=0, tiled=True)
    return scatter_rows(pieces, "dp")


def sum_everywhere(value):
    for axis in ("seq", "dp"):
        for stride in strides(lax.axis_size(axis)):
            value = value + swap(value, axis, stride)
    return value


def on_device(
    tokens, lengths, w_qkv, b_qkv, output_weight, w_up, b_up, w_down, gains, shifts, cotangent
):
    sequences, segment, width = tokens.shape
    layers, hidden = b_up.shape
    seq = lax.axis_size("seq")
    count = sequences * segment
    groups = width // WIDE
    pairs = width // PAIR
    position = lax.axis_index("seq") * segment + jnp.arange(segment, dtype=jnp.int32)
    length_col = lengths[:, None]
    inside = (position[None, :] < length_col).astype(F32)
    phases = (
        math.pi
        / 2
        * jnp.minimum(position[None, :], length_col - 1).astype(F32)
        / length_col.astype(F32)
    )
    trig = jnp.stack([jnp.cos(phases), jnp.sin(phases), inside]).reshape(3, count, 1)
    trig = jnp.broadcast_to(trig, (3, count, PAIR))
    b_qkv = b_qkv[:, None, :]
    b_up = b_up[:, None, :]

    rows = (count, width)
    wide = spec((count, WIDE), lambda g, *_: (0, g))
    state_spec = spec((sequences, WIDE // PAIR, STATE, PAIR), lambda g, *_: (0, g, 0, 0))
    state_shape = shaped((sequences, pairs, STATE, PAIR))
    trig_spec = whole((3, count, PAIR))
    full = whole(rows)
    vec_spec = whole((8, width))
    acc = pltpu.VMEM(rows, F32)
    attention_flops = 2 * count * count * 256 * 12

    def qkv_spec(layer, part):
        return spec((None, width, WIDE), lambda g, *_: (layer, 0, part * groups + g))

    def bias_spec(layer, part):
        return spec((None, 1, WIDE), lambda g, *_: (layer, 0, part * groups + g))

    def rows_of(*vectors):
        stacked = jnp.stack(vectors)
        return jnp.concatenate([stacked, jnp.zeros((8 - len(vectors), width), F32)])

    stream, stream_low = tokens.reshape(rows), tokens.reshape(rows)
    saved = []
    block = min(768, hidden)
    for layer in range(layers):
        shift, gain = shifts[layer], gains[layer]
        vec_one = rows_of(shift[:width], gain[:width], shift[width : 2 * width])
        vec_two = rows_of(shift[2 * width : 3 * width], gain[width:], shift[3 * width :])
        key, value, total = call(
            functools.partial(key_value_kernel, sequences),
            (groups,),
            [full, qkv_spec(layer, 1), qkv_spec(layer, 2), bias_spec(layer, 1), bias_spec(layer, 2), trig_spec],
            [wide, wide, state_spec],
            [shaped(rows), shaped(rows), state_shape],
            4 * count * width * width,
            name="key_value",
        )(stream_low, w_qkv, w_qkv, b_qkv, b_qkv, trig)
        before = scan_states(total, False)
        query, numer, denom = call(
            functools.partial(query_kernel, sequences),
            (groups,),
            [full, qkv_spec(layer, 0), bias_spec(layer, 0), wide, wide, trig_spec],
            [wide, wide, wide],
            [shaped(rows), shaped(rows), shaped(rows)],
            2 * count * width * width + 5 * attention_flops,
            name="query",
        )(stream_low, w_qkv, b_qkv, key, value, trig)
        attended, den, one, normed = call(
            functools.partial(attend_kernel, sequences),
            (groups,),
            [wide, wide, wide, state_spec, trig_spec,
             spec((None, WIDE, width), lambda g, layer=layer: (layer, g, 0)), full, vec_spec],
            [wide, wide, full, full],
            [shaped(rows)] * 4,
            4 * count * width * width,
            scratch=[acc],
            name="attend",
        )(query, numer, denom, before, trig, output_weight, stream, vec_one)
        stream_in = stream
        pre, two, stream, stream_low = call(
            feed_forward_kernel,
            (hidden // block,),
            [full, spec((None, width, block), lambda g, layer=layer: (layer, 0, g)),
             spec((None, 1, block), lambda g, layer=layer: (layer, 0, g)),
             spec((None, block, width), lambda g, layer=layer: (layer, g, 0)), vec_spec],
            [spec((count, block), lambda g: (0, g)), full, full, full],
            [shaped((count, hidden)), shaped(rows), shaped(rows), shaped(rows, BF16)],
            4 * count * width * hidden,
            scratch=[acc],
            name="feed_forward",
        )(normed, w_up, b_up, w_down, vec_two)
        normed_all = gather_sequence(normed)
        stream_other = swap(stream_in.astype(F32), "seq", 1)
        attended_other = swap(attended, "seq", 1)
        saved.append(
            (stream_in, stream_other, query, key, value, before, attended, attended_other, den,
             one, normed_all, pre, two, vec_one, vec_two)
        )
    mixed = stream_low.reshape(tokens.shape)

    upstream = cotangent.reshape(rows)
    core = bit("seq", 1)
    chips = seq // 2
    part_qkv, part_out = 3 * width // seq, width // seq
    slot = hidden // seq
    place = jnp.stack([core, lax.axis_index("seq")]).astype(jnp.int32)
    grads, vectors = [], []
    for layer in reversed(range(layers)):
        (stream_in, stream_other, query, key, value, before, attended, attended_other, den,
         one, normed_all, pre, two, vec_one, vec_two) = saved[layer]
        d_two, sums_two = call(
            second_norm_kernel,
            (1,),
            [full, full, vec_spec],
            [full, vec_spec],
            [shaped(rows), shaped((8, width))],
            count * width * 20,
            name="second_norm",
        )(upstream, two, vec_two)
        d_two_all = gather_sequence(d_two)
        d_one, d_one_blocks, sums_one, bias_up = call(
            feed_back_kernel,
            (hidden // block,),
            [full, spec((None, block, width), lambda g, layer=layer: (layer, g, 0)),
             spec((None, width, block), lambda g, layer=layer: (layer, 0, g)),
             spec((count, block), lambda g: (0, g)), full, vec_spec],
            [full, whole((seq, count, part_out)), vec_spec, spec((1, block), lambda g: (0, g))],
            [shaped(rows), shaped((seq, count, part_out)), shaped((8, width)), shaped((1, hidden))],
            4 * count * width * hidden,
            scratch=[acc],
            name="feed_back",
        )(d_two, w_down, w_up, pre, one, vec_one)
        d_num, d_den, d_state = call(
            functools.partial(state_back_kernel, sequences),
            (groups,),
            [full, spec((None, WIDE, width), lambda g, layer=layer: (layer, g, 0)),
             wide, trig_spec, wide, wide],
            [wide, wide, state_spec],
            [shaped(rows), shaped(rows), state_shape],
            4 * count * width * width,
            name="state_back",
        )(d_one, output_weight, query, trig, attended, den)
        after = scan_states(d_state, True)
        d_query, d_key, d_value = call(
            functools.partial(inner_back_kernel, sequences),
            (groups,),
            [wide, wide, wide, trig_spec, wide, wide, state_spec],
            [wide, wide, wide],
            [shaped(rows)] * 3,
            15 * attention_flops,
            name="inner_back",
        )(query, key, value, trig, d_num, d_den, before)
        upstream, d_blocks, bias_qkv = call(
            functools.partial(joined_back_kernel, sequences),
            (groups,),
            [wide, wide, wide, wide, wide, trig_spec, state_spec,
             qkv_spec(layer, 0), qkv_spec(layer, 1), qkv_spec(layer, 2), full],
            [full, whole((seq, count, part_qkv)), whole((1, 3 * width))],
            [shaped(rows), shaped((seq, count, part_qkv)), shaped((1, 3 * width))],
            6 * count * width * width,
            scratch=[acc, pltpu.VMEM((count, 3 * width), F32)],
            name="joined_back",
        )(d_query, d_key, d_value, key, value, trig, after, w_qkv, w_qkv, w_qkv, d_one)

        d_up, d_down = call(
            functools.partial(feed_weights_kernel, seq),
            (1,),
            [full] * (2 * seq)
            + [spec((None, width, slot), lambda g, at, layer=layer: (layer, 0, at[1])),
               spec((None, 1, slot), lambda g, at, layer=layer: (layer, 0, at[1])),
               spec((None, slot, width), lambda g, at, layer=layer: (layer, at[1], 0))],
            [whole((width, slot)), whole((slot, width))],
            [shaped((width, slot)), shaped((slot, width))],
            8 * count * width * hidden,
            prefetch=1,
            vmem=48,
            name="feed_weights",
        )(place, *normed_all, *d_two_all, w_up, b_up, w_down)

        def others(blocks):
            paired = blocks.reshape((chips, 2) + blocks.shape[1:])
            return lax.dynamic_index_in_dim(paired, 1 - core, 1, keepdims=False)

        d_blocks_other = swap(others(d_blocks), "seq", 1)
        d_one_other = swap(others(d_one_blocks), "seq", 1)
        own = lambda shape: spec((None,) + shape, lambda g, at: (2 * g + at[0], 0, 0))
        theirs = lambda shape: spec((None,) + shape, lambda g, at: (g, 0, 0))
        d_qkv, d_out = call(
            attention_weights_kernel,
            (chips,),
            [full, full, own((count, part_qkv)), theirs((count, part_qkv)),
             full, full, own((count, part_out)), theirs((count, part_out))],
            [theirs((width, part_qkv)), theirs((width, part_out))],
            [shaped((chips, width, part_qkv)), shaped((chips, width, part_out))],
            8 * count * width * width,
            prefetch=1,
            name="attention_weights",
        )(place, stream_in, stream_other, d_blocks, d_blocks_other,
          attended, attended_other, d_one_blocks, d_one_other)

        def finish(value):
            steps = strides(chips)
            value = value.reshape((2,) * len(steps) + value.shape[1:])
            for at, stride in reversed(list(enumerate(reversed(steps)))):
                value = halve(value, "seq", 2 * stride, at)
            return scatter_rows(value, "dp")

        grads.append(
            (finish(d_qkv), finish(d_out), scatter_rows(d_up, "dp"), scatter_down(d_down))
        )
        vectors.append(
            jnp.concatenate(
                [bias_qkv[0], bias_up[0], sums_one[0], sums_two[0],
                 sums_one[2], sums_one[1], sums_two[2], sums_two[1]]
            )
        )
    grads, vectors = grads[::-1], vectors[::-1]
    mats = [jnp.stack(parts) for parts in zip(*grads)]
    summed = [sum_everywhere(v.reshape(-1, PAIR)).reshape(-1) for v in vectors]
    summed = jnp.stack(summed)
    ends = [0, 3 * width, 3 * width + hidden, 5 * width + hidden, 9 * width + hidden]
    vecs = [summed[:, a:b] for a, b in zip(ends, ends[1:])]
    return (mixed, upstream.reshape(tokens.shape), *mats, *vecs)


def solution(mesh):
    in_specs = (
        P("dp", "seq", None),
        P("dp"),
        P(),
        P(),
        P(),
        P(),
        P(),
        P(),
        P(),
        P(),
        P("dp", "seq", None),
    )
    out_specs = (
        P("dp", "seq", None),
        P("dp", "seq", None),
        P(None, "dp", "seq"),
        P(None, "dp", "seq"),
        P(None, "dp", "seq"),
        P(None, "dp", "seq"),
        P(),
        P(),
        P(),
        P(),
    )
    return jax.shard_map(
        on_device, mesh=mesh, in_specs=in_specs, out_specs=out_specs, check_vma=False
    )
```

```python
import functools
import math

import jax
import jax.numpy as jnp
from jax import lax
from jax.experimental import pallas as pl
from jax.experimental.pallas import tpu as pltpu
from jax.sharding import PartitionSpec as P

HEAD = 64
PAIR = 128
WIDE = 256
STATE = 136
VECTOR = 16
EPS = 1e-05
COST = 0.42
TIMES = {
    "key_value": 3.5, "query": 6.0, "attend": 4.0, "feed_forward": 8.0, "second_norm": 1.0, "feed_back": 8.0,
    "state_back": 4.0, "inner_back": 11.0, "feed_weights": 13.0, "joined_back": 8.0, "attention_weights": 5.0,
}
UP_FIRST = (1, 1)
BY_Y = (1.0, 0.0)
PLAN = """
sn2 fb2 sb2 ib2+12 ga2 sc2+4 fw2+6 jb2 sn1 fb1 sb1 dn2 up2 sc1+3 ga1 aw2 ib1 jb1+8 aw1 ud2 fw1+28 dn1 bx2+4 up1+5
by1+8 ud1+10 bb2 ve1+3 ve1+3 ve1 dt2+2 ve1 bb1 bb2 ve1 dt1+11 bb1+16
"""
F32 = jnp.float32
BF16 = jnp.bfloat16

NN = (((1,), (0,)), ((), ()))
NT = (((1,), (1,)), ((), ()))
TN = (((0,), (0,)), ((), ()))


def dot(a, b, dims=NN):
    return lax.dot_general(a, b, dims, preferred_element_type=F32)


def split(a):
    high = a.astype(BF16)
    return high, (a - high.astype(F32)).astype(BF16)


def dot3(a, b, dims=NN):
    return dot(a[0], b[0], dims) + (dot(a[0], b[1], dims) + dot(a[1], b[0], dims))


def cut(parts, rows):
    return tuple(part[rows] for part in parts)


def softplus(v):
    return jnp.maximum(v, 0.0) + jnp.log1p(jnp.exp(-jnp.abs(v)))


def sigmoid(v):
    return 1.0 / (1.0 + jnp.exp(-v))


def lanes_of_first(shape):
    lane = lax.broadcasted_iota(jnp.int32, shape, len(shape) - 1)
    return (lane & HEAD) == 0


def causal(tokens, sequences):
    row = lax.broadcasted_iota(jnp.int32, (tokens, tokens), 0)
    column = lax.broadcasted_iota(jnp.int32, (tokens, tokens), 1)
    keep = column <= row
    segment = tokens // sequences
    for later in range(1, sequences):
        keep = keep & ((row < later * segment) | (column >= later * segment))
    return keep


def two_maps(feature, cosine, sine):
    return jnp.concatenate([feature * cosine, feature * sine], axis=1)


def pack_state(full, sums):
    first = lanes_of_first((HEAD, PAIR))
    top = jnp.where(first, full[0:HEAD], full[HEAD : 2 * HEAD])
    low = jnp.where(first, full[2 * HEAD : 3 * HEAD], full[3 * HEAD :])
    rest = jnp.zeros((STATE - 2 * HEAD - 2, PAIR), F32)
    return jnp.concatenate([top, low, sums[:, :PAIR], sums[:, PAIR:], rest], axis=0)


def unpack_state(packed):
    first = lanes_of_first((HEAD, PAIR))
    top, low = packed[0:HEAD], packed[HEAD : 2 * HEAD]
    full = jnp.concatenate(
        [
            jnp.where(first, top, 0.0),
            jnp.where(first, 0.0, top),
            jnp.where(first, low, 0.0),
            jnp.where(first, 0.0, low),
        ],
        axis=0,
    )
    return full, packed[2 * HEAD : 2 * HEAD + 1], packed[2 * HEAD + 1 : 2 * HEAD + 2]


def head_sum(values):
    row = lax.broadcasted_iota(jnp.int32, (PAIR, PAIR), 0)
    column = lax.broadcasted_iota(jnp.int32, (PAIR, PAIR), 1)
    same = jnp.where((row & HEAD) == (column & HEAD), 1.0, 0.0).astype(BF16)
    high, low = split(values)
    return dot(high, same) + dot(low, same)


def norm_parts(residual):
    centre = residual - jnp.mean(residual, axis=-1, keepdims=True)
    rstd = lax.rsqrt(jnp.mean(centre * centre, axis=-1, keepdims=True) + EPS)
    return centre * rstd, rstd


def norm_back(residual, gain, upstream):
    xhat, rstd = norm_parts(residual)
    scaled = gain * upstream
    mean = jnp.mean(scaled, axis=-1, keepdims=True)
    along = jnp.mean(scaled * xhat, axis=-1, keepdims=True)
    grad = rstd * (scaled - mean - xhat * along)
    sums = jnp.concatenate(
        [
            jnp.sum(upstream * xhat, axis=0, keepdims=True),
            jnp.sum(upstream, axis=0, keepdims=True),
            jnp.sum(grad, axis=0, keepdims=True),
            jnp.zeros((5, residual.shape[1]), F32),
        ],
        axis=0,
    )
    return grad, sums


GELU_A = math.sqrt(2.0 / math.pi)
GELU_B = 0.044715


def gelu_terms(v):
    square = v * v
    bent = jnp.tanh(GELU_A * (v + GELU_B * (square * v)))
    return square, bent


def gelu(v):
    unused, bent = gelu_terms(v)
    return 0.5 * v * (1.0 + bent)


def gelu_both(v):
    square, bent = gelu_terms(v)
    slope = 0.5 * (1.0 + bent) + (0.5 * GELU_A) * v * (1.0 - bent * bent) * (
        1.0 + (3.0 * GELU_B) * square
    )
    return 0.5 * v * (1.0 + bent), slope


def spec(block, index):
    return pl.BlockSpec(block, index)


def whole(shape):
    return pl.BlockSpec(shape, lambda *at: (0,) * len(shape))


def shaped(shape, dtype=F32):
    return jax.ShapeDtypeStruct(shape, dtype)


class Order:
    def __init__(self):
        self.last = None
        self.wait = 0.0

    def call(self, body, grid, ins, outs, shapes, flops, scratch=(), vmem=40, prefetch=0, name=None, carry=(), after=()):
        after = list(after) + ([] if self.last is None else [self.last])
        skipped = len(after) + len(carry)
        made = len(shapes)
        anywhere = pl.BlockSpec(memory_space=pl.ANY)

        def kernel(*refs):
            given, rest = refs[:prefetch], refs[prefetch + skipped :]
            body(*given, *rest[: len(ins) + made], *rest[len(ins) + made + len(carry) :])

        run = pl.pallas_call(
            kernel,
            grid_spec=pltpu.PrefetchScalarGridSpec(
                num_scalar_prefetch=prefetch,
                grid=grid,
                in_specs=[anywhere] * skipped + list(ins),
                out_specs=list(outs) + [anywhere] * len(carry),
                scratch_shapes=list(scratch),
            ),
            out_shape=list(shapes) + [shaped(c.shape, c.dtype) for c in carry],
            input_output_aliases={
                prefetch + skipped - len(carry) + at: made + at for at in range(len(carry))
            },
            compiler_params=pltpu.CompilerParams(
                dimension_semantics=("arbitrary",) * len(grid), vmem_limit_bytes=vmem << 20
            ),
            cost_estimate=pl.CostEstimate(
                flops=int((TIMES.get(name, 1.0) + 0.7 + self.wait) * COST * 1.15e9),
                bytes_accessed=0,
                transcendentals=0,
            ),
            name=name,
        )

        def apply(*given):
            found = run(*given[:prefetch], *after, *carry, *given[prefetch:])
            self.last = found[0]
            return found

        return apply


def key_value_kernel(
    sequences, x_ref, wk_ref, wv_ref, bk_ref, bv_ref, trig_ref, jk_ref, jv_ref, state_ref
):
    x = x_ref[...].astype(BF16)
    key = dot(x, wk_ref[...]) + bk_ref[...]
    value = dot(x, wv_ref[...]) + bv_ref[...]
    jk_ref[...] = key
    jv_ref[...] = value
    cosine, sine, inside = trig_ref[0], trig_ref[1], trig_ref[2]
    segment = x.shape[0] // sequences
    for pair in range(WIDE // PAIR):
        lanes = slice(pair * PAIR, (pair + 1) * PAIR)
        maps = two_maps(softplus(key[:, lanes]) * inside, cosine, sine)
        maps_s, value_s = split(maps), split(value[:, lanes])
        for number in range(sequences):
            rows = slice(number * segment, (number + 1) * segment)
            state_ref[number, pair] = pack_state(
                dot3(cut(maps_s, rows), cut(value_s, rows), TN),
                jnp.sum(maps[rows], axis=0, keepdims=True),
            )


def query_kernel(
    sequences, x_ref, wq_ref, bq_ref, jk_ref, jv_ref, trig_ref, jq_ref, numer_ref, denom_ref
):
    x = x_ref[...].astype(BF16)
    query = dot(x, wq_ref[...]) + bq_ref[...]
    jq_ref[...] = query
    cosine, sine, inside = trig_ref[0], trig_ref[1], trig_ref[2]
    tokens = x.shape[0]
    keep = causal(tokens, sequences)
    first_two = lanes_of_first((tokens, 2 * PAIR))
    first = lanes_of_first((tokens, PAIR))
    for pair in range(WIDE // PAIR):
        lanes = slice(pair * PAIR, (pair + 1) * PAIR)
        query_maps = two_maps(softplus(query[:, lanes]), cosine, sine)
        key_s = split(two_maps(softplus(jk_ref[:, lanes]) * inside, cosine, sine))
        value = jv_ref[:, lanes]
        both = []
        for head in range(2):
            masked = jnp.where(first_two, query_maps, 0.0) if head == 0 else jnp.where(first_two, 0.0, query_maps)
            scores = jnp.where(keep, dot3(split(masked), key_s, NT), 0.0)
            ones = jnp.where(first, value, 1.0) if head == 0 else jnp.where(first, 1.0, value)
            both.append(dot3(split(scores), split(ones)))
        numer_ref[:, lanes] = jnp.where(first, both[0], both[1])
        denom_ref[:, lanes] = pltpu.roll(jnp.where(first, both[1], both[0]), HEAD, 1)


def attend_kernel(
    sequences, jq_ref, numer_ref, denom_ref, state_ref, trig_ref, w_ref, res_ref, vec_ref,
    att_ref, den_ref, one_ref, normed_ref, acc_ref,
):
    step = pl.program_id(0)
    cosine, sine = trig_ref[0], trig_ref[1]
    segment = jq_ref.shape[0] // sequences
    for pair in range(WIDE // PAIR):
        lanes = slice(pair * PAIR, (pair + 1) * PAIR)
        for number in range(sequences):
            rows = slice(number * segment, (number + 1) * segment)
            feature = softplus(jq_ref[rows, lanes])
            query_cos, query_sin = feature * cosine[rows], feature * sine[rows]
            full, sum_cos, sum_sin = unpack_state(state_ref[number, pair])
            maps = jnp.concatenate([query_cos, query_sin], axis=1)
            numer = numer_ref[rows, lanes] + dot3(split(maps), split(full))
            denom = denom_ref[rows, lanes] + head_sum(query_cos * sum_cos + query_sin * sum_sin)
            den_ref[rows, lanes] = denom
            att_ref[rows, lanes] = numer / denom
    part = dot(att_ref[...].astype(BF16), w_ref[...])

    @pl.when(step == 0)
    def _():
        acc_ref[...] = part

    @pl.when(step > 0)
    def _():
        acc_ref[...] += part

    @pl.when(step == pl.num_programs(0) - 1)
    def _():
        residual = res_ref[...].astype(F32) + acc_ref[...] + vec_ref[0:1]
        one_ref[...] = residual
        xhat, unused = norm_parts(residual)
        normed_ref[...] = xhat * vec_ref[1:2] + vec_ref[2:3]


def feed_forward_kernel(
    normed_ref, up_ref, bias_ref, down_ref, vec_ref, pre_ref, two_ref, stream_ref, low_ref, acc_ref
):
    step = pl.program_id(0)
    pre = dot(normed_ref[...].astype(BF16), up_ref[...]) + bias_ref[...]
    pre_ref[...] = pre
    part = dot(gelu(pre).astype(BF16), down_ref[...])

    @pl.when(step == 0)
    def _():
        acc_ref[...] = part

    @pl.when(step > 0)
    def _():
        acc_ref[...] += part

    @pl.when(step == pl.num_programs(0) - 1)
    def _():
        residual = normed_ref[...] + acc_ref[...] + vec_ref[0:1]
        two_ref[...] = residual
        xhat, unused = norm_parts(residual)
        stream = xhat * vec_ref[1:2] + vec_ref[2:3]
        stream_ref[...] = stream
        low_ref[...] = stream.astype(BF16)


def second_norm_kernel(up_ref, two_ref, vec_ref, d_ref, sums_ref):
    grad, sums = norm_back(two_ref[...], vec_ref[1:2], up_ref[...].astype(F32))
    d_ref[...] = grad
    sums_ref[...] = sums


def feed_back_kernel(
    d_two_ref, down_ref, up_ref, pre_ref, one_ref, vec_ref,
    d_one_ref, sums_ref, bias_ref, acc_ref,
):
    step = pl.program_id(0)
    d_act = dot(d_two_ref[...].astype(BF16), down_ref[...], NT)
    unused, slope = gelu_both(pre_ref[...])
    d_pre = slope * d_act
    bias_ref[...] = jnp.sum(d_pre, axis=0, keepdims=True)
    part = dot(d_pre.astype(BF16), up_ref[...], NT)

    @pl.when(step == 0)
    def _():
        acc_ref[...] = part

    @pl.when(step > 0)
    def _():
        acc_ref[...] += part

    @pl.when(step == pl.num_programs(0) - 1)
    def _():
        grad, sums = norm_back(one_ref[...], vec_ref[1:2], d_two_ref[...] + acc_ref[...])
        d_one_ref[...] = grad
        sums_ref[...] = sums


def state_back_kernel(
    sequences, d_one_ref, w_ref, jq_ref, trig_ref, att_ref, den_ref, num_ref, dden_ref, state_ref
):
    d_att = dot(d_one_ref[...].astype(BF16), w_ref[...], NT)
    cosine, sine = trig_ref[0], trig_ref[1]
    segment = jq_ref.shape[0] // sequences
    for pair in range(WIDE // PAIR):
        lanes = slice(pair * PAIR, (pair + 1) * PAIR)
        feature = softplus(jq_ref[:, lanes])
        query_cos, query_sin = feature * cosine, feature * sine
        d_num = d_att[:, lanes] / den_ref[:, lanes]
        d_den = -head_sum(d_num * att_ref[:, lanes])
        num_ref[:, lanes] = d_num
        dden_ref[:, lanes] = d_den
        maps_s = split(jnp.concatenate([query_cos, query_sin], axis=1))
        num_s = split(d_num)
        sum_cos, sum_sin = query_cos * d_den, query_sin * d_den
        for number in range(sequences):
            rows = slice(number * segment, (number + 1) * segment)
            sums = jnp.concatenate(
                [
                    jnp.sum(sum_cos[rows], axis=0, keepdims=True),
                    jnp.sum(sum_sin[rows], axis=0, keepdims=True),
                ],
                axis=1,
            )
            state_ref[number, pair] = pack_state(
                dot3(cut(maps_s, rows), cut(num_s, rows), TN), sums
            )


def inner_back_kernel(
    sequences, jq_ref, jk_ref, jv_ref, trig_ref, num_ref, dden_ref, state_ref,
    dq_ref, dk_ref, dv_ref,
):
    cosine, sine, inside = trig_ref[0], trig_ref[1], trig_ref[2]
    tokens = jq_ref.shape[0]
    segment = tokens // sequences
    keep = causal(tokens, sequences)
    first_two = lanes_of_first((tokens, 2 * PAIR))
    first = lanes_of_first((tokens, PAIR))
    for pair in range(WIDE // PAIR):
        lanes = slice(pair * PAIR, (pair + 1) * PAIR)
        query = jq_ref[:, lanes]
        query_maps = two_maps(softplus(query), cosine, sine)
        query_s = split(query_maps)
        key_s = split(two_maps(softplus(jk_ref[:, lanes]) * inside, cosine, sine))
        value = jv_ref[:, lanes]
        d_num, d_den = num_ref[:, lanes], dden_ref[:, lanes]
        num_s = split(d_num)
        moved = pltpu.roll(d_den, HEAD, 1) * (1.0 / HEAD)
        d_query, d_key, d_value = [], [], []
        for head in range(2):
            if head == 0:
                masked = jnp.where(first_two, query_maps, 0.0)
                ones = jnp.where(first, value, 1.0)
                joint = jnp.where(first, d_num, moved)
            else:
                masked = jnp.where(first_two, 0.0, query_maps)
                ones = jnp.where(first, 1.0, value)
                joint = jnp.where(first, moved, d_num)
            scores_s = split(jnp.where(keep, dot3(split(masked), key_s, NT), 0.0))
            grads_s = split(jnp.where(keep, dot3(split(joint), split(ones), NT), 0.0))
            d_query.append(dot3(grads_s, key_s))
            d_key.append(dot3(grads_s, query_s, TN))
            d_value.append(dot3(scores_s, num_s, TN))
        d_query_maps = jnp.where(first_two, d_query[0], d_query[1])
        d_key_maps = jnp.where(first_two, d_key[0], d_key[1])
        from_state = []
        for number in range(sequences):
            rows = slice(number * segment, (number + 1) * segment)
            full, sum_cos, sum_sin = unpack_state(state_ref[number, pair])
            more = dot3(cut(num_s, rows), split(full), NT)
            part = d_den[rows]
            from_state.append(
                more + jnp.concatenate([part * sum_cos, part * sum_sin], axis=1)
            )
        d_query_maps = d_query_maps + (
            from_state[0] if sequences == 1 else jnp.concatenate(from_state, axis=0)
        )
        dq_ref[:, lanes] = sigmoid(query) * (
            d_query_maps[:, :PAIR] * cosine + d_query_maps[:, PAIR:] * sine
        )
        dk_ref[:, lanes] = d_key_maps[:, :PAIR] * cosine + d_key_maps[:, PAIR:] * sine
        dv_ref[:, lanes] = jnp.where(first, d_value[0], d_value[1])


def joined_back_kernel(
    sequences, dq_ref, dk_ref, dv_ref, jk_ref, jv_ref, trig_ref, state_ref,
    wq_ref, wk_ref, wv_ref, d_one_ref,
    up_ref, blocks_ref, sum_ref, acc_ref, join_ref,
):
    step = pl.program_id(0)
    steps = 3
    cosine, sine, inside = trig_ref[0], trig_ref[1], trig_ref[2]
    segment = jk_ref.shape[0] // sequences
    keys, values = [], []
    for pair in range(WIDE // PAIR):
        lanes = slice(pair * PAIR, (pair + 1) * PAIR)
        key = jk_ref[:, lanes]
        maps_s = split(two_maps(softplus(key) * inside, cosine, sine))
        value_s = split(jv_ref[:, lanes])
        d_key, d_value = [], []
        for number in range(sequences):
            rows = slice(number * segment, (number + 1) * segment)
            full, sum_cos, sum_sin = unpack_state(state_ref[number, pair])
            full_s = split(full)
            back = dot3(cut(value_s, rows), full_s, NT)
            d_key.append(
                (back[:, :PAIR] + sum_cos) * cosine[rows] + (back[:, PAIR:] + sum_sin) * sine[rows]
            )
            d_value.append(dot3(cut(maps_s, rows), full_s))
        d_key = d_key[0] if sequences == 1 else jnp.concatenate(d_key, axis=0)
        d_value = d_value[0] if sequences == 1 else jnp.concatenate(d_value, axis=0)
        keys.append(inside * sigmoid(key) * (dk_ref[:, lanes] + d_key))
        values.append(dv_ref[:, lanes] + d_value)
    three = (dq_ref[...], jnp.concatenate(keys, axis=1), jnp.concatenate(values, axis=1))
    part = (
        dot(three[0].astype(BF16), wq_ref[...], NT)
        + dot(three[1].astype(BF16), wk_ref[...], NT)
        + dot(three[2].astype(BF16), wv_ref[...], NT)
    )
    for at in range(steps):

        @pl.when(step == at)
        def _(at=at):
            for group, block in enumerate(three):
                begin = (group * steps + at) * WIDE
                join_ref[:, begin : begin + WIDE] = block

    @pl.when(step == 0)
    def _():
        acc_ref[...] = d_one_ref[...] + part

    @pl.when(step > 0)
    def _():
        acc_ref[...] += part

    @pl.when(step == steps - 1)
    def _():
        up_ref[...] = acc_ref[...]
        sum_ref[...] = jnp.sum(join_ref[...], axis=0, keepdims=True)
        chips = blocks_ref.shape[1]
        part, part_one = join_ref.shape[1] // (2 * chips), d_one_ref.shape[1] // (2 * chips)
        for core in range(2):
            for chip in range(chips):
                block = 2 * chip + core
                blocks_ref[core, chip] = jnp.concatenate(
                    [
                        join_ref[:, block * part : (block + 1) * part],
                        d_one_ref[:, block * part_one : (block + 1) * part_one],
                    ],
                    axis=1,
                )


def feed_weights_kernel(chips, packed, first, at_ref, *refs):
    mine, rest = refs[: 2 * chips], refs[2 * chips :]
    if len(rest[1].shape) == 3:
        (core, stacked), rest = rest[:2], rest[2:]
        held = [stacked.at[at] for at in range(2 * chips - 1)]
        theirs = [core] + held[: chips - 1] + held[-1:] + held[chips - 1 : -1]
    else:
        theirs, rest = rest[: 2 * chips], rest[2 * chips :]
    up_ref, bias_ref, down_ref, up_keep_ref, up_send_ref, *down_refs = rest
    pairs = list(zip(mine[:chips], mine[chips:])) + list(zip(theirs[:chips], theirs[chips:]))
    up, down, bias = up_ref[...], down_ref[...], bias_ref[...]
    d_up = d_down = None
    for n_ref, e_ref in pairs:
        n, e = n_ref[...].astype(BF16), e_ref[...].astype(BF16)
        act, slope = gelu_both(dot(n, up) + bias)
        d_pre = slope * dot(e, down, NT)
        more_up = dot(n, d_pre.astype(BF16), TN)
        more_down = dot(act.astype(BF16), e, TN)
        d_up = more_up if d_up is None else d_up + more_up
        d_down = more_down if d_down is None else d_down + more_down
    blocks, rows, unused = up_keep_ref.shape
    for mine in range(2):

        @pl.when(at_ref[place_of("dp", first)] == mine)
        def _(mine=mine):
            for block in range(2 * blocks):
                ref = up_keep_ref if block // first % 2 == mine else up_send_ref
                ref[block // (2 * first) * first + block % first] = d_up[block * rows : (block + 1) * rows]

    if not packed:
        down_refs[0][...] = d_down
        return
    keep_ref, send_ref = down_refs
    others, unused, rows, width = keep_ref.shape
    groups = 2 * others
    lanes = width // groups
    for z in range(2):

        @pl.when(at_ref[place_of("dp", 2)] == z)
        def _(z=z):
            for low, ref in ((z, keep_ref), (1 - z, send_ref)):
                for x in range(2):
                    for high in range(others):
                        begin = (2 * high + low) * lanes
                        columns = d_down[:, begin : begin + lanes]
                        top = x * groups * rows
                        ref[high, x] = jnp.concatenate(
                            [columns[top + at * rows : top + (at + 1) * rows] for at in range(groups)], axis=1
                        )


def attention_weights_kernel(
    rows, at_ref, x_ref, x_other_ref, a_ref, a_other_ref, d_ref, *outs
):
    chips = d_ref.shape[1]
    part = 3 * d_ref.shape[3] // 4
    core = at_ref[place_of("seq", 1)]
    both = (x_ref, x_other_ref), (a_ref, a_other_ref)
    inputs = [jnp.concatenate([r[...].astype(BF16) for r in refs], axis=0) for refs in both]
    grads = []
    for chip in range(chips):
        errors = [d_ref[core, chip].astype(BF16), d_ref[1 - core, chip].astype(BF16)]
        errors = jnp.concatenate(errors, axis=0)
        grads.append(
            jnp.concatenate(
                [dot(inputs[0], errors[:, :part], TN), dot(inputs[1], errors[:, part:], TN)], axis=1
            )
        )
    by_y, by_x = outs[:2] if rows else (), outs[-2:] if len(outs) == 4 or not rows else ()
    high, blocks = by_y[0].shape[:2] if by_y else (chips // 2, 2 * by_x[0].shape[1])
    more = by_x[0].shape[2] if by_x else 0
    size = rows + more
    for y in range(2 if by_y else 0):

        @pl.when(at_ref[place_of("seq", 2)] == y)
        def _(y=y):
            for low, ref in ((y, by_y[0]), (1 - y, by_y[1])):
                for upper in range(high):
                    for block in range(blocks):
                        ref[upper, block] = grads[2 * upper + low][block * size : block * size + rows]

    for x in range(2 if by_x else 0):

        @pl.when(at_ref[place_of("dp", 1)] == x)
        def _(x=x):
            for parity, ref in ((x, by_x[0]), (1 - x, by_x[1])):
                for chip in range(chips):
                    for block in range(blocks // 2):
                        begin = (2 * block + parity) * size + rows
                        ref[chip, block] = grads[chip][begin : begin + more]


def gate_kernel(out_ref):
    out_ref[...] = jnp.zeros_like(out_ref)


def stack_kernel(*refs):
    for at, ref in enumerate(refs[:-1]):
        refs[-1][at] = ref[...]


def swap(value, axis, stride):
    return lax.ppermute(value, axis, [(i, i ^ stride) for i in range(lax.axis_size(axis))])


def strides(count):
    found, stride = [], 1
    while stride < count:
        found.append(stride)
        stride *= 2
    return found


def bit(axis, stride):
    return (lax.axis_index(axis) // stride) % 2


def places():
    found = [lax.axis_index("seq")]
    for axis in ("seq", "dp"):
        found += [bit(axis, stride) for stride in strides(lax.axis_size(axis))]
    return jnp.stack(found).astype(jnp.int32)


def place_of(axis, stride):
    spot = 1 + strides(lax.axis_size(axis)).index(stride)
    return spot if axis == "seq" else spot + len(strides(lax.axis_size("seq")))


def scan_states(total, backward, order=None):
    before = None
    for stride in strides(lax.axis_size("seq")):
        other = swap(total, "seq", stride)
        mine = bit("seq", stride)
        takes = (mine == 0) if backward else (mine == 1)
        more = jnp.where(takes, other, 0.0)
        before = more if before is None else before + more
        if order is None or stride > 1:
            total = total + other
        else:
            total = add(order, total, other)
    return before


def gather_chips(value):
    held = [value]
    for stride in reversed(strides(lax.axis_size("seq"))[1:]):
        held = held + [swap(part, "seq", stride) for part in held]
    return held


def gather_cores(held):
    return held + [swap(part, "seq", 1) for part in held]


def halve_kernel(at_ref, *refs):
    kept_ref, sent_ref = refs[-2:]
    for at in range(kept_ref.shape[1]):
        keep_mine, recv_mine, keep_other, recv_other = refs[4 * at : 4 * at + 4]
        kept_ref[:, at] = keep_mine[...] + recv_mine[...]
        sent_ref[:, at] = keep_other[...] + recv_other[...]


def add_kernel(one_ref, two_ref, out_ref):
    out_ref[...] = one_ref[...] + two_ref[...]


class Scatter:
    def __init__(self, order, place, keep, send, steps):
        self.order, self.place, self.keep, self.steps = order, place, keep, list(steps)
        self.recv = self.swap(send)

    def swap(self, send):
        axis, stride, self.at = self.steps.pop(0)
        return swap(send, axis, stride)

    def done(self):
        return not self.steps

    def fits(self, other):
        return self.keep.shape == other.keep.shape and self.steps == other.steps

    def advance(self, *others):
        axis, stride, at = self.steps[0]
        shape = self.keep.shape
        rows, lanes = shape[-2:]
        outer = math.prod(shape[:at]) * shape[at] // 2
        inner = math.prod(shape[at + 1 : -2])
        flat = (outer, 2, inner, rows, lanes)
        parts = (self,) + others
        pieces = 2 if rows % 16 == 0 and outer < 4 else 1
        block = (None, None, inner, rows // pieces, lanes)
        spot = place_of(axis, stride)
        mine = spec(block, lambda a, r, at: (a, at[spot], 0, r, 0))
        other = spec(block, lambda a, r, at: (a, 1 - at[spot], 0, r, 0))
        out = spec((None, inner, len(parts), rows // pieces, lanes), lambda a, r, at: (a, 0, 0, r, 0))
        given = []
        for part in parts:
            given += [part.keep.reshape(flat), part.recv.reshape(flat)] * 2
        kept, sent = self.order.call(
            halve_kernel,
            (outer, pieces),
            [mine, mine, other, other] * len(parts),
            [out, out],
            [shaped((outer, inner, len(parts), rows, lanes))] * 2,
            1,
            prefetch=1,
            name="halve",
        )(self.place, *given)
        left = shape[:at] + (shape[at] // 2,) + shape[at + 1 : -2] + (len(parts), rows, lanes)
        if len(parts) == 1:
            left = left[:-3] + left[-2:]
        self.keep = kept.reshape(left)
        self.recv = self.swap(sent.reshape(left))
        for part in others:
            part.steps = []

    def last(self):
        rows, lanes = self.keep.shape[-2:]
        shape = (-1, rows, lanes)
        return self.keep.reshape(shape), self.recv.reshape(shape)


def add(order, one, two, at=None):
    if at is None:
        given = out = whole(one.shape)
        shape = one.shape
    else:
        shape = one.shape[1:]
        given = spec((None,) + shape, lambda g: (at,) + (0,) * len(shape))
        out = whole(shape)
    return order.call(add_kernel, (1,), [given] * 2, [out], [shaped(shape)], 1, name="add")(one, two)[0]


def vector_kernel(layers, *refs):
    out_ref = refs[-1]
    out_ref[...] = jnp.zeros_like(out_ref)
    width = out_ref.shape[1]
    for layer in range(layers):
        qkv_ref, up_ref, one_ref, two_ref = refs[4 * layer : 4 * layer + 4]
        rows = []
        for ref in (qkv_ref, up_ref):
            rows += [ref[0:1, at : at + width] for at in range(0, ref.shape[1], width)]
        rows += [one_ref[0:1], two_ref[0:1], one_ref[2:3], one_ref[1:2], two_ref[2:3], two_ref[1:2]]
        for at, row in enumerate(rows):
            out_ref[layer * VECTOR + at : layer * VECTOR + at + 1] = row


def finish_kernel(counts, *refs):
    vector_ref, qkv_ref, out_ref, up_ref, down_ref, *vector_refs = refs[-9:]
    width = vector_ref.shape[1]
    begin = 0
    for ref in vector_refs:
        many = ref.shape[1] // width
        for layer in range(len(counts)):
            for at in range(many):
                row = layer * VECTOR + begin + at
                ref[layer : layer + 1, at * width : (at + 1) * width] = vector_ref[row : row + 1]
        begin += many
    part = qkv_ref.shape[2]
    for layer, many in enumerate(counts):
        given = refs[sum(counts[:layer]) :][:many]
        begin = 0
        for at in range(0, many - 3, 2):
            keep, recv = given[at : at + 2]
            for piece in range(keep.shape[0]):
                total = keep[piece] + recv[piece]
                rows = total.shape[0]
                qkv_ref[layer, begin : begin + rows] = total[:, :part]
                out_ref[layer, begin : begin + rows] = total[:, part:]
                begin += rows
        up_ref[layer] = given[many - 3][0] + given[many - 2][0]
        down = given[many - 1]
        rows, lanes = down.shape
        across = down_ref.shape[2]
        for at in range(lanes // across):
            down_ref[layer, at * rows : (at + 1) * rows] = down[:, at * across : (at + 1) * across]


def scatter_down_whole(value):
    seq, dp = lax.axis_size("seq"), lax.axis_size("dp")
    value = lax.all_to_all(value, "seq", split_axis=1, concat_axis=0, tiled=True)
    value = value.reshape(dp, value.shape[0] // dp, value.shape[1])
    for stride in strides(dp):
        mine = bit("dp", stride)
        pairs = value.reshape((value.shape[0] // 2, 2) + value.shape[1:])
        keep = lax.dynamic_index_in_dim(pairs, mine, 1, keepdims=False)
        send = lax.dynamic_index_in_dim(pairs, 1 - mine, 1, keepdims=False)
        value = keep + swap(send, "dp", stride)
    return value[0]


def transpose_down(value):
    seq, dp = lax.axis_size("seq"), lax.axis_size("dp")
    pairs = []
    for z in range(seq):
        for x in range(2):
            for s in range(seq):
                pairs.append((s * dp + 2 * z + x, z * dp + 2 * s + x))
    return lax.ppermute(value, ("seq", "dp"), pairs)


def on_device(
    tokens, lengths, w_qkv, b_qkv, output_weight, w_up, b_up, w_down, gains, shifts, cotangent
):
    sequences, segment, width = tokens.shape
    layers, hidden = b_up.shape
    seq = lax.axis_size("seq")
    count = sequences * segment
    groups = width // WIDE
    pairs = width // PAIR
    position = lax.axis_index("seq") * segment + jnp.arange(segment, dtype=jnp.int32)
    length_col = lengths[:, None]
    inside = (position[None, :] < length_col).astype(F32)
    phases = (
        math.pi
        / 2
        * jnp.minimum(position[None, :], length_col - 1).astype(F32)
        / length_col.astype(F32)
    )
    trig = jnp.stack([jnp.cos(phases), jnp.sin(phases), inside]).reshape(3, count, 1)
    trig = jnp.broadcast_to(trig, (3, count, PAIR))
    b_qkv = b_qkv[:, None, :]
    b_up = b_up[:, None, :]

    rows = (count, width)
    wide = spec((count, WIDE), lambda g, *_: (0, g))
    state_spec = spec((sequences, WIDE // PAIR, STATE, PAIR), lambda g, *_: (0, g, 0, 0))
    state_shape = shaped((sequences, pairs, STATE, PAIR))
    trig_spec = whole((3, count, PAIR))
    full = whole(rows)
    vec_spec = whole((8, width))
    acc = pltpu.VMEM(rows, F32)
    attention_flops = 2 * count * count * 256 * 12

    def qkv_spec(layer, part):
        return spec((None, width, WIDE), lambda g, *_: (layer, 0, part * groups + g))

    def bias_spec(layer, part):
        return spec((None, 1, WIDE), lambda g, *_: (layer, 0, part * groups + g))

    def rows_of(*vectors):
        stacked = jnp.stack(vectors)
        return jnp.concatenate([stacked, jnp.zeros((8 - len(vectors), width), F32)])

    stream, stream_low = tokens.reshape(rows), tokens.reshape(rows)
    saved = []
    block = min(768, hidden)
    order = Order()
    call = order.call
    place = places()
    waiting = []
    for layer in range(layers):
        shift, gain = shifts[layer], gains[layer]
        vec_one = rows_of(shift[:width], gain[:width], shift[width : 2 * width])
        vec_two = rows_of(shift[2 * width : 3 * width], gain[width:], shift[3 * width :])
        key, value, total = call(
            functools.partial(key_value_kernel, sequences),
            (groups,),
            [full, qkv_spec(layer, 1), qkv_spec(layer, 2), bias_spec(layer, 1), bias_spec(layer, 2), trig_spec],
            [wide, wide, state_spec],
            [shaped(rows), shaped(rows), state_shape],
            4 * count * width * width,
            name="key_value",
            after=waiting,
        )(stream_low, w_qkv, w_qkv, b_qkv, b_qkv, trig)
        before = scan_states(total, False)
        stream_other = swap(stream.astype(F32), "seq", 1)
        query, numer, denom = call(
            functools.partial(query_kernel, sequences),
            (groups,),
            [full, qkv_spec(layer, 0), bias_spec(layer, 0), wide, wide, trig_spec],
            [wide, wide, wide],
            [shaped(rows), shaped(rows), shaped(rows)],
            2 * count * width * width + 5 * attention_flops,
            name="query",
        )(stream_low, w_qkv, b_qkv, key, value, trig)
        attended, den, one, normed = call(
            functools.partial(attend_kernel, sequences),
            (groups,),
            [wide, wide, wide, state_spec, trig_spec,
             spec((None, WIDE, width), lambda g, layer=layer: (layer, g, 0)), full, vec_spec],
            [wide, wide, full, full],
            [shaped(rows)] * 4,
            4 * count * width * width,
            scratch=[acc],
            name="attend",
        )(query, numer, denom, before, trig, output_weight, stream, vec_one)
        stream_in = stream
        attended_other = swap(attended, "seq", 1)
        normed_chips = [normed] if layer < layers - 1 else gather_chips(normed)
        pre, two, stream, stream_low = call(
            feed_forward_kernel,
            (hidden // block,),
            [full, spec((None, width, block), lambda g, layer=layer: (layer, 0, g)),
             spec((None, 1, block), lambda g, layer=layer: (layer, 0, g)),
             spec((None, block, width), lambda g, layer=layer: (layer, g, 0)), vec_spec],
            [spec((count, block), lambda g: (0, g)), full, full, full],
            [shaped((count, hidden)), shaped(rows), shaped(rows), shaped(rows, BF16)],
            4 * count * width * hidden,
            scratch=[acc],
            name="feed_forward",
            after=[stream_other],
        )(normed, w_up, b_up, w_down, vec_two)
        normed_core = swap(normed, "seq", 1)
        waiting = [attended_other, normed_core]
        saved.append(
            (normed_chips, stream_in, stream_other, query, key, value, before, attended, attended_other,
             den, one, pre, two, vec_one, vec_two, normed_core)
        )
    mixed = stream_low.reshape(tokens.shape)

    upstream = cotangent.reshape(rows)
    chips, dp = seq // 2, lax.axis_size("dp")
    lanes = 4 * width // seq
    slot = hidden // seq
    size = width // dp
    uppers = [int(size * part) // 8 * 8 for part in BY_Y]
    packed = dp == 2 * seq
    down_shape = (seq // 2, 2, slot // (2 * seq), width) if packed else (slot, width)
    down_count = 2 if packed else 1
    up_shape = (dp // 2, size, slot)
    d_shape = (2, chips, count, lanes)
    x_and_z = [("dp", stride) for stride in strides(dp)]
    above = [("seq", stride) for stride in strides(seq)[1:]]
    work = [dict() for _ in range(layers)]

    def norm_step(layer):
        now = work[layer]
        normed_chips, *unused, two, vec_one, vec_two, normed_core = saved[layer]
        now["d_two"], now["sums_two"] = call(
            second_norm_kernel,
            (1,),
            [full, full, vec_spec],
            [full, vec_spec],
            [shaped(rows), shaped((8, width))],
            count * width * 20,
            name="second_norm",
            after=waiting if layer == layers - 1 else saved[layer][0][1:],
        )(upstream, two, vec_two)
        now["errors"] = gather_chips(now["d_two"])
        if layer == layers - 1:
            now["error_core"] = swap(now["d_two"], "seq", 1)

    def feed_step(layer):
        now = work[layer]
        (normed_chips, stream_in, stream_other, query, key, value, before, attended, attended_other,
         den, one, pre, two, vec_one, vec_two, unused) = saved[layer]
        now["d_one"], now["sums_one"], now["bias_up"] = call(
            feed_back_kernel,
            (hidden // block,),
            [full, spec((None, block, width), lambda g: (layer, g, 0)),
             spec((None, width, block), lambda g: (layer, 0, g)),
             spec((count, block), lambda g: (0, g)), full, vec_spec],
            [full, vec_spec, spec((1, block), lambda g: (0, g))],
            [shaped(rows), shaped((8, width)), shaped((1, hidden))],
            4 * count * width * hidden,
            scratch=[acc],
            name="feed_back",
        )(now["d_two"], w_down, w_up, pre, one, vec_one)

    def state_step(layer):
        now = work[layer]
        (normed_chips, stream_in, stream_other, query, key, value, before, attended, attended_other,
         den, one, pre, two, vec_one, vec_two, unused) = saved[layer]
        now["d_num"], now["d_den"], now["d_state"] = call(
            functools.partial(state_back_kernel, sequences),
            (groups,),
            [full, spec((None, WIDE, width), lambda g: (layer, g, 0)),
             wide, trig_spec, wide, wide],
            [wide, wide, state_spec],
            [shaped(rows), shaped(rows), state_shape],
            4 * count * width * width,
            name="state_back",
            after=[now["error_core"]] if layer == layers - 1 else (),
        )(now["d_one"], output_weight, query, trig, attended, den)

    def scan_step(layer):
        work[layer]["after"] = scan_states(work[layer]["d_state"], True, order)
        if layer > 0:
            normed_chips = saved[layer - 1][0]
            unused, held = gate([normed_chips[0]])
            normed_chips[:] = gather_chips(held[0])

    def inner_step(layer):
        now = work[layer]
        (normed_chips, stream_in, stream_other, query, key, value, before, attended, attended_other,
         den, one, pre, two, vec_one, vec_two, unused) = saved[layer]
        now["inner"] = call(
            functools.partial(inner_back_kernel, sequences),
            (groups,),
            [wide, wide, wide, trig_spec, wide, wide, state_spec],
            [wide, wide, wide],
            [shaped(rows)] * 3,
            15 * attention_flops,
            name="inner_back",
            after=saved[layer][0][1:] if layer == layers - 1 else (),
        )(query, key, value, trig, now["d_num"], now["d_den"], before)

    def gate(held):
        unused, *held = call(
            gate_kernel, (1,), [], [whole((8, PAIR))], [shaped((8, PAIR))], 0, name="gate", carry=held
        )()
        return unused, held

    def gate_step(layer):
        now = work[layer]
        normed_chips = saved[layer][0]
        held = normed_chips[1:] + now["errors"][1:]
        if layer == layers - 1:
            unused, held = gate(held)
            now["mine"] = normed_chips[:1] + held[: chips - 1] + now["errors"][:1] + held[chips - 1 :]
            theirs = [swap(part, "seq", 1) for part in held]
            core = [saved[layer][-1], now["error_core"]]
            now["theirs"] = core[:1] + theirs[: chips - 1] + core[1:] + theirs[chips - 1 :]
        else:
            held = held + now["errors"][:1]
            stacked = (len(held),) + rows
            now["mine"] = normed_chips + now["errors"]
            joint = call(
                stack_kernel, (1,), [whole(rows)] * len(held), [whole(stacked)], [shaped(stacked)], 0, name="stack"
            )(*held)[0]
            now["theirs"] = swap(joint, "seq", 1)
            now["core"] = saved[layer][-1]

    def feed_weights_step(layer):
        now = work[layer]
        first = UP_FIRST[layer] if packed else 1
        stacked = (2 * chips - 1,) + rows
        last = layer == layers - 1
        theirs = now["theirs"] if last else [now["core"], now["theirs"]]
        theirs_specs = [full] * (2 * chips) if last else [full, whole(stacked)]
        up_keep, up_send, *downs = call(
            functools.partial(feed_weights_kernel, chips, packed, first),
            (1,),
            [full] * (2 * chips)
            + theirs_specs
            + [spec((None, width, slot), lambda g, at: (layer, 0, at[0])),
               spec((None, 1, slot), lambda g, at: (layer, 0, at[0])),
               spec((None, slot, width), lambda g, at: (layer, at[0], 0))],
            [whole(up_shape)] * 2 + [whole(down_shape)] * down_count,
            [shaped(up_shape)] * 2 + [shaped(down_shape)] * down_count,
            8 * count * width * hidden,
            prefetch=1,
            vmem=56,
            name="feed_weights",
        )(place, *now["mine"], *theirs, w_up, b_up, w_down)
        parts = (dp // (2 * first), first) + up_shape[1:]
        steps = [("dp", first, 0)] + [("dp", stride, 1) for stride in strides(first)]
        steps += [("dp", stride, 0) for stride in strides(dp) if stride > first]
        now["up"] = Scatter(order, place, up_keep.reshape(parts), up_send.reshape(parts), steps)
        if packed:
            steps = [("dp", 2, 0), ("dp", 1, 1)] + [("dp", 2 * stride, 0) for stride in strides(seq)[1:]]
            now["dn"] = Scatter(order, place, *downs, steps)
        else:
            now["dn"] = scatter_down_whole(*downs)

    def joined_step(layer):
        nonlocal upstream
        now = work[layer]
        (normed_chips, stream_in, stream_other, query, key, value, before, attended, attended_other,
         den, one, pre, two, vec_one, vec_two, unused) = saved[layer]
        upstream, blocks, now["bias_qkv"] = call(
            functools.partial(joined_back_kernel, sequences),
            (groups,),
            [wide, wide, wide, wide, wide, trig_spec, state_spec,
             qkv_spec(layer, 0), qkv_spec(layer, 1), qkv_spec(layer, 2), full],
            [full, whole(d_shape), whole((1, 3 * width))],
            [shaped(rows), shaped(d_shape), shaped((1, 3 * width))],
            6 * count * width * width,
            scratch=[acc, pltpu.VMEM((count, 3 * width), F32)],
            name="joined_back",
        )(*now["inner"], key, value, trig, now["after"], w_qkv, w_qkv, w_qkv, now["d_one"])
        pairs = [[2 * chip, 2 * chip + 1] for chip in range(chips)]
        now["d_blocks"] = lax.all_to_all(blocks, "seq", 0, 0, axis_index_groups=pairs)

    def attention_weights_step(layer):
        now = work[layer]
        (normed_chips, stream_in, stream_other, query, key, value, before, attended, attended_other,
         den, one, pre, two, vec_one, vec_two, unused) = saved[layer]
        upper = uppers[layer]
        y_shape = (chips // 2, dp, upper, lanes)
        x_shape = (chips, dp // 2, size - upper, lanes)
        shapes = ([y_shape] * 2 if upper else []) + ([x_shape] * 2 if upper < size else [])
        found = call(
            functools.partial(attention_weights_kernel, upper),
            (1,),
            [full] * 4 + [whole(d_shape)],
            [whole(shape) for shape in shapes],
            [shaped(shape) for shape in shapes],
            8 * count * width * width,
            prefetch=1,
            name="attention_weights",
        )(place, stream_in, stream_other, attended, attended_other, now["d_blocks"])
        if upper:
            now["by"] = Scatter(
                order, place, *found[:2],
                [(*step, 0) for step in above] + [(*step, 1) for step in x_and_z],
            )
        if upper < size:
            now["bx"] = Scatter(
                order, place, *found[-2:],
                [(*x_and_z[0], 1)] + [(*step, 0) for step in above] + [(*step, 1) for step in x_and_z[1:]],
            )

    def move(layer, name):
        now = work[layer]
        if name in ("ud", "bb"):
            first, second = (now.get(part) for part in {"ud": ("up", "dn"), "bb": ("by", "bx")}[name])
            both = isinstance(first, Scatter) and isinstance(second, Scatter)
            if both and not first.done() and first.fits(second):
                first.advance(second)
                del now["dn" if name == "ud" else "bx"]
            else:
                move(layer, "up" if name == "ud" else "by")
                move(layer, "dn" if name == "ud" else "bx")
            return
        scatter = now.get(name)
        if name == "dt":
            if packed and "down" not in now:
                held = (now.get("dn") or now["up"]).last()
                now["down"] = transpose_down(add(order, *held, at=held[0].shape[0] - 1))
        elif isinstance(scatter, Scatter) and not scatter.done():
            scatter.advance()

    steps = {
        "sn": norm_step, "fb": feed_step, "sb": state_step, "sc": scan_step, "ib": inner_step,
        "ga": gate_step, "fw": feed_weights_step, "jb": joined_step, "aw": attention_weights_step,
    }
    hops = [(axis, stride) for axis in ("seq", "dp") for stride in strides(lax.axis_size(axis))]
    summed = moving = None
    for word in PLAN.split():
        word, unused, wait = word.partition("+")
        name, layer = word[:2], int(word[2:]) - 1
        order.wait = float(wait or 0)
        if name == "ve":
            if summed is None:
                pieces = []
                for now in work:
                    pieces += [now["bias_qkv"], now["bias_up"], now["sums_one"], now["sums_two"]]
                shape = (layers * VECTOR, width)
                summed = call(
                    functools.partial(vector_kernel, layers), (1,), [whole(p.shape) for p in pieces],
                    [whole(shape)], [shaped(shape)], 1, name="vectors",
                )(*pieces)[0]
            elif moving is not None:
                summed, moving = add(order, summed, moving), None
            if hops:
                moving = swap(summed, *hops.pop(0))
        elif name in steps:
            steps[name](layer)
        else:
            move(layer, name)
    while hops or moving is not None:
        summed = add(order, summed, moving)
        moving = swap(summed, *hops.pop(0)) if hops else None
    for _ in range(2 * len(x_and_z) + len(above)):
        for layer in reversed(range(layers)):
            for name in ("up", "dn", "by", "bx"):
                move(layer, name)
    given, counts = [], []
    for layer in range(layers):
        move(layer, "dt")
        now = work[layer]
        begin = len(given)
        for name in ("by", "bx", "up"):
            given += now[name].last() if name in now else ()
        given.append(now["down"] if packed else now["dn"])
        counts.append(len(given) - begin)
    part = 3 * lanes // 4
    out_shapes = [
        shaped((layers, size, part)),
        shaped((layers, size, lanes - part)),
        shaped((layers, size, slot)),
        shaped((layers, hidden // dp, width // seq)),
        shaped((layers, 3 * width)),
        shaped((layers, hidden)),
        shaped((layers, 2 * width)),
        shaped((layers, 4 * width)),
    ]
    given.append(summed)
    outs = call(
        functools.partial(finish_kernel, counts),
        (1,),
        [whole(g.shape) for g in given],
        [whole(o.shape) for o in out_shapes],
        out_shapes,
        1,
        name="finish",
    )(*given)
    return (mixed, upstream.reshape(tokens.shape), *outs)


def solution(mesh):
    in_specs = (
        P("dp", "seq", None),
        P("dp"),
        P(),
        P(),
        P(),
        P(),
        P(),
        P(),
        P(),
        P(),
        P("dp", "seq", None),
    )
    out_specs = (
        P("dp", "seq", None),
        P("dp", "seq", None),
        P(None, "dp", "seq"),
        P(None, "dp", "seq"),
        P(None, "dp", "seq"),
        P(None, "dp", "seq"),
        P(),
        P(),
        P(),
        P(),
    )
    return jax.shard_map(
        on_device, mesh=mesh, in_specs=in_specs, out_specs=out_specs, check_vma=False
    )
```

```python
import functools
import math

import jax
import jax.numpy as jnp
from jax import lax
from jax.experimental import pallas as pl
from jax.experimental.pallas import tpu as pltpu
from jax.sharding import PartitionSpec as P

HEAD = 64
PAIR = 128
WIDE = 256
STATE = 136
VECTOR = 16
EPS = 1e-05
COST = 0.34
TIMES = {
    "key_value": 3.5, "query": 6.0, "attend": 4.0, "feed_forward": 8.0, "second_norm": 1.0, "feed_back": 8.0,
    "state_back": 4.0, "inner_back": 11.0, "feed_weights": 13.0, "joined_back": 8.0, "attention_weights": 5.0,
}
UP_FIRST = (1, 1)
BY_Y = (1.0, 1.0)
PLAN = (
    "sn2", "fb2", "sb2", "ib2", "sc2+5", "ga2+5", "fw2", "jb2", "sn1", "fb1",
    "sb1", "up2", "dn2", "ib1", "sc1", "ga1", "aw2+3", "jb1", "ud2", "ve1",
    "fw1", "ve1", "aw1+4", "by2", "dt2+6", "up1+8", "dn1+6", "ve1+8", "bb2", "dx2",
    "ud1", "ve1+5", "by1", "bb2", "ve1+3", "dt1+10", "bb1+15", "bb1+15",
)
F32 = jnp.float32
BF16 = jnp.bfloat16

NN = (((1,), (0,)), ((), ()))
NT = (((1,), (1,)), ((), ()))
TN = (((0,), (0,)), ((), ()))


def dot(a, b, dims=NN):
    return lax.dot_general(a, b, dims, preferred_element_type=F32)


def split(a):
    high = a.astype(BF16)
    return high, (a - high.astype(F32)).astype(BF16)


def dot3(a, b, dims=NN):
    return dot(a[0], b[0], dims) + (dot(a[0], b[1], dims) + dot(a[1], b[0], dims))


def cut(parts, rows):
    return tuple(part[rows] for part in parts)


def softplus(v):
    return jnp.maximum(v, 0.0) + jnp.log1p(jnp.exp(-jnp.abs(v)))


def sigmoid(v):
    return 1.0 / (1.0 + jnp.exp(-v))


def lanes_of_first(shape):
    lane = lax.broadcasted_iota(jnp.int32, shape, len(shape) - 1)
    return (lane & HEAD) == 0


def causal(tokens, sequences):
    row = lax.broadcasted_iota(jnp.int32, (tokens, tokens), 0)
    column = lax.broadcasted_iota(jnp.int32, (tokens, tokens), 1)
    keep = column <= row
    segment = tokens // sequences
    for later in range(1, sequences):
        keep = keep & ((row < later * segment) | (column >= later * segment))
    return keep


def two_maps(feature, cosine, sine):
    return jnp.concatenate([feature * cosine, feature * sine], axis=1)


def pack_state(full, sums):
    first = lanes_of_first((HEAD, PAIR))
    top = jnp.where(first, full[0:HEAD], full[HEAD : 2 * HEAD])
    low = jnp.where(first, full[2 * HEAD : 3 * HEAD], full[3 * HEAD :])
    rest = jnp.zeros((STATE - 2 * HEAD - 2, PAIR), F32)
    return jnp.concatenate([top, low, sums[:, :PAIR], sums[:, PAIR:], rest], axis=0)


def unpack_state(packed):
    first = lanes_of_first((HEAD, PAIR))
    top, low = packed[0:HEAD], packed[HEAD : 2 * HEAD]
    full = jnp.concatenate(
        [
            jnp.where(first, top, 0.0),
            jnp.where(first, 0.0, top),
            jnp.where(first, low, 0.0),
            jnp.where(first, 0.0, low),
        ],
        axis=0,
    )
    return full, packed[2 * HEAD : 2 * HEAD + 1], packed[2 * HEAD + 1 : 2 * HEAD + 2]


def head_sum(values):
    row = lax.broadcasted_iota(jnp.int32, (PAIR, PAIR), 0)
    column = lax.broadcasted_iota(jnp.int32, (PAIR, PAIR), 1)
    same = jnp.where((row & HEAD) == (column & HEAD), 1.0, 0.0).astype(BF16)
    high, low = split(values)
    return dot(high, same) + dot(low, same)


def norm_parts(residual):
    centre = residual - jnp.mean(residual, axis=-1, keepdims=True)
    rstd = lax.rsqrt(jnp.mean(centre * centre, axis=-1, keepdims=True) + EPS)
    return centre * rstd, rstd


def norm_back(residual, gain, upstream):
    xhat, rstd = norm_parts(residual)
    scaled = gain * upstream
    mean = jnp.mean(scaled, axis=-1, keepdims=True)
    along = jnp.mean(scaled * xhat, axis=-1, keepdims=True)
    grad = rstd * (scaled - mean - xhat * along)
    sums = jnp.concatenate(
        [
            jnp.sum(upstream * xhat, axis=0, keepdims=True),
            jnp.sum(upstream, axis=0, keepdims=True),
            jnp.sum(grad, axis=0, keepdims=True),
            jnp.zeros((5, residual.shape[1]), F32),
        ],
        axis=0,
    )
    return grad, sums


GELU_A = math.sqrt(2.0 / math.pi)
GELU_B = 0.044715


def gelu_terms(v):
    square = v * v
    bent = jnp.tanh(GELU_A * (v + GELU_B * (square * v)))
    return square, bent


def gelu(v):
    unused, bent = gelu_terms(v)
    return 0.5 * v * (1.0 + bent)


def gelu_both(v):
    square, bent = gelu_terms(v)
    slope = 0.5 * (1.0 + bent) + (0.5 * GELU_A) * v * (1.0 - bent * bent) * (
        1.0 + (3.0 * GELU_B) * square
    )
    return 0.5 * v * (1.0 + bent), slope


def spec(block, index):
    return pl.BlockSpec(block, index)


def whole(shape):
    return pl.BlockSpec(shape, lambda *at: (0,) * len(shape))


def shaped(shape, dtype=F32):
    return jax.ShapeDtypeStruct(shape, dtype)


class Order:
    def __init__(self):
        self.last = None
        self.ready = []
        self.wait = 0.0

    def call(self, body, grid, ins, outs, shapes, flops, scratch=(), vmem=40, prefetch=0, name=None, carry=(), after=()):
        after = list(after) + self.ready + ([] if self.last is None else [self.last])
        self.ready = []
        skipped = len(after) + len(carry)
        made = len(shapes)
        anywhere = pl.BlockSpec(memory_space=pl.ANY)

        def kernel(*refs):
            given, rest = refs[:prefetch], refs[prefetch + skipped :]
            body(*given, *rest[: len(ins) + made], *rest[len(ins) + made + len(carry) :])

        run = pl.pallas_call(
            kernel,
            grid_spec=pltpu.PrefetchScalarGridSpec(
                num_scalar_prefetch=prefetch,
                grid=grid,
                in_specs=[anywhere] * skipped + list(ins),
                out_specs=list(outs) + [anywhere] * len(carry),
                scratch_shapes=list(scratch),
            ),
            out_shape=list(shapes) + [shaped(c.shape, c.dtype) for c in carry],
            input_output_aliases={
                prefetch + skipped - len(carry) + at: made + at for at in range(len(carry))
            },
            compiler_params=pltpu.CompilerParams(
                dimension_semantics=("arbitrary",) * len(grid), vmem_limit_bytes=vmem << 20
            ),
            cost_estimate=pl.CostEstimate(
                flops=int((TIMES.get(name, 1.0) + 0.7 + self.wait) * COST * 1.15e9),
                bytes_accessed=0,
                transcendentals=0,
            ),
            name=name,
        )

        def apply(*given):
            found = run(*given[:prefetch], *after, *carry, *given[prefetch:])
            self.last = found[0]
            return found

        return apply


def key_value_kernel(
    sequences, x_ref, wk_ref, wv_ref, bk_ref, bv_ref, trig_ref, jk_ref, jv_ref, state_ref
):
    x = x_ref[...].astype(BF16)
    key = dot(x, wk_ref[...]) + bk_ref[...]
    value = dot(x, wv_ref[...]) + bv_ref[...]
    jk_ref[...] = key
    jv_ref[...] = value
    cosine, sine, inside = trig_ref[0], trig_ref[1], trig_ref[2]
    segment = x.shape[0] // sequences
    for pair in range(WIDE // PAIR):
        lanes = slice(pair * PAIR, (pair + 1) * PAIR)
        maps = two_maps(softplus(key[:, lanes]) * inside, cosine, sine)
        maps_s, value_s = split(maps), split(value[:, lanes])
        for number in range(sequences):
            rows = slice(number * segment, (number + 1) * segment)
            state_ref[number, pair] = pack_state(
                dot3(cut(maps_s, rows), cut(value_s, rows), TN),
                jnp.sum(maps[rows], axis=0, keepdims=True),
            )


def query_kernel(
    sequences, x_ref, wq_ref, bq_ref, jk_ref, jv_ref, trig_ref, jq_ref, numer_ref, denom_ref
):
    x = x_ref[...].astype(BF16)
    query = dot(x, wq_ref[...]) + bq_ref[...]
    jq_ref[...] = query
    cosine, sine, inside = trig_ref[0], trig_ref[1], trig_ref[2]
    tokens = x.shape[0]
    keep = causal(tokens, sequences)
    first_two = lanes_of_first((tokens, 2 * PAIR))
    first = lanes_of_first((tokens, PAIR))
    for pair in range(WIDE // PAIR):
        lanes = slice(pair * PAIR, (pair + 1) * PAIR)
        query_maps = two_maps(softplus(query[:, lanes]), cosine, sine)
        key_s = split(two_maps(softplus(jk_ref[:, lanes]) * inside, cosine, sine))
        value = jv_ref[:, lanes]
        both = []
        for head in range(2):
            masked = jnp.where(first_two, query_maps, 0.0) if head == 0 else jnp.where(first_two, 0.0, query_maps)
            scores = jnp.where(keep, dot3(split(masked), key_s, NT), 0.0)
            ones = jnp.where(first, value, 1.0) if head == 0 else jnp.where(first, 1.0, value)
            both.append(dot3(split(scores), split(ones)))
        numer_ref[:, lanes] = jnp.where(first, both[0], both[1])
        denom_ref[:, lanes] = pltpu.roll(jnp.where(first, both[1], both[0]), HEAD, 1)


def attend_kernel(
    sequences, jq_ref, numer_ref, denom_ref, state_ref, trig_ref, w_ref, res_ref, vec_ref,
    att_ref, den_ref, one_ref, normed_ref, acc_ref,
):
    step = pl.program_id(0)
    cosine, sine = trig_ref[0], trig_ref[1]
    segment = jq_ref.shape[0] // sequences
    for pair in range(WIDE // PAIR):
        lanes = slice(pair * PAIR, (pair + 1) * PAIR)
        for number in range(sequences):
            rows = slice(number * segment, (number + 1) * segment)
            feature = softplus(jq_ref[rows, lanes])
            query_cos, query_sin = feature * cosine[rows], feature * sine[rows]
            full, sum_cos, sum_sin = unpack_state(state_ref[number, pair])
            maps = jnp.concatenate([query_cos, query_sin], axis=1)
            numer = numer_ref[rows, lanes] + dot3(split(maps), split(full))
            denom = denom_ref[rows, lanes] + head_sum(query_cos * sum_cos + query_sin * sum_sin)
            den_ref[rows, lanes] = denom
            att_ref[rows, lanes] = numer / denom
    part = dot(att_ref[...].astype(BF16), w_ref[...])

    @pl.when(step == 0)
    def _():
        acc_ref[...] = part

    @pl.when(step > 0)
    def _():
        acc_ref[...] += part

    @pl.when(step == pl.num_programs(0) - 1)
    def _():
        residual = res_ref[...].astype(F32) + acc_ref[...] + vec_ref[0:1]
        one_ref[...] = residual
        xhat, unused = norm_parts(residual)
        normed_ref[...] = xhat * vec_ref[1:2] + vec_ref[2:3]


def feed_forward_kernel(
    normed_ref, up_ref, bias_ref, down_ref, vec_ref, pre_ref, two_ref, stream_ref, low_ref, acc_ref
):
    step = pl.program_id(0)
    pre = dot(normed_ref[...].astype(BF16), up_ref[...]) + bias_ref[...]
    pre_ref[...] = pre
    part = dot(gelu(pre).astype(BF16), down_ref[...])

    @pl.when(step == 0)
    def _():
        acc_ref[...] = part

    @pl.when(step > 0)
    def _():
        acc_ref[...] += part

    @pl.when(step == pl.num_programs(0) - 1)
    def _():
        residual = normed_ref[...] + acc_ref[...] + vec_ref[0:1]
        two_ref[...] = residual
        xhat, unused = norm_parts(residual)
        stream = xhat * vec_ref[1:2] + vec_ref[2:3]
        stream_ref[...] = stream
        low_ref[...] = stream.astype(BF16)


def second_norm_kernel(up_ref, two_ref, vec_ref, d_ref, sums_ref):
    grad, sums = norm_back(two_ref[...], vec_ref[1:2], up_ref[...].astype(F32))
    d_ref[...] = grad
    sums_ref[...] = sums


def feed_back_kernel(
    d_two_ref, down_ref, up_ref, pre_ref, one_ref, vec_ref,
    d_one_ref, sums_ref, bias_ref, acc_ref,
):
    step = pl.program_id(0)
    d_act = dot(d_two_ref[...].astype(BF16), down_ref[...], NT)
    unused, slope = gelu_both(pre_ref[...])
    d_pre = slope * d_act
    bias_ref[...] = jnp.sum(d_pre, axis=0, keepdims=True)
    part = dot(d_pre.astype(BF16), up_ref[...], NT)

    @pl.when(step == 0)
    def _():
        acc_ref[...] = part

    @pl.when(step > 0)
    def _():
        acc_ref[...] += part

    @pl.when(step == pl.num_programs(0) - 1)
    def _():
        grad, sums = norm_back(one_ref[...], vec_ref[1:2], d_two_ref[...] + acc_ref[...])
        d_one_ref[...] = grad
        sums_ref[...] = sums


def state_back_kernel(
    sequences, d_one_ref, w_ref, jq_ref, trig_ref, att_ref, den_ref, num_ref, dden_ref, state_ref
):
    d_att = dot(d_one_ref[...].astype(BF16), w_ref[...], NT)
    cosine, sine = trig_ref[0], trig_ref[1]
    segment = jq_ref.shape[0] // sequences
    for pair in range(WIDE // PAIR):
        lanes = slice(pair * PAIR, (pair + 1) * PAIR)
        feature = softplus(jq_ref[:, lanes])
        query_cos, query_sin = feature * cosine, feature * sine
        d_num = d_att[:, lanes] / den_ref[:, lanes]
        d_den = -head_sum(d_num * att_ref[:, lanes])
        num_ref[:, lanes] = d_num
        dden_ref[:, lanes] = d_den
        maps_s = split(jnp.concatenate([query_cos, query_sin], axis=1))
        num_s = split(d_num)
        sum_cos, sum_sin = query_cos * d_den, query_sin * d_den
        for number in range(sequences):
            rows = slice(number * segment, (number + 1) * segment)
            sums = jnp.concatenate(
                [
                    jnp.sum(sum_cos[rows], axis=0, keepdims=True),
                    jnp.sum(sum_sin[rows], axis=0, keepdims=True),
                ],
                axis=1,
            )
            state_ref[number, pair] = pack_state(
                dot3(cut(maps_s, rows), cut(num_s, rows), TN), sums
            )


def inner_back_kernel(
    sequences, jq_ref, jk_ref, jv_ref, trig_ref, num_ref, dden_ref, state_ref,
    dq_ref, dk_ref, dv_ref,
):
    cosine, sine, inside = trig_ref[0], trig_ref[1], trig_ref[2]
    tokens = jq_ref.shape[0]
    segment = tokens // sequences
    keep = causal(tokens, sequences)
    first_two = lanes_of_first((tokens, 2 * PAIR))
    first = lanes_of_first((tokens, PAIR))
    for pair in range(WIDE // PAIR):
        lanes = slice(pair * PAIR, (pair + 1) * PAIR)
        query = jq_ref[:, lanes]
        query_maps = two_maps(softplus(query), cosine, sine)
        query_s = split(query_maps)
        key_s = split(two_maps(softplus(jk_ref[:, lanes]) * inside, cosine, sine))
        value = jv_ref[:, lanes]
        d_num, d_den = num_ref[:, lanes], dden_ref[:, lanes]
        num_s = split(d_num)
        moved = pltpu.roll(d_den, HEAD, 1) * (1.0 / HEAD)
        d_query, d_key, d_value = [], [], []
        for head in range(2):
            if head == 0:
                masked = jnp.where(first_two, query_maps, 0.0)
                ones = jnp.where(first, value, 1.0)
                joint = jnp.where(first, d_num, moved)
            else:
                masked = jnp.where(first_two, 0.0, query_maps)
                ones = jnp.where(first, 1.0, value)
                joint = jnp.where(first, moved, d_num)
            scores_s = split(jnp.where(keep, dot3(split(masked), key_s, NT), 0.0))
            grads_s = split(jnp.where(keep, dot3(split(joint), split(ones), NT), 0.0))
            d_query.append(dot3(grads_s, key_s))
            d_key.append(dot3(grads_s, query_s, TN))
            d_value.append(dot3(scores_s, num_s, TN))
        d_query_maps = jnp.where(first_two, d_query[0], d_query[1])
        d_key_maps = jnp.where(first_two, d_key[0], d_key[1])
        from_state = []
        for number in range(sequences):
            rows = slice(number * segment, (number + 1) * segment)
            full, sum_cos, sum_sin = unpack_state(state_ref[number, pair])
            more = dot3(cut(num_s, rows), split(full), NT)
            part = d_den[rows]
            from_state.append(
                more + jnp.concatenate([part * sum_cos, part * sum_sin], axis=1)
            )
        d_query_maps = d_query_maps + (
            from_state[0] if sequences == 1 else jnp.concatenate(from_state, axis=0)
        )
        dq_ref[:, lanes] = sigmoid(query) * (
            d_query_maps[:, :PAIR] * cosine + d_query_maps[:, PAIR:] * sine
        )
        dk_ref[:, lanes] = d_key_maps[:, :PAIR] * cosine + d_key_maps[:, PAIR:] * sine
        dv_ref[:, lanes] = jnp.where(first, d_value[0], d_value[1])


def joined_back_kernel(
    sequences, at_ref, dq_ref, dk_ref, dv_ref, jk_ref, jv_ref, trig_ref, state_ref,
    wq_ref, wk_ref, wv_ref, d_one_ref,
    up_ref, mine_ref, sum_ref, *rest,
):
    *other_refs, acc_ref, join_ref = rest
    step = pl.program_id(0)
    steps = 3
    cosine, sine, inside = trig_ref[0], trig_ref[1], trig_ref[2]
    segment = jk_ref.shape[0] // sequences
    keys, values = [], []
    for pair in range(WIDE // PAIR):
        lanes = slice(pair * PAIR, (pair + 1) * PAIR)
        key = jk_ref[:, lanes]
        maps_s = split(two_maps(softplus(key) * inside, cosine, sine))
        value_s = split(jv_ref[:, lanes])
        d_key, d_value = [], []
        for number in range(sequences):
            rows = slice(number * segment, (number + 1) * segment)
            full, sum_cos, sum_sin = unpack_state(state_ref[number, pair])
            full_s = split(full)
            back = dot3(cut(value_s, rows), full_s, NT)
            d_key.append(
                (back[:, :PAIR] + sum_cos) * cosine[rows] + (back[:, PAIR:] + sum_sin) * sine[rows]
            )
            d_value.append(dot3(cut(maps_s, rows), full_s))
        d_key = d_key[0] if sequences == 1 else jnp.concatenate(d_key, axis=0)
        d_value = d_value[0] if sequences == 1 else jnp.concatenate(d_value, axis=0)
        keys.append(inside * sigmoid(key) * (dk_ref[:, lanes] + d_key))
        values.append(dv_ref[:, lanes] + d_value)
    three = (dq_ref[...], jnp.concatenate(keys, axis=1), jnp.concatenate(values, axis=1))
    part = (
        dot(three[0].astype(BF16), wq_ref[...], NT)
        + dot(three[1].astype(BF16), wk_ref[...], NT)
        + dot(three[2].astype(BF16), wv_ref[...], NT)
    )
    for at in range(steps):

        @pl.when(step == at)
        def _(at=at):
            for group, block in enumerate(three):
                begin = (group * steps + at) * WIDE
                join_ref[:, begin : begin + WIDE] = block

    @pl.when(step == 0)
    def _():
        acc_ref[...] = d_one_ref[...] + part

    @pl.when(step > 0)
    def _():
        acc_ref[...] += part

    @pl.when(step == steps - 1)
    def _():
        up_ref[...] = acc_ref[...]
        sum_ref[...] = jnp.sum(join_ref[...], axis=0, keepdims=True)
        chips = mine_ref.shape[0]
        part, part_one = join_ref.shape[1] // (2 * chips), d_one_ref.shape[1] // (2 * chips)
        for core in range(2):

            @pl.when(at_ref[place_of("seq", 1)] == core)
            def _(core=core):
                for block in range(2 * chips):
                    others = other_refs[0] if len(other_refs) == 1 else other_refs[block // 2]
                    ref = mine_ref if block % 2 == core else others
                    ref[block // 2 % ref.shape[0]] = jnp.concatenate(
                        [
                            join_ref[:, block * part : (block + 1) * part],
                            d_one_ref[:, block * part_one : (block + 1) * part_one],
                        ],
                        axis=1,
                    )


def feed_weights_kernel(chips, packed, first, at_ref, *refs):
    mine, theirs, rest = refs[: 2 * chips], refs[2 * chips : 4 * chips], refs[4 * chips :]
    up_ref, bias_ref, down_ref, up_keep_ref, up_send_ref, *down_refs = rest
    pairs = list(zip(mine[:chips], mine[chips:])) + list(zip(theirs[:chips], theirs[chips:]))
    up, down, bias = up_ref[...], down_ref[...], bias_ref[...]
    d_up = d_down = None
    for n_ref, e_ref in pairs:
        n, e = n_ref[...].astype(BF16), e_ref[...].astype(BF16)
        act, slope = gelu_both(dot(n, up) + bias)
        d_pre = slope * dot(e, down, NT)
        more_up = dot(n, d_pre.astype(BF16), TN)
        more_down = dot(act.astype(BF16), e, TN)
        d_up = more_up if d_up is None else d_up + more_up
        d_down = more_down if d_down is None else d_down + more_down
    def down_piece(x, z, rows):
        groups = blocks // 2
        lanes = d_down.shape[1] // groups
        top, begin = x * groups * rows, z * lanes
        columns = d_down[:, begin : begin + lanes]
        return jnp.concatenate([columns[top + at * rows : top + (at + 1) * rows] for at in range(groups)], axis=1)

    if first == 0:
        halves, unused, rows, unused = up_keep_ref.shape
        blocks = 2 * halves
        for mine in range(2):

            @pl.when(at_ref[place_of("dp", 1)] == mine)
            def _(mine=mine):
                for block in range(blocks):
                    ref = up_keep_ref if block % 2 == mine else up_send_ref
                    ref[block // 2, 0] = d_up[block * rows : (block + 1) * rows]
                    ref[block // 2, 1] = down_piece(block % 2, block // 2, rows)

        return
    halves, rows, unused = up_keep_ref.shape
    blocks = 2 * halves
    for mine in range(2):

        @pl.when(at_ref[place_of("dp", first)] == mine)
        def _(mine=mine):
            for block in range(blocks):
                ref = up_keep_ref if block // first % 2 == mine else up_send_ref
                ref[block // (2 * first) * first + block % first] = d_up[block * rows : (block + 1) * rows]

    if not packed:
        down_refs[0][...] = d_down
        return
    keep_ref, send_ref = down_refs
    others, unused, rows, unused = keep_ref.shape
    for z in range(2):

        @pl.when(at_ref[place_of("dp", 2)] == z)
        def _(z=z):
            for low, ref in ((z, keep_ref), (1 - z, send_ref)):
                for x in range(2):
                    for high in range(others):
                        ref[high, x] = down_piece(x, 2 * high + low, rows)


def attention_weights_kernel(
    rows, many, at_ref, x_ref, x_other_ref, a_ref, a_other_ref, d_ref, *outs
):
    others, outs = outs[:many], outs[many:]
    chips = d_ref.shape[0]
    part = 3 * d_ref.shape[2] // 4
    both = (x_ref, x_other_ref), (a_ref, a_other_ref)
    inputs = [jnp.concatenate([r[...].astype(BF16) for r in refs], axis=0) for refs in both]
    grads = []
    for chip in range(chips):
        other = others[0][chip] if many == 1 else others[chip][0]
        errors = jnp.concatenate([d_ref[chip].astype(BF16), other.astype(BF16)], axis=0)
        grads.append(
            jnp.concatenate(
                [dot(inputs[0], errors[:, :part], TN), dot(inputs[1], errors[:, part:], TN)], axis=1
            )
        )
    by_y, by_x = outs[:2] if rows else (), outs[-2:] if len(outs) == 4 or not rows else ()
    high, blocks = by_y[0].shape[:2] if by_y else (chips // 2, 2 * by_x[0].shape[1])
    more = by_x[0].shape[2] if by_x else 0
    size = rows + more
    for y in range(2 if by_y else 0):

        @pl.when(at_ref[place_of("seq", 2)] == y)
        def _(y=y):
            for low, ref in ((y, by_y[0]), (1 - y, by_y[1])):
                for upper in range(high):
                    for block in range(blocks):
                        ref[upper, block] = grads[2 * upper + low][block * size : block * size + rows]

    for x in range(2 if by_x else 0):

        @pl.when(at_ref[place_of("dp", 1)] == x)
        def _(x=x):
            for parity, ref in ((x, by_x[0]), (1 - x, by_x[1])):
                for chip in range(chips):
                    for block in range(blocks // 2):
                        begin = (2 * block + parity) * size + rows
                        ref[chip, block] = grads[chip][begin : begin + more]


def gate_kernel(out_ref):
    out_ref[...] = jnp.zeros_like(out_ref)


def swap(value, axis, stride):
    return lax.ppermute(value, axis, [(i, i ^ stride) for i in range(lax.axis_size(axis))])


def strides(count):
    found, stride = [], 1
    while stride < count:
        found.append(stride)
        stride *= 2
    return found


def bit(axis, stride):
    return (lax.axis_index(axis) // stride) % 2


def places():
    found = [lax.axis_index("seq")]
    for axis in ("seq", "dp"):
        found += [bit(axis, stride) for stride in strides(lax.axis_size(axis))]
    return jnp.stack(found).astype(jnp.int32)


def place_of(axis, stride):
    spot = 1 + strides(lax.axis_size(axis)).index(stride)
    return spot if axis == "seq" else spot + len(strides(lax.axis_size("seq")))


def scan_states(total, backward, order=None):
    before = None
    for stride in strides(lax.axis_size("seq")):
        other = swap(total, "seq", stride)
        mine = bit("seq", stride)
        takes = (mine == 0) if backward else (mine == 1)
        more = jnp.where(takes, other, 0.0)
        before = more if before is None else before + more
        if order is None or stride > 1:
            total = total + other
        else:
            total = add(order, total, other)
    return before


def gather_chips(value):
    held = [value]
    for stride in reversed(strides(lax.axis_size("seq"))[1:]):
        held = held + [swap(part, "seq", stride) for part in held]
    return held


def gather_cores(held):
    return held + [swap(part, "seq", 1) for part in held]


def halve_kernel(at_ref, *refs):
    kept_ref, sent_ref = refs[-2:]
    for at in range(kept_ref.shape[1]):
        keep_mine, recv_mine, keep_other, recv_other = refs[4 * at : 4 * at + 4]
        kept_ref[:, at] = keep_mine[...] + recv_mine[...]
        sent_ref[:, at] = keep_other[...] + recv_other[...]


def add_kernel(one_ref, two_ref, out_ref):
    out_ref[...] = one_ref[...] + two_ref[...]


class Scatter:
    def __init__(self, order, place, keep, send, steps):
        self.order, self.place, self.keep, self.steps = order, place, keep, list(steps)
        self.recv = self.swap(send)

    def swap(self, send):
        axis, stride, self.at = self.steps.pop(0)
        return swap(send, axis, stride)

    def done(self):
        return not self.steps

    def fits(self, other):
        return self.keep.shape == other.keep.shape and self.steps == other.steps

    def advance(self, *others):
        axis, stride, at = self.steps[0]
        shape = self.keep.shape
        rows, lanes = shape[-2:]
        outer = math.prod(shape[:at]) * shape[at] // 2
        inner = math.prod(shape[at + 1 : -2])
        flat = (outer, 2, inner, rows, lanes)
        parts = (self,) + others
        pieces = 2 if rows % 16 == 0 and outer < 4 else 1
        block = (None, None, inner, rows // pieces, lanes)
        spot = place_of(axis, stride)
        mine = spec(block, lambda a, r, at: (a, at[spot], 0, r, 0))
        other = spec(block, lambda a, r, at: (a, 1 - at[spot], 0, r, 0))
        out = spec((None, inner, len(parts), rows // pieces, lanes), lambda a, r, at: (a, 0, 0, r, 0))
        given = []
        for part in parts:
            given += [part.keep.reshape(flat), part.recv.reshape(flat)] * 2
        kept, sent = self.order.call(
            halve_kernel,
            (outer, pieces),
            [mine, mine, other, other] * len(parts),
            [out, out],
            [shaped((outer, inner, len(parts), rows, lanes))] * 2,
            1,
            prefetch=1,
            name="halve",
        )(self.place, *given)
        left = shape[:at] + (shape[at] // 2,) + shape[at + 1 : -2] + (len(parts), rows, lanes)
        if len(parts) == 1:
            left = left[:-3] + left[-2:]
        self.keep = kept.reshape(left)
        self.recv = self.swap(sent.reshape(left))
        for part in others:
            part.steps = []

    def last(self):
        rows, lanes = self.keep.shape[-2:]
        shape = (-1, rows, lanes)
        return self.keep.reshape(shape), self.recv.reshape(shape)


def add(order, one, two, at=None):
    if at is None:
        given = out = whole(one.shape)
        shape = one.shape
    else:
        shape = one.shape[1:]
        given = spec((None,) + shape, lambda g: (at,) + (0,) * len(shape))
        out = whole(shape)
    return order.call(add_kernel, (1,), [given] * 2, [out], [shaped(shape)], 1, name="add")(one, two)[0]


def vector_kernel(layers, *refs):
    out_ref = refs[-1]
    out_ref[...] = jnp.zeros_like(out_ref)
    width = out_ref.shape[1]
    for layer in range(layers):
        qkv_ref, up_ref, one_ref, two_ref = refs[4 * layer : 4 * layer + 4]
        rows = []
        for ref in (qkv_ref, up_ref):
            rows += [ref[0:1, at : at + width] for at in range(0, ref.shape[1], width)]
        rows += [one_ref[0:1], two_ref[0:1], one_ref[2:3], one_ref[1:2], two_ref[2:3], two_ref[1:2]]
        for at, row in enumerate(rows):
            out_ref[layer * VECTOR + at : layer * VECTOR + at + 1] = row


def finish_kernel(counts, *refs):
    vector_ref, qkv_ref, out_ref, up_ref, down_ref, *vector_refs = refs[-9:]
    width = vector_ref.shape[1]
    begin = 0
    for ref in vector_refs:
        many = ref.shape[1] // width
        for layer in range(len(counts)):
            for at in range(many):
                row = layer * VECTOR + begin + at
                ref[layer : layer + 1, at * width : (at + 1) * width] = vector_ref[row : row + 1]
        begin += many
    part = qkv_ref.shape[2]
    for layer, many in enumerate(counts):
        given = refs[sum(counts[:layer]) :][:many]
        begin = 0
        for at in range(0, many - 3, 2):
            keep, recv = given[at : at + 2]
            for piece in range(keep.shape[0]):
                total = keep[piece] + recv[piece]
                rows = total.shape[0]
                qkv_ref[layer, begin : begin + rows] = total[:, :part]
                out_ref[layer, begin : begin + rows] = total[:, part:]
                begin += rows
        up_ref[layer] = given[many - 3][0] + given[many - 2][0]
        down = given[many - 1]
        rows, lanes = down.shape
        across = down_ref.shape[2]
        for at in range(lanes // across):
            down_ref[layer, at * rows : (at + 1) * rows] = down[:, at * across : (at + 1) * across]


def scatter_down_whole(value):
    seq, dp = lax.axis_size("seq"), lax.axis_size("dp")
    value = lax.all_to_all(value, "seq", split_axis=1, concat_axis=0, tiled=True)
    value = value.reshape(dp, value.shape[0] // dp, value.shape[1])
    for stride in strides(dp):
        mine = bit("dp", stride)
        pairs = value.reshape((value.shape[0] // 2, 2) + value.shape[1:])
        keep = lax.dynamic_index_in_dim(pairs, mine, 1, keepdims=False)
        send = lax.dynamic_index_in_dim(pairs, 1 - mine, 1, keepdims=False)
        value = keep + swap(send, "dp", stride)
    return value[0]


def transpose_down(value):
    seq, dp = lax.axis_size("seq"), lax.axis_size("dp")
    pairs = []
    for z in range(seq):
        for x in range(2):
            for s in range(seq):
                pairs.append((s * dp + 2 * z + x, z * dp + 2 * s + x))
    return lax.ppermute(value, ("seq", "dp"), pairs)


def on_device(
    tokens, lengths, w_qkv, b_qkv, output_weight, w_up, b_up, w_down, gains, shifts, cotangent
):
    sequences, segment, width = tokens.shape
    layers, hidden = b_up.shape
    seq = lax.axis_size("seq")
    count = sequences * segment
    groups = width // WIDE
    pairs = width // PAIR
    position = lax.axis_index("seq") * segment + jnp.arange(segment, dtype=jnp.int32)
    length_col = lengths[:, None]
    inside = (position[None, :] < length_col).astype(F32)
    phases = (
        math.pi
        / 2
        * jnp.minimum(position[None, :], length_col - 1).astype(F32)
        / length_col.astype(F32)
    )
    trig = jnp.stack([jnp.cos(phases), jnp.sin(phases), inside]).reshape(3, count, 1)
    trig = jnp.broadcast_to(trig, (3, count, PAIR))
    b_qkv = b_qkv[:, None, :]
    b_up = b_up[:, None, :]

    rows = (count, width)
    wide = spec((count, WIDE), lambda g, *_: (0, g))
    state_spec = spec((sequences, WIDE // PAIR, STATE, PAIR), lambda g, *_: (0, g, 0, 0))
    state_shape = shaped((sequences, pairs, STATE, PAIR))
    trig_spec = whole((3, count, PAIR))
    full = whole(rows)
    vec_spec = whole((8, width))
    acc = pltpu.VMEM(rows, F32)
    attention_flops = 2 * count * count * 256 * 12

    def qkv_spec(layer, part):
        return spec((None, width, WIDE), lambda g, *_: (layer, 0, part * groups + g))

    def bias_spec(layer, part):
        return spec((None, 1, WIDE), lambda g, *_: (layer, 0, part * groups + g))

    def rows_of(*vectors):
        stacked = jnp.stack(vectors)
        return jnp.concatenate([stacked, jnp.zeros((8 - len(vectors), width), F32)])

    stream, stream_low = tokens.reshape(rows), tokens.reshape(rows)
    saved = []
    block = min(768, hidden)
    order = Order()
    call = order.call
    place = places()
    waiting = []
    for layer in range(layers):
        shift, gain = shifts[layer], gains[layer]
        vec_one = rows_of(shift[:width], gain[:width], shift[width : 2 * width])
        vec_two = rows_of(shift[2 * width : 3 * width], gain[width:], shift[3 * width :])
        key, value, total = call(
            functools.partial(key_value_kernel, sequences),
            (groups,),
            [full, qkv_spec(layer, 1), qkv_spec(layer, 2), bias_spec(layer, 1), bias_spec(layer, 2), trig_spec],
            [wide, wide, state_spec],
            [shaped(rows), shaped(rows), state_shape],
            4 * count * width * width,
            name="key_value",
            after=waiting,
        )(stream_low, w_qkv, w_qkv, b_qkv, b_qkv, trig)
        before = scan_states(total, False)
        stream_other = swap(stream.astype(F32), "seq", 1)
        query, numer, denom = call(
            functools.partial(query_kernel, sequences),
            (groups,),
            [full, qkv_spec(layer, 0), bias_spec(layer, 0), wide, wide, trig_spec],
            [wide, wide, wide],
            [shaped(rows), shaped(rows), shaped(rows)],
            2 * count * width * width + 5 * attention_flops,
            name="query",
        )(stream_low, w_qkv, b_qkv, key, value, trig)
        attended, den, one, normed = call(
            functools.partial(attend_kernel, sequences),
            (groups,),
            [wide, wide, wide, state_spec, trig_spec,
             spec((None, WIDE, width), lambda g, layer=layer: (layer, g, 0)), full, vec_spec],
            [wide, wide, full, full],
            [shaped(rows)] * 4,
            4 * count * width * width,
            scratch=[acc],
            name="attend",
        )(query, numer, denom, before, trig, output_weight, stream, vec_one)
        stream_in = stream
        attended_other = swap(attended, "seq", 1)
        normed_chips = [normed] if layer < layers - 1 else gather_chips(normed)
        pre, two, stream, stream_low = call(
            feed_forward_kernel,
            (hidden // block,),
            [full, spec((None, width, block), lambda g, layer=layer: (layer, 0, g)),
             spec((None, 1, block), lambda g, layer=layer: (layer, 0, g)),
             spec((None, block, width), lambda g, layer=layer: (layer, g, 0)), vec_spec],
            [spec((count, block), lambda g: (0, g)), full, full, full],
            [shaped((count, hidden)), shaped(rows), shaped(rows), shaped(rows, BF16)],
            4 * count * width * hidden,
            scratch=[acc],
            name="feed_forward",
            after=[stream_other],
        )(normed, w_up, b_up, w_down, vec_two)
        normed_core = swap(normed, "seq", 1)
        waiting = [attended_other, normed_core]
        saved.append(
            (normed_chips, stream_in, stream_other, query, key, value, before, attended, attended_other,
             den, one, pre, two, vec_one, vec_two, normed_core)
        )
    mixed = stream_low.reshape(tokens.shape)

    upstream = cotangent.reshape(rows)
    chips, dp = seq // 2, lax.axis_size("dp")
    lanes = 4 * width // seq
    slot = hidden // seq
    size = width // dp
    uppers = [int(size * part) // 8 * 8 for part in BY_Y]
    packed = dp == 2 * seq
    down_shape = (seq // 2, 2, slot // (2 * seq), width) if packed else (slot, width)
    down_count = 2 if packed else 1
    up_shape = (dp // 2, size, slot)
    d_shape = (chips, count, lanes)
    x_and_z = [("dp", stride) for stride in strides(dp)]
    above = [("seq", stride) for stride in strides(seq)[1:]]
    work = [dict() for _ in range(layers)]

    def norm_step(layer):
        now = work[layer]
        normed_chips, *unused, two, vec_one, vec_two, normed_core = saved[layer]
        carry = [] if layer == layers - 1 else normed_chips[1:]
        now["d_two"], now["sums_two"], *carry = call(
            second_norm_kernel,
            (1,),
            [full, full, vec_spec],
            [full, vec_spec],
            [shaped(rows), shaped((8, width))],
            count * width * 20,
            name="second_norm",
            after=waiting if layer == layers - 1 else (),
            carry=carry,
        )(upstream, two, vec_two)
        now["errors"] = gather_chips(now["d_two"])
        now["error_core"] = swap(now["d_two"], "seq", 1)
        if layer < layers - 1:
            normed_chips[1:] = carry
            now["normed_cores"] = [swap(part, "seq", 1) for part in carry]

    def feed_step(layer):
        now = work[layer]
        (normed_chips, stream_in, stream_other, query, key, value, before, attended, attended_other,
         den, one, pre, two, vec_one, vec_two, unused) = saved[layer]
        now["d_one"], now["sums_one"], now["bias_up"] = call(
            feed_back_kernel,
            (hidden // block,),
            [full, spec((None, block, width), lambda g: (layer, g, 0)),
             spec((None, width, block), lambda g: (layer, 0, g)),
             spec((count, block), lambda g: (0, g)), full, vec_spec],
            [full, vec_spec, spec((1, block), lambda g: (0, g))],
            [shaped(rows), shaped((8, width)), shaped((1, hidden))],
            4 * count * width * hidden,
            scratch=[acc],
            name="feed_back",
        )(now["d_two"], w_down, w_up, pre, one, vec_one)

    def state_step(layer):
        now = work[layer]
        (normed_chips, stream_in, stream_other, query, key, value, before, attended, attended_other,
         den, one, pre, two, vec_one, vec_two, unused) = saved[layer]
        now["d_num"], now["d_den"], now["d_state"] = call(
            functools.partial(state_back_kernel, sequences),
            (groups,),
            [full, spec((None, WIDE, width), lambda g: (layer, g, 0)),
             wide, trig_spec, wide, wide],
            [wide, wide, state_spec],
            [shaped(rows), shaped(rows), state_shape],
            4 * count * width * width,
            name="state_back",
            after=[] if layer == layers - 1 else [now["error_core"]] + now["normed_cores"],
        )(now["d_one"], output_weight, query, trig, attended, den)

    def scan_step(layer):
        work[layer]["after"] = scan_states(work[layer]["d_state"], True, order)
        if layer > 0:
            normed_chips = saved[layer - 1][0]
            unused, held = gate([normed_chips[0]])
            normed_chips[:] = gather_chips(held[0])

    def inner_step(layer):
        now = work[layer]
        (normed_chips, stream_in, stream_other, query, key, value, before, attended, attended_other,
         den, one, pre, two, vec_one, vec_two, unused) = saved[layer]
        now["inner"] = call(
            functools.partial(inner_back_kernel, sequences),
            (groups,),
            [wide, wide, wide, trig_spec, wide, wide, state_spec],
            [wide, wide, wide],
            [shaped(rows)] * 3,
            15 * attention_flops,
            name="inner_back",
            after=saved[layer][0][1:] if layer == layers - 1 else (),
        )(query, key, value, trig, now["d_num"], now["d_den"], before)

    def gate(held):
        unused, *held = call(
            gate_kernel, (1,), [], [whole((8, PAIR))], [shaped((8, PAIR))], 0, name="gate", carry=held
        )()
        return unused, held

    def gate_step(layer):
        now = work[layer]
        held = now["errors"][1:]
        if layer == layers - 1:
            held = saved[layer][0][1:] + held
        unused, held = gate(held)
        if layer == layers - 1:
            saved[layer][0][1:] = held[: chips - 1]
            now["normed_cores"] = [swap(part, "seq", 1) for part in held[: chips - 1]]
        now["errors"][1:] = held[1 - chips :]
        now["error_cores"] = [swap(part, "seq", 1) for part in held[1 - chips :]]

    def feed_weights_step(layer):
        now = work[layer]
        first = UP_FIRST[layer] if packed else 1
        mine = saved[layer][0] + now["errors"]
        theirs = [saved[layer][-1]] + now["normed_cores"] + [now["error_core"]] + now["error_cores"]
        shapes = [(dp // 2, 2, size, width)] * 2 if first == 0 else [up_shape] * 2 + [down_shape] * down_count
        up_keep, up_send, *downs = call(
            functools.partial(feed_weights_kernel, chips, packed, first),
            (1,),
            [full] * (4 * chips)
            + [spec((None, width, slot), lambda g, at: (layer, 0, at[0])),
               spec((None, 1, slot), lambda g, at: (layer, 0, at[0])),
               spec((None, slot, width), lambda g, at: (layer, at[0], 0))],
            [whole(shape) for shape in shapes],
            [shaped(shape) for shape in shapes],
            8 * count * width * hidden,
            prefetch=1,
            vmem=56,
            name="feed_weights",
        )(place, *mine, *theirs, w_up, b_up, w_down)
        if first == 0:
            now["up"] = Scatter(order, place, up_keep, up_send, [("dp", stride, 0) for stride in strides(dp)])
            return
        parts = (dp // (2 * first), first) + up_shape[1:]
        steps = [("dp", first, 0)] + [("dp", stride, 1) for stride in strides(first)]
        steps += [("dp", stride, 0) for stride in strides(dp) if stride > first]
        now["up"] = Scatter(order, place, up_keep.reshape(parts), up_send.reshape(parts), steps)
        if packed:
            steps = [("dp", 2, 0), ("dp", 1, 1)] + [("dp", 2 * stride, 0) for stride in strides(seq)[1:]]
            now["dn"] = Scatter(order, place, *downs, steps)
        else:
            now["dn"] = scatter_down_whole(*downs)

    def joined_step(layer):
        nonlocal upstream
        now = work[layer]
        (normed_chips, stream_in, stream_other, query, key, value, before, attended, attended_other,
         den, one, pre, two, vec_one, vec_two, unused) = saved[layer]
        sends = [(1,) + d_shape[1:]] * chips if layer == 0 else [d_shape]
        upstream, now["d_mine"], now["bias_qkv"], *d_sends = call(
            functools.partial(joined_back_kernel, sequences),
            (groups,),
            [wide, wide, wide, wide, wide, trig_spec, state_spec,
             qkv_spec(layer, 0), qkv_spec(layer, 1), qkv_spec(layer, 2), full],
            [full, whole(d_shape), whole((1, 3 * width))] + [whole(shape) for shape in sends],
            [shaped(rows), shaped(d_shape), shaped((1, 3 * width))] + [shaped(shape) for shape in sends],
            6 * count * width * width,
            scratch=[acc, pltpu.VMEM((count, 3 * width), F32)],
            prefetch=1,
            name="joined_back",
        )(place, *now["inner"], key, value, trig, now["after"], w_qkv, w_qkv, w_qkv, now["d_one"])
        now["d_other"] = [swap(part, "seq", 1) for part in d_sends]

    def attention_weights_step(layer):
        now = work[layer]
        (normed_chips, stream_in, stream_other, query, key, value, before, attended, attended_other,
         den, one, pre, two, vec_one, vec_two, unused) = saved[layer]
        upper = uppers[layer]
        y_shape = (chips // 2, dp, upper, lanes)
        x_shape = (chips, dp // 2, size - upper, lanes)
        shapes = ([y_shape] * 2 if upper else []) + ([x_shape] * 2 if upper < size else [])
        found = call(
            functools.partial(attention_weights_kernel, upper, len(now["d_other"])),
            (1,),
            [full] * 4 + [whole(d_shape)] + [whole(part.shape) for part in now["d_other"]],
            [whole(shape) for shape in shapes],
            [shaped(shape) for shape in shapes],
            8 * count * width * width,
            prefetch=1,
            name="attention_weights",
        )(place, stream_in, stream_other, attended, attended_other, now["d_mine"], *now["d_other"])
        if upper:
            now["by"] = Scatter(
                order, place, *found[:2],
                [(*step, 0) for step in above] + [(*step, 1) for step in x_and_z],
            )
        if upper < size:
            now["bx"] = Scatter(
                order, place, *found[-2:],
                [(*x_and_z[0], 1)] + [(*step, 0) for step in above] + [(*step, 1) for step in x_and_z[1:]],
            )

    def move(layer, name):
        now = work[layer]
        if name == "ud" and UP_FIRST[layer] == 0 and packed:
            name = "up"
        if name in ("ud", "bb"):
            first, second = (now.get(part) for part in {"ud": ("up", "dn"), "bb": ("by", "bx")}[name])
            both = isinstance(first, Scatter) and isinstance(second, Scatter)
            if both and not first.done() and first.fits(second):
                first.advance(second)
                del now["dn" if name == "ud" else "bx"]
            else:
                move(layer, "up" if name == "ud" else "by")
                move(layer, "dn" if name == "ud" else "bx")
            return
        scatter = now.get(name)
        if name == "dx":
            order.ready = [now["down"]] if "down" in now else []
        elif name == "dt":
            if packed and "down" not in now:
                held = (now.get("dn") or now["up"]).last()
                now["down"] = transpose_down(add(order, *held, at=held[0].shape[0] - 1))
        elif isinstance(scatter, Scatter) and not scatter.done():
            scatter.advance()

    steps = {
        "sn": norm_step, "fb": feed_step, "sb": state_step, "sc": scan_step, "ib": inner_step,
        "ga": gate_step, "fw": feed_weights_step, "jb": joined_step, "aw": attention_weights_step,
    }
    hops = [("dp", stride) for stride in strides(dp)[1:]] + [("seq", stride) for stride in strides(seq)]
    hops.append(("dp", 1))
    summed = moving = None
    for word in PLAN:
        word, unused, wait = word.partition("+")
        name, layer = word[:2], int(word[2:]) - 1
        order.wait = float(wait or 0)
        if name == "ve":
            if summed is None:
                pieces = []
                for now in work:
                    pieces += [now["bias_qkv"], now["bias_up"], now["sums_one"], now["sums_two"]]
                shape = (layers * VECTOR, width)
                summed = call(
                    functools.partial(vector_kernel, layers), (1,), [whole(p.shape) for p in pieces],
                    [whole(shape)], [shaped(shape)], 1, name="vectors",
                )(*pieces)[0]
            elif moving is not None:
                summed, moving = add(order, summed, moving), None
            if hops:
                moving = swap(summed, *hops.pop(0))
        elif name in steps:
            steps[name](layer)
        else:
            move(layer, name)
    while hops or moving is not None:
        summed = add(order, summed, moving)
        moving = swap(summed, *hops.pop(0)) if hops else None
    for _ in range(2 * len(x_and_z) + len(above)):
        for layer in reversed(range(layers)):
            for name in ("up", "dn", "by", "bx"):
                move(layer, name)
    given, counts = [], []
    for layer in range(layers):
        move(layer, "dt")
        now = work[layer]
        begin = len(given)
        for name in ("by", "bx", "up"):
            given += now[name].last() if name in now else ()
        given.append(now["down"] if packed else now["dn"])
        counts.append(len(given) - begin)
    part = 3 * lanes // 4
    out_shapes = [
        shaped((layers, size, part)),
        shaped((layers, size, lanes - part)),
        shaped((layers, size, slot)),
        shaped((layers, hidden // dp, width // seq)),
        shaped((layers, 3 * width)),
        shaped((layers, hidden)),
        shaped((layers, 2 * width)),
        shaped((layers, 4 * width)),
    ]
    given.append(summed)
    outs = call(
        functools.partial(finish_kernel, counts),
        (1,),
        [whole(g.shape) for g in given],
        [whole(o.shape) for o in out_shapes],
        out_shapes,
        1,
        name="finish",
    )(*given)
    return (mixed, upstream.reshape(tokens.shape), *outs)


def solution(mesh):
    in_specs = (
        P("dp", "seq", None),
        P("dp"),
        P(),
        P(),
        P(),
        P(),
        P(),
        P(),
        P(),
        P(),
        P("dp", "seq", None),
    )
    out_specs = (
        P("dp", "seq", None),
        P("dp", "seq", None),
        P(None, "dp", "seq"),
        P(None, "dp", "seq"),
        P(None, "dp", "seq"),
        P(None, "dp", "seq"),
        P(),
        P(),
        P(),
        P(),
    )
    return jax.shard_map(
        on_device, mesh=mesh, in_specs=in_specs, out_specs=out_specs, check_vma=False
    )
```

```python
import functools
import math

import jax
import jax.numpy as jnp
from jax import lax
from jax.experimental import pallas as pl
from jax.experimental.pallas import tpu as pltpu
from jax.sharding import PartitionSpec as P

HEAD = 64
PAIR = 128
WIDE = 256
STATE = 136
VECTOR = 16
EPS = 1e-05
COST = 0.28
TIMES = {
    "key_value": 3.5, "query": 6.0, "attend": 4.0, "feed_forward": 8.0, "second_norm": 1.0, "feed_back": 8.0,
    "state_back": 4.0, "inner_back": 7.0, "feed_weights": 13.0, "joined_back": 8.0, "attention_weights": 5.0,
}
UP_FIRST = (1, 1)
BY_Y = (1.0, 1.0)
PLAN = (
    "sn2", "fb2", "sb2", "ib2", "ga2+5", "sc2", "fw2", "jb2", "sn1", "fb1",
    "sb1", "up2", "dn2", "ib1", "sc1", "ga1+8", "ud2", "sx1", "aw2", "jb1",
    "ve1", "fw1", "ve1", "dt2", "aw1+8", "by2", "up1+8", "dn1+8", "dx2", "ve1+6",
    "bb2+5", "ud1+8", "bb2", "by1", "ve1+20", "dt1", "bb1+8", "ba2+5", "dx1", "bb1+15",
    "ve1",
)
F32 = jnp.float32
BF16 = jnp.bfloat16

NN = (((1,), (0,)), ((), ()))
NT = (((1,), (1,)), ((), ()))
TN = (((0,), (0,)), ((), ()))


def dot(a, b, dims=NN):
    return lax.dot_general(a, b, dims, preferred_element_type=F32)


def split(a):
    high = a.astype(BF16)
    return high, (a - high.astype(F32)).astype(BF16)


def dot3(a, b, dims=NN):
    return dot(a[0], b[0], dims) + (dot(a[0], b[1], dims) + dot(a[1], b[0], dims))


def dot2(a, b, dims=NN):
    return dot(a, b[0], dims) + dot(a, b[1], dims)


def cut(parts, rows):
    return tuple(part[rows] for part in parts)


def softplus(v):
    return jnp.maximum(v, 0.0) + jnp.log1p(jnp.exp(-jnp.abs(v)))


def sigmoid(v):
    return 1.0 / (1.0 + jnp.exp(-v))


def lanes_of_first(shape):
    lane = lax.broadcasted_iota(jnp.int32, shape, len(shape) - 1)
    return (lane & HEAD) == 0


def causal(tokens, sequences):
    row = lax.broadcasted_iota(jnp.int32, (tokens, tokens), 0)
    column = lax.broadcasted_iota(jnp.int32, (tokens, tokens), 1)
    keep = column <= row
    segment = tokens // sequences
    for later in range(1, sequences):
        keep = keep & ((row < later * segment) | (column >= later * segment))
    return keep


def two_maps(feature, cosine, sine):
    return jnp.concatenate([feature * cosine, feature * sine], axis=1)


def pack_state(full, sums):
    first = lanes_of_first((HEAD, PAIR))
    top = jnp.where(first, full[0:HEAD], full[HEAD : 2 * HEAD])
    low = jnp.where(first, full[2 * HEAD : 3 * HEAD], full[3 * HEAD :])
    rest = jnp.zeros((STATE - 2 * HEAD - 2, PAIR), F32)
    return jnp.concatenate([top, low, sums[:, :PAIR], sums[:, PAIR:], rest], axis=0)


def unpack_state(packed):
    first = lanes_of_first((HEAD, PAIR))
    top, low = packed[0:HEAD], packed[HEAD : 2 * HEAD]
    full = jnp.concatenate(
        [
            jnp.where(first, top, 0.0),
            jnp.where(first, 0.0, top),
            jnp.where(first, low, 0.0),
            jnp.where(first, 0.0, low),
        ],
        axis=0,
    )
    return full, packed[2 * HEAD : 2 * HEAD + 1], packed[2 * HEAD + 1 : 2 * HEAD + 2]


def head_sum(values):
    row = lax.broadcasted_iota(jnp.int32, (PAIR, PAIR), 0)
    column = lax.broadcasted_iota(jnp.int32, (PAIR, PAIR), 1)
    same = jnp.where((row & HEAD) == (column & HEAD), 1.0, 0.0).astype(BF16)
    high, low = split(values)
    return dot(high, same) + dot(low, same)


def norm_parts(residual):
    centre = residual - jnp.mean(residual, axis=-1, keepdims=True)
    rstd = lax.rsqrt(jnp.mean(centre * centre, axis=-1, keepdims=True) + EPS)
    return centre * rstd, rstd


def norm_back(residual, gain, upstream):
    xhat, rstd = norm_parts(residual)
    scaled = gain * upstream
    mean = jnp.mean(scaled, axis=-1, keepdims=True)
    along = jnp.mean(scaled * xhat, axis=-1, keepdims=True)
    grad = rstd * (scaled - mean - xhat * along)
    sums = jnp.concatenate(
        [
            jnp.sum(upstream * xhat, axis=0, keepdims=True),
            jnp.sum(upstream, axis=0, keepdims=True),
            jnp.sum(grad, axis=0, keepdims=True),
            jnp.zeros((5, residual.shape[1]), F32),
        ],
        axis=0,
    )
    return grad, sums


GELU_A = math.sqrt(2.0 / math.pi)
GELU_B = 0.044715


def gelu_terms(v):
    square = v * v
    bent = jnp.tanh(GELU_A * (v + GELU_B * (square * v)))
    return square, bent


def gelu(v):
    unused, bent = gelu_terms(v)
    return 0.5 * v * (1.0 + bent)


def gelu_both(v):
    square, bent = gelu_terms(v)
    slope = 0.5 * (1.0 + bent) + (0.5 * GELU_A) * v * (1.0 - bent * bent) * (
        1.0 + (3.0 * GELU_B) * square
    )
    return 0.5 * v * (1.0 + bent), slope


def spec(block, index):
    return pl.BlockSpec(block, index)


def whole(shape):
    return pl.BlockSpec(shape, lambda *at: (0,) * len(shape))


def shaped(shape, dtype=F32):
    return jax.ShapeDtypeStruct(shape, dtype)


class Order:
    def __init__(self):
        self.last = None
        self.ready = []
        self.wait = 0.0

    def call(self, body, grid, ins, outs, shapes, flops, scratch=(), vmem=40, prefetch=0, name=None, carry=(), after=()):
        after = list(after) + self.ready + ([] if self.last is None else [self.last])
        self.ready = []
        skipped = len(after) + len(carry)
        made = len(shapes)
        anywhere = pl.BlockSpec(memory_space=pl.ANY)

        def kernel(*refs):
            given, rest = refs[:prefetch], refs[prefetch + skipped :]
            body(*given, *rest[: len(ins) + made], *rest[len(ins) + made + len(carry) :])

        run = pl.pallas_call(
            kernel,
            grid_spec=pltpu.PrefetchScalarGridSpec(
                num_scalar_prefetch=prefetch,
                grid=grid,
                in_specs=[anywhere] * skipped + list(ins),
                out_specs=list(outs) + [anywhere] * len(carry),
                scratch_shapes=list(scratch),
            ),
            out_shape=list(shapes) + [shaped(c.shape, c.dtype) for c in carry],
            input_output_aliases={
                prefetch + skipped - len(carry) + at: made + at for at in range(len(carry))
            },
            compiler_params=pltpu.CompilerParams(
                dimension_semantics=("arbitrary",) * len(grid), vmem_limit_bytes=vmem << 20
            ),
            cost_estimate=pl.CostEstimate(
                flops=int((TIMES.get(name, 1.0) + 0.7 + self.wait) * COST * 1.15e9),
                bytes_accessed=0,
                transcendentals=0,
            ),
            name=name,
        )

        def apply(*given):
            found = run(*given[:prefetch], *after, *carry, *given[prefetch:])
            self.last = found[0]
            return found

        return apply


def key_value_kernel(
    sequences, x_ref, wk_ref, wv_ref, bk_ref, bv_ref, trig_ref, jk_ref, jv_ref, state_ref
):
    x = x_ref[...].astype(BF16)
    key = dot(x, wk_ref[...]) + bk_ref[...]
    value = dot(x, wv_ref[...]) + bv_ref[...]
    jk_ref[...] = key
    jv_ref[...] = value
    cosine, sine, inside = trig_ref[0], trig_ref[1], trig_ref[2]
    segment = x.shape[0] // sequences
    for pair in range(WIDE // PAIR):
        lanes = slice(pair * PAIR, (pair + 1) * PAIR)
        maps = two_maps(softplus(key[:, lanes]) * inside, cosine, sine)
        maps_s, value_s = split(maps), split(value[:, lanes])
        for number in range(sequences):
            rows = slice(number * segment, (number + 1) * segment)
            state_ref[number, pair] = pack_state(
                dot3(cut(maps_s, rows), cut(value_s, rows), TN),
                jnp.sum(maps[rows], axis=0, keepdims=True),
            )


def query_kernel(
    sequences, x_ref, wq_ref, bq_ref, jk_ref, jv_ref, trig_ref, jq_ref, numer_ref, denom_ref
):
    x = x_ref[...].astype(BF16)
    query = dot(x, wq_ref[...]) + bq_ref[...]
    jq_ref[...] = query
    cosine, sine, inside = trig_ref[0], trig_ref[1], trig_ref[2]
    tokens = x.shape[0]
    keep = causal(tokens, sequences)
    first_two = lanes_of_first((tokens, 2 * PAIR))
    first = lanes_of_first((tokens, PAIR))
    for pair in range(WIDE // PAIR):
        lanes = slice(pair * PAIR, (pair + 1) * PAIR)
        query_maps = two_maps(softplus(query[:, lanes]), cosine, sine)
        key_maps = two_maps(softplus(jk_ref[:, lanes]) * inside, cosine, sine).astype(BF16)
        value = jv_ref[:, lanes]
        both = []
        for head in range(2):
            masked = jnp.where(first_two, query_maps, 0.0) if head == 0 else jnp.where(first_two, 0.0, query_maps)
            scores = jnp.where(keep, dot(masked.astype(BF16), key_maps, NT), 0.0)
            ones = jnp.where(first, value, 1.0) if head == 0 else jnp.where(first, 1.0, value)
            both.append(dot2(scores.astype(BF16), split(ones)))
        numer_ref[:, lanes] = jnp.where(first, both[0], both[1])
        denom_ref[:, lanes] = pltpu.roll(jnp.where(first, both[1], both[0]), HEAD, 1)


def attend_kernel(
    sequences, steps, at_ref, jq_ref, numer_ref, denom_ref, trig_ref, w_ref, res_ref, vec_ref, *rest
):
    state_refs, (att_ref, den_ref, one_ref, normed_ref, acc_ref) = rest[:steps], rest[steps:]
    step = pl.program_id(0)
    cosine, sine = trig_ref[0], trig_ref[1]
    segment = jq_ref.shape[0] // sequences
    for pair in range(WIDE // PAIR):
        lanes = slice(pair * PAIR, (pair + 1) * PAIR)
        for number in range(sequences):
            rows = slice(number * segment, (number + 1) * segment)
            feature = softplus(jq_ref[rows, lanes])
            maps = jnp.concatenate([feature * cosine[rows], feature * sine[rows]], axis=1).astype(BF16)
            full, sum_cos, sum_sin = unpack_state(add_states(at_ref, state_refs, number, pair, False))
            numer = numer_ref[rows, lanes] + dot2(maps, split(full))
            query_cos, query_sin = maps[:, :PAIR].astype(F32), maps[:, PAIR:].astype(F32)
            denom = denom_ref[rows, lanes] + head_sum(query_cos * sum_cos + query_sin * sum_sin)
            den_ref[rows, lanes] = denom
            att_ref[rows, lanes] = numer / denom
    part = dot(att_ref[...].astype(BF16), w_ref[...])

    @pl.when(step == 0)
    def _():
        acc_ref[...] = part

    @pl.when(step > 0)
    def _():
        acc_ref[...] += part

    @pl.when(step == pl.num_programs(0) - 1)
    def _():
        residual = res_ref[...].astype(F32) + acc_ref[...] + vec_ref[0:1]
        one_ref[...] = residual
        xhat, unused = norm_parts(residual)
        normed_ref[...] = xhat * vec_ref[1:2] + vec_ref[2:3]


def feed_forward_kernel(
    normed_ref, up_ref, bias_ref, down_ref, vec_ref, pre_ref, two_ref, stream_ref, low_ref, acc_ref
):
    step = pl.program_id(0)
    pre = dot(normed_ref[...].astype(BF16), up_ref[...]) + bias_ref[...]
    pre_ref[...] = pre
    part = dot(gelu(pre).astype(BF16), down_ref[...])

    @pl.when(step == 0)
    def _():
        acc_ref[...] = part

    @pl.when(step > 0)
    def _():
        acc_ref[...] += part

    @pl.when(step == pl.num_programs(0) - 1)
    def _():
        residual = normed_ref[...] + acc_ref[...] + vec_ref[0:1]
        two_ref[...] = residual
        xhat, unused = norm_parts(residual)
        stream = xhat * vec_ref[1:2] + vec_ref[2:3]
        stream_ref[...] = stream
        low_ref[...] = stream.astype(BF16)


def second_norm_kernel(up_ref, two_ref, vec_ref, d_ref, sums_ref):
    grad, sums = norm_back(two_ref[...], vec_ref[1:2], up_ref[...].astype(F32))
    d_ref[...] = grad
    sums_ref[...] = sums


def feed_back_kernel(
    d_two_ref, down_ref, up_ref, pre_ref, one_ref, vec_ref,
    d_one_ref, sums_ref, bias_ref, acc_ref,
):
    step = pl.program_id(0)
    d_act = dot(d_two_ref[...].astype(BF16), down_ref[...], NT)
    unused, slope = gelu_both(pre_ref[...])
    d_pre = slope * d_act
    bias_ref[...] = jnp.sum(d_pre, axis=0, keepdims=True)
    part = dot(d_pre.astype(BF16), up_ref[...], NT)

    @pl.when(step == 0)
    def _():
        acc_ref[...] = part

    @pl.when(step > 0)
    def _():
        acc_ref[...] += part

    @pl.when(step == pl.num_programs(0) - 1)
    def _():
        grad, sums = norm_back(one_ref[...], vec_ref[1:2], d_two_ref[...] + acc_ref[...])
        d_one_ref[...] = grad
        sums_ref[...] = sums


def state_back_kernel(
    sequences, d_one_ref, w_ref, jq_ref, trig_ref, att_ref, den_ref, num_ref, dden_ref, state_ref
):
    d_att = dot(d_one_ref[...].astype(BF16), w_ref[...], NT)
    cosine, sine = trig_ref[0], trig_ref[1]
    segment = jq_ref.shape[0] // sequences
    for pair in range(WIDE // PAIR):
        lanes = slice(pair * PAIR, (pair + 1) * PAIR)
        feature = softplus(jq_ref[:, lanes])
        query_cos, query_sin = feature * cosine, feature * sine
        d_num = d_att[:, lanes] / den_ref[:, lanes]
        d_den = -head_sum(d_num * att_ref[:, lanes])
        num_ref[:, lanes] = d_num
        dden_ref[:, lanes] = d_den
        maps_s = split(jnp.concatenate([query_cos, query_sin], axis=1))
        num_s = split(d_num)
        sum_cos, sum_sin = query_cos * d_den, query_sin * d_den
        for number in range(sequences):
            rows = slice(number * segment, (number + 1) * segment)
            sums = jnp.concatenate(
                [
                    jnp.sum(sum_cos[rows], axis=0, keepdims=True),
                    jnp.sum(sum_sin[rows], axis=0, keepdims=True),
                ],
                axis=1,
            )
            state_ref[number, pair] = pack_state(
                dot3(cut(maps_s, rows), cut(num_s, rows), TN), sums
            )


def inner_back_kernel(
    sequences, at_ref, jq_ref, jk_ref, jv_ref, trig_ref, num_ref, dden_ref, *rest
):
    *state_refs, dq_ref, dk_ref, dv_ref = rest
    cosine, sine, inside = trig_ref[0], trig_ref[1], trig_ref[2]
    tokens = jq_ref.shape[0]
    segment = tokens // sequences
    keep = causal(tokens, sequences)
    first_two = lanes_of_first((tokens, 2 * PAIR))
    first = lanes_of_first((tokens, PAIR))
    for pair in range(WIDE // PAIR):
        lanes = slice(pair * PAIR, (pair + 1) * PAIR)
        query = jq_ref[:, lanes]
        query_maps = two_maps(softplus(query), cosine, sine)
        query_low = query_maps.astype(BF16)
        key_low = two_maps(softplus(jk_ref[:, lanes]) * inside, cosine, sine).astype(BF16)
        value = jv_ref[:, lanes]
        d_num, d_den = num_ref[:, lanes], dden_ref[:, lanes]
        num_s = split(d_num)
        moved = pltpu.roll(d_den, HEAD, 1) * (1.0 / HEAD)
        d_query, d_key, d_value = [], [], []
        for head in range(2):
            if head == 0:
                masked = jnp.where(first_two, query_maps, 0.0)
                ones = jnp.where(first, value, 1.0)
                joint = jnp.where(first, d_num, moved)
            else:
                masked = jnp.where(first_two, 0.0, query_maps)
                ones = jnp.where(first, 1.0, value)
                joint = jnp.where(first, moved, d_num)
            scores = jnp.where(keep, dot(masked.astype(BF16), key_low, NT), 0.0).astype(BF16)
            grads = jnp.where(keep, dot3(split(joint), split(ones), NT), 0.0).astype(BF16)
            d_query.append(dot(grads, key_low))
            d_key.append(dot(grads, query_low, TN))
            d_value.append(dot(scores, num_s[0], TN))
        d_query_maps = jnp.where(first_two, d_query[0], d_query[1])
        d_key_maps = jnp.where(first_two, d_key[0], d_key[1])
        from_state = []
        for number in range(sequences):
            rows = slice(number * segment, (number + 1) * segment)
            full, sum_cos, sum_sin = unpack_state(add_states(at_ref, state_refs, number, pair, False))
            more = dot3(cut(num_s, rows), split(full), NT)
            part = d_den[rows]
            from_state.append(
                more + jnp.concatenate([part * sum_cos, part * sum_sin], axis=1)
            )
        d_query_maps = d_query_maps + (
            from_state[0] if sequences == 1 else jnp.concatenate(from_state, axis=0)
        )
        dq_ref[:, lanes] = sigmoid(query) * (
            d_query_maps[:, :PAIR] * cosine + d_query_maps[:, PAIR:] * sine
        )
        dk_ref[:, lanes] = d_key_maps[:, :PAIR] * cosine + d_key_maps[:, PAIR:] * sine
        dv_ref[:, lanes] = jnp.where(first, d_value[0], d_value[1])


def joined_back_kernel(
    sequences, scan, at_ref, dq_ref, dk_ref, dv_ref, jk_ref, jv_ref, trig_ref,
    wq_ref, wk_ref, wv_ref, d_one_ref, *rest,
):
    state_refs, (up_ref, mine_ref, sum_ref, *other_refs, acc_ref, join_ref) = rest[:scan], rest[scan:]
    step = pl.program_id(0)
    steps = 3
    cosine, sine, inside = trig_ref[0], trig_ref[1], trig_ref[2]
    segment = jk_ref.shape[0] // sequences
    keys, values = [], []
    for pair in range(WIDE // PAIR):
        lanes = slice(pair * PAIR, (pair + 1) * PAIR)
        key = jk_ref[:, lanes]
        maps_s = split(two_maps(softplus(key) * inside, cosine, sine))
        value_s = split(jv_ref[:, lanes])
        d_key, d_value = [], []
        for number in range(sequences):
            rows = slice(number * segment, (number + 1) * segment)
            full, sum_cos, sum_sin = unpack_state(add_states(at_ref, state_refs, number, pair, True))
            full_s = split(full)
            back = dot3(cut(value_s, rows), full_s, NT)
            d_key.append(
                (back[:, :PAIR] + sum_cos) * cosine[rows] + (back[:, PAIR:] + sum_sin) * sine[rows]
            )
            d_value.append(dot3(cut(maps_s, rows), full_s))
        d_key = d_key[0] if sequences == 1 else jnp.concatenate(d_key, axis=0)
        d_value = d_value[0] if sequences == 1 else jnp.concatenate(d_value, axis=0)
        keys.append(inside * sigmoid(key) * (dk_ref[:, lanes] + d_key))
        values.append(dv_ref[:, lanes] + d_value)
    three = (dq_ref[...], jnp.concatenate(keys, axis=1), jnp.concatenate(values, axis=1))
    part = (
        dot(three[0].astype(BF16), wq_ref[...], NT)
        + dot(three[1].astype(BF16), wk_ref[...], NT)
        + dot(three[2].astype(BF16), wv_ref[...], NT)
    )
    for at in range(steps):

        @pl.when(step == at)
        def _(at=at):
            for group, block in enumerate(three):
                begin = (group * steps + at) * WIDE
                join_ref[:, begin : begin + WIDE] = block

    @pl.when(step == 0)
    def _():
        acc_ref[...] = d_one_ref[...] + part

    @pl.when(step > 0)
    def _():
        acc_ref[...] += part

    @pl.when(step == steps - 1)
    def _():
        up_ref[...] = acc_ref[...]
        sum_ref[...] = jnp.sum(join_ref[...], axis=0, keepdims=True)
        chips = mine_ref.shape[0]
        part, part_one = join_ref.shape[1] // (2 * chips), d_one_ref.shape[1] // (2 * chips)
        for core in range(2):

            @pl.when(at_ref[place_of("seq", 1)] == core)
            def _(core=core):
                for block in range(2 * chips):
                    others = other_refs[0] if len(other_refs) == 1 else other_refs[block // 2]
                    ref = mine_ref if block % 2 == core else others
                    ref[block // 2 % ref.shape[0]] = jnp.concatenate(
                        [
                            join_ref[:, block * part : (block + 1) * part],
                            d_one_ref[:, block * part_one : (block + 1) * part_one],
                        ],
                        axis=1,
                    )


def feed_weights_kernel(chips, packed, first, at_ref, *refs):
    mine, theirs, rest = refs[: 2 * chips], refs[2 * chips : 4 * chips], refs[4 * chips :]
    up_ref, bias_ref, down_ref, up_keep_ref, up_send_ref, *down_refs = rest
    pairs = list(zip(mine[:chips], mine[chips:])) + list(zip(theirs[:chips], theirs[chips:]))
    up, down, bias = up_ref[...], down_ref[...], bias_ref[...]
    normed, errors, ups, acts = [], [], [], []
    for n_ref, e_ref in pairs:
        n, e = n_ref[...].astype(BF16), e_ref[...].astype(BF16)
        act, slope = gelu_both(dot(n, up) + bias)
        normed.append(n)
        errors.append(e)
        ups.append((slope * dot(e, down, NT)).astype(BF16))
        acts.append(act.astype(BF16))
    normed, errors, ups, acts = (jnp.concatenate(parts, axis=0) for parts in (normed, errors, ups, acts))
    d_up = dot(normed, ups, TN)
    d_down = dot(acts, errors, TN)

    def down_piece(x, z, rows):
        groups = blocks // 2
        lanes = d_down.shape[1] // groups
        top, begin = x * groups * rows, z * lanes
        columns = d_down[:, begin : begin + lanes]
        return jnp.concatenate([columns[top + at * rows : top + (at + 1) * rows] for at in range(groups)], axis=1)

    if first == 0:
        halves, unused, rows, unused = up_keep_ref.shape
        blocks = 2 * halves
        for mine in range(2):

            @pl.when(at_ref[place_of("dp", 1)] == mine)
            def _(mine=mine):
                for block in range(blocks):
                    ref = up_keep_ref if block % 2 == mine else up_send_ref
                    ref[block // 2, 0] = d_up[block * rows : (block + 1) * rows]
                    ref[block // 2, 1] = down_piece(block % 2, block // 2, rows)

        return
    halves, rows, unused = up_keep_ref.shape
    blocks = 2 * halves
    for mine in range(2):

        @pl.when(at_ref[place_of("dp", first)] == mine)
        def _(mine=mine):
            for block in range(blocks):
                ref = up_keep_ref if block // first % 2 == mine else up_send_ref
                ref[block // (2 * first) * first + block % first] = d_up[block * rows : (block + 1) * rows]

    if not packed:
        down_refs[0][...] = d_down
        return
    keep_ref, send_ref = down_refs
    others, unused, rows, unused = keep_ref.shape
    for z in range(2):

        @pl.when(at_ref[place_of("dp", 2)] == z)
        def _(z=z):
            for low, ref in ((z, keep_ref), (1 - z, send_ref)):
                for x in range(2):
                    for high in range(others):
                        ref[high, x] = down_piece(x, 2 * high + low, rows)


def attention_weights_kernel(
    rows, many, at_ref, x_ref, x_other_ref, a_ref, a_other_ref, d_ref, *outs
):
    others, outs = outs[:many], outs[many:]
    chips = d_ref.shape[0]
    part = 3 * d_ref.shape[2] // 4
    both = (x_ref, x_other_ref), (a_ref, a_other_ref)
    inputs = [jnp.concatenate([r[...].astype(BF16) for r in refs], axis=0) for refs in both]
    grads = []
    for chip in range(chips):
        other = others[0][chip] if many == 1 else others[chip][0]
        errors = jnp.concatenate([d_ref[chip].astype(BF16), other.astype(BF16)], axis=0)
        grads.append(
            jnp.concatenate(
                [dot(inputs[0], errors[:, :part], TN), dot(inputs[1], errors[:, part:], TN)], axis=1
            )
        )
    by_y, by_x = outs[:2] if rows else (), outs[-2:] if len(outs) == 4 or not rows else ()
    high, blocks = by_y[0].shape[:2] if by_y else (chips // 2, 2 * by_x[0].shape[1])
    more = by_x[0].shape[2] if by_x else 0
    size = rows + more
    for y in range(2 if by_y else 0):

        @pl.when(at_ref[place_of("seq", 2)] == y)
        def _(y=y):
            for low, ref in ((y, by_y[0]), (1 - y, by_y[1])):
                for upper in range(high):
                    for block in range(blocks):
                        ref[upper, block] = grads[2 * upper + low][block * size : block * size + rows]

    for x in range(2 if by_x else 0):

        @pl.when(at_ref[place_of("dp", 1)] == x)
        def _(x=x):
            for parity, ref in ((x, by_x[0]), (1 - x, by_x[1])):
                for chip in range(chips):
                    for block in range(blocks // 2):
                        begin = (2 * block + parity) * size + rows
                        ref[chip, block] = grads[chip][begin : begin + more]


def gate_kernel(out_ref):
    out_ref[...] = jnp.zeros_like(out_ref)


def swap(value, axis, stride):
    return lax.ppermute(value, axis, [(i, i ^ stride) for i in range(lax.axis_size(axis))])


def strides(count):
    found, stride = [], 1
    while stride < count:
        found.append(stride)
        stride *= 2
    return found


def bit(axis, stride):
    return (lax.axis_index(axis) // stride) % 2


def places():
    found = [lax.axis_index("seq")]
    for axis in ("seq", "dp"):
        found += [bit(axis, stride) for stride in strides(lax.axis_size(axis))]
    return jnp.stack(found).astype(jnp.int32)


def place_of(axis, stride):
    spot = 1 + strides(lax.axis_size(axis)).index(stride)
    return spot if axis == "seq" else spot + len(strides(lax.axis_size("seq")))


def scan_states(total, order=None):
    steps = strides(lax.axis_size("seq"))
    others = []
    for stride in steps:
        others.append(swap(total, "seq", stride))
        if stride < steps[-1]:
            total = total + others[-1] if order is None else add(order, total, others[-1])
    return others


def add_states(at_ref, refs, number, pair, backward):
    total = None
    for step, ref in enumerate(refs):
        part = ref[number, pair]
        part = jnp.where((at_ref[1 + step] == 0) == backward, part, jnp.zeros_like(part))
        total = part if total is None else total + part
    return total


def gather_chips(value):
    held = [value]
    for stride in reversed(strides(lax.axis_size("seq"))[1:]):
        held = held + [swap(part, "seq", stride) for part in held]
    return held


def gather_cores(held):
    return held + [swap(part, "seq", 1) for part in held]


def halve_kernel(at_ref, *refs):
    kept_ref, sent_ref = refs[-2:]
    for at in range(kept_ref.shape[1]):
        keep_mine, recv_mine, keep_other, recv_other = refs[4 * at : 4 * at + 4]
        kept_ref[:, at] = keep_mine[...] + recv_mine[...]
        sent_ref[:, at] = keep_other[...] + recv_other[...]


def add_kernel(one_ref, two_ref, out_ref):
    out_ref[...] = one_ref[...] + two_ref[...]


class Scatter:
    def __init__(self, order, place, keep, send, steps):
        self.order, self.place, self.keep, self.steps = order, place, keep, list(steps)
        self.recv = self.swap(send)

    def swap(self, send):
        axis, stride, self.at = self.steps.pop(0)
        return swap(send, axis, stride)

    def done(self):
        return not self.steps

    def fits(self, other):
        return self.keep.shape == other.keep.shape and self.steps == other.steps

    def advance(self, *others):
        axis, stride, at = self.steps[0]
        shape = self.keep.shape
        rows, lanes = shape[-2:]
        outer = math.prod(shape[:at]) * shape[at] // 2
        inner = math.prod(shape[at + 1 : -2])
        flat = (outer, 2, inner, rows, lanes)
        parts = (self,) + others
        pieces = 2 if rows % 16 == 0 and outer < 4 else 1
        block = (None, None, inner, rows // pieces, lanes)
        spot = place_of(axis, stride)
        mine = spec(block, lambda a, r, at: (a, at[spot], 0, r, 0))
        other = spec(block, lambda a, r, at: (a, 1 - at[spot], 0, r, 0))
        out = spec((None, inner, len(parts), rows // pieces, lanes), lambda a, r, at: (a, 0, 0, r, 0))
        given = []
        for part in parts:
            given += [part.keep.reshape(flat), part.recv.reshape(flat)] * 2
        kept, sent = self.order.call(
            halve_kernel,
            (outer, pieces),
            [mine, mine, other, other] * len(parts),
            [out, out],
            [shaped((outer, inner, len(parts), rows, lanes))] * 2,
            1,
            prefetch=1,
            name="halve",
        )(self.place, *given)
        left = shape[:at] + (shape[at] // 2,) + shape[at + 1 : -2] + (len(parts), rows, lanes)
        if len(parts) == 1:
            left = left[:-3] + left[-2:]
        self.keep = kept.reshape(left)
        self.recv = self.swap(sent.reshape(left))
        for part in others:
            part.steps = []

    def last(self):
        rows, lanes = self.keep.shape[-2:]
        shape = (-1, rows, lanes)
        return [part.reshape(shape) for part in (self.keep, self.recv) if part is not None]


def add(order, one, two, at=None):
    if at is None:
        given = out = whole(one.shape)
        shape = one.shape
    else:
        shape = one.shape[1:]
        given = spec((None,) + shape, lambda g: (at,) + (0,) * len(shape))
        out = whole(shape)
    return order.call(add_kernel, (1,), [given] * 2, [out], [shaped(shape)], 1, name="add")(one, two)[0]


def vector_kernel(layers, *refs):
    out_ref = refs[-1]
    out_ref[...] = jnp.zeros_like(out_ref)
    width = out_ref.shape[1]
    for layer in range(layers):
        qkv_ref, up_ref, one_ref, two_ref = refs[4 * layer : 4 * layer + 4]
        rows = []
        for ref in (qkv_ref, up_ref):
            rows += [ref[0:1, at : at + width] for at in range(0, ref.shape[1], width)]
        rows += [one_ref[0:1], two_ref[0:1], one_ref[2:3], one_ref[1:2], two_ref[2:3], two_ref[1:2]]
        for at, row in enumerate(rows):
            out_ref[layer * VECTOR + at : layer * VECTOR + at + 1] = row


def finish_kernel(counts, *refs):
    vector_ref, qkv_ref, out_ref, up_ref, down_ref, *vector_refs = refs[-9:]
    width = vector_ref.shape[1]
    begin = 0
    for ref in vector_refs:
        many = ref.shape[1] // width
        for layer in range(len(counts)):
            for at in range(many):
                row = layer * VECTOR + begin + at
                ref[layer : layer + 1, at * width : (at + 1) * width] = vector_ref[row : row + 1]
        begin += many
    part = qkv_ref.shape[2]
    given = list(refs)
    for layer, many in enumerate(counts):
        sums = []
        for number in many:
            sums.append(given[:number])
            given = given[number:]
        down, given = given[0], given[1:]
        begin = 0
        for parts in sums[:-1]:
            for piece in range(parts[0].shape[0]):
                total = sum(part[piece] for part in parts[1:]) + parts[0][piece]
                rows = total.shape[0]
                qkv_ref[layer, begin : begin + rows] = total[:, :part]
                out_ref[layer, begin : begin + rows] = total[:, part:]
                begin += rows
        up_ref[layer] = sum(part[0] for part in sums[-1][1:]) + sums[-1][0][0]
        rows, lanes = down.shape
        across = down_ref.shape[2]
        for at in range(lanes // across):
            down_ref[layer, at * rows : (at + 1) * rows] = down[:, at * across : (at + 1) * across]


def scatter_down_whole(value):
    seq, dp = lax.axis_size("seq"), lax.axis_size("dp")
    value = lax.all_to_all(value, "seq", split_axis=1, concat_axis=0, tiled=True)
    value = value.reshape(dp, value.shape[0] // dp, value.shape[1])
    for stride in strides(dp):
        mine = bit("dp", stride)
        pairs = value.reshape((value.shape[0] // 2, 2) + value.shape[1:])
        keep = lax.dynamic_index_in_dim(pairs, mine, 1, keepdims=False)
        send = lax.dynamic_index_in_dim(pairs, 1 - mine, 1, keepdims=False)
        value = keep + swap(send, "dp", stride)
    return value[0]


def transpose_down(value):
    seq, dp = lax.axis_size("seq"), lax.axis_size("dp")
    pairs = []
    for z in range(seq):
        for x in range(2):
            for s in range(seq):
                pairs.append((s * dp + 2 * z + x, z * dp + 2 * s + x))
    return lax.ppermute(value, ("seq", "dp"), pairs)


def on_device(
    tokens, lengths, w_qkv, b_qkv, output_weight, w_up, b_up, w_down, gains, shifts, cotangent
):
    sequences, segment, width = tokens.shape
    layers, hidden = b_up.shape
    seq = lax.axis_size("seq")
    count = sequences * segment
    groups = width // WIDE
    pairs = width // PAIR
    position = lax.axis_index("seq") * segment + jnp.arange(segment, dtype=jnp.int32)
    length_col = lengths[:, None]
    inside = (position[None, :] < length_col).astype(F32)
    phases = (
        math.pi
        / 2
        * jnp.minimum(position[None, :], length_col - 1).astype(F32)
        / length_col.astype(F32)
    )
    trig = jnp.stack([jnp.cos(phases), jnp.sin(phases), inside]).reshape(3, count, 1)
    trig = jnp.broadcast_to(trig, (3, count, PAIR))
    b_qkv = b_qkv[:, None, :]
    b_up = b_up[:, None, :]

    rows = (count, width)
    wide = spec((count, WIDE), lambda g, *_: (0, g))
    state_spec = spec((sequences, WIDE // PAIR, STATE, PAIR), lambda g, *_: (0, g, 0, 0))
    state_shape = shaped((sequences, pairs, STATE, PAIR))
    trig_spec = whole((3, count, PAIR))
    full = whole(rows)
    vec_spec = whole((8, width))
    acc = pltpu.VMEM(rows, F32)
    attention_flops = 2 * count * count * 256 * 12

    def qkv_spec(layer, part):
        return spec((None, width, WIDE), lambda g, *_: (layer, 0, part * groups + g))

    def bias_spec(layer, part):
        return spec((None, 1, WIDE), lambda g, *_: (layer, 0, part * groups + g))

    def rows_of(*vectors):
        stacked = jnp.stack(vectors)
        return jnp.concatenate([stacked, jnp.zeros((8 - len(vectors), width), F32)])

    stream, stream_low = tokens.reshape(rows), tokens.reshape(rows)
    saved = []
    block = min(768, hidden)
    order = Order()
    call = order.call
    place = places()
    waiting = []
    for layer in range(layers):
        shift, gain = shifts[layer], gains[layer]
        vec_one = rows_of(shift[:width], gain[:width], shift[width : 2 * width])
        vec_two = rows_of(shift[2 * width : 3 * width], gain[width:], shift[3 * width :])
        key, value, total = call(
            functools.partial(key_value_kernel, sequences),
            (groups,),
            [full, qkv_spec(layer, 1), qkv_spec(layer, 2), bias_spec(layer, 1), bias_spec(layer, 2), trig_spec],
            [wide, wide, state_spec],
            [shaped(rows), shaped(rows), state_shape],
            4 * count * width * width,
            name="key_value",
            after=waiting,
        )(stream_low, w_qkv, w_qkv, b_qkv, b_qkv, trig)
        before = scan_states(total, order)
        stream_other = swap(stream.astype(F32), "seq", 1)
        crossing = saved[-1][0][1:] if saved else []
        query, numer, denom, *crossing = call(
            functools.partial(query_kernel, sequences),
            (groups,),
            [full, qkv_spec(layer, 0), bias_spec(layer, 0), wide, wide, trig_spec],
            [wide, wide, wide],
            [shaped(rows), shaped(rows), shaped(rows)],
            2 * count * width * width + 5 * attention_flops,
            name="query",
            carry=crossing,
        )(stream_low, w_qkv, b_qkv, key, value, trig)
        if saved:
            saved[-1][0][1:] = crossing
            saved[-1][-1].extend(swap(part, "seq", 1) for part in crossing)
        attended, den, one, normed = call(
            functools.partial(attend_kernel, sequences, len(before)),
            (groups,),
            [wide, wide, wide, trig_spec,
             spec((None, WIDE, width), lambda g, at, layer=layer: (layer, g, 0)), full, vec_spec]
            + [state_spec] * len(before),
            [wide, wide, full, full],
            [shaped(rows)] * 4,
            4 * count * width * width,
            scratch=[acc],
            prefetch=1,
            name="attend",
        )(place, query, numer, denom, trig, output_weight, stream, vec_one, *before)
        stream_in = stream
        attended_other = swap(attended, "seq", 1)
        normed_chips = gather_chips(normed)
        pre, two, stream, stream_low = call(
            feed_forward_kernel,
            (hidden // block,),
            [full, spec((None, width, block), lambda g, layer=layer: (layer, 0, g)),
             spec((None, 1, block), lambda g, layer=layer: (layer, 0, g)),
             spec((None, block, width), lambda g, layer=layer: (layer, g, 0)), vec_spec],
            [spec((count, block), lambda g: (0, g)), full, full, full],
            [shaped((count, hidden)), shaped(rows), shaped(rows), shaped(rows, BF16)],
            4 * count * width * hidden,
            scratch=[acc],
            name="feed_forward",
            after=[stream_other],
        )(normed, w_up, b_up, w_down, vec_two)
        normed_cores = [swap(normed, "seq", 1)]
        waiting = [attended_other, normed_cores[0]]
        saved.append(
            (normed_chips, stream_in, stream_other, query, key, value, before, attended, attended_other,
             den, one, pre, two, vec_one, vec_two, normed_cores)
        )
    mixed = stream_low.reshape(tokens.shape)

    upstream = cotangent.reshape(rows)
    chips, dp = seq // 2, lax.axis_size("dp")
    lanes = 4 * width // seq
    slot = hidden // seq
    size = width // dp
    uppers = [int(size * part) // 8 * 8 for part in BY_Y]
    packed = dp == 2 * seq
    down_shape = (seq // 2, 2, slot // (2 * seq), width) if packed else (slot, width)
    down_count = 2 if packed else 1
    up_shape = (dp // 2, size, slot)
    d_shape = (chips, count, lanes)
    x_and_z = [("dp", stride) for stride in strides(dp)]
    above = [("seq", stride) for stride in strides(seq)[1:]]
    work = [dict() for _ in range(layers)]

    def norm_step(layer):
        now = work[layer]
        normed_chips, *unused, two, vec_one, vec_two, normed_cores = saved[layer]
        now["d_two"], now["sums_two"] = call(
            second_norm_kernel,
            (1,),
            [full, full, vec_spec],
            [full, vec_spec],
            [shaped(rows), shaped((8, width))],
            count * width * 20,
            name="second_norm",
            after=waiting + saved[layer - 1][-1][1:] if layer == layers - 1 else (),
        )(upstream, two, vec_two)
        now["errors"] = gather_chips(now["d_two"])
        now["error_core"] = swap(now["d_two"], "seq", 1)

    def feed_step(layer):
        now = work[layer]
        (normed_chips, stream_in, stream_other, query, key, value, before, attended, attended_other,
         den, one, pre, two, vec_one, vec_two, unused) = saved[layer]
        now["d_one"], now["sums_one"], now["bias_up"] = call(
            feed_back_kernel,
            (hidden // block,),
            [full, spec((None, block, width), lambda g: (layer, g, 0)),
             spec((None, width, block), lambda g: (layer, 0, g)),
             spec((count, block), lambda g: (0, g)), full, vec_spec],
            [full, vec_spec, spec((1, block), lambda g: (0, g))],
            [shaped(rows), shaped((8, width)), shaped((1, hidden))],
            4 * count * width * hidden,
            scratch=[acc],
            name="feed_back",
        )(now["d_two"], w_down, w_up, pre, one, vec_one)

    def state_step(layer):
        now = work[layer]
        (normed_chips, stream_in, stream_other, query, key, value, before, attended, attended_other,
         den, one, pre, two, vec_one, vec_two, unused) = saved[layer]
        now["d_num"], now["d_den"], now["d_state"] = call(
            functools.partial(state_back_kernel, sequences),
            (groups,),
            [full, spec((None, WIDE, width), lambda g: (layer, g, 0)),
             wide, trig_spec, wide, wide],
            [wide, wide, state_spec],
            [shaped(rows), shaped(rows), state_shape],
            4 * count * width * width,
            name="state_back",
        )(now["d_one"], output_weight, query, trig, attended, den)

    def scan_step(layer):
        work[layer]["after"] = scan_states(work[layer]["d_state"], order)

    def inner_step(layer):
        now = work[layer]
        (normed_chips, stream_in, stream_other, query, key, value, before, attended, attended_other,
         den, one, pre, two, vec_one, vec_two, unused) = saved[layer]
        now["inner"] = call(
            functools.partial(inner_back_kernel, sequences),
            (groups,),
            [wide, wide, wide, trig_spec, wide, wide] + [state_spec] * len(before),
            [wide, wide, wide],
            [shaped(rows)] * 3,
            15 * attention_flops,
            prefetch=1,
            name="inner_back",
            after=saved[layer][0][1:] if layer == layers - 1 else (),
        )(place, query, key, value, trig, now["d_num"], now["d_den"], *before)

    def gate(held):
        unused, *held = call(
            gate_kernel, (1,), [], [whole((8, PAIR))], [shaped((8, PAIR))], 0, name="gate", carry=held
        )()
        return unused, held

    def gate_step(layer):
        now = work[layer]
        normed_chips, *unused, normed_cores = saved[layer]
        held = now["errors"][1:]
        if layer == layers - 1:
            held = normed_chips[1:] + held
        unused, held = gate(held)
        if layer == layers - 1:
            normed_chips[1:] = held[: chips - 1]
            normed_cores.extend(swap(part, "seq", 1) for part in normed_chips[1:])
        now["errors"][1:] = held[1 - chips :]
        now["error_cores"] = [swap(part, "seq", 1) for part in now["errors"][1:]]

    def feed_weights_step(layer):
        now = work[layer]
        first = UP_FIRST[layer] if packed else 1
        mine = saved[layer][0] + now["errors"]
        theirs = saved[layer][-1] + [now["error_core"]] + now["error_cores"]
        shapes = [(dp // 2, 2, size, width)] * 2 if first == 0 else [up_shape] * 2 + [down_shape] * down_count
        up_keep, up_send, *downs = call(
            functools.partial(feed_weights_kernel, chips, packed, first),
            (1,),
            [full] * (4 * chips)
            + [spec((None, width, slot), lambda g, at: (layer, 0, at[0])),
               spec((None, 1, slot), lambda g, at: (layer, 0, at[0])),
               spec((None, slot, width), lambda g, at: (layer, at[0], 0))],
            [whole(shape) for shape in shapes],
            [shaped(shape) for shape in shapes],
            8 * count * width * hidden,
            prefetch=1,
            vmem=56,
            name="feed_weights",
        )(place, *mine, *theirs, w_up, b_up, w_down)
        if first == 0:
            now["up"] = Scatter(order, place, up_keep, up_send, [("dp", stride, 0) for stride in strides(dp)])
            return
        parts = (dp // (2 * first), first) + up_shape[1:]
        steps = [("dp", first, 0)] + [("dp", stride, 1) for stride in strides(first)]
        steps += [("dp", stride, 0) for stride in strides(dp) if stride > first]
        now["up"] = Scatter(order, place, up_keep.reshape(parts), up_send.reshape(parts), steps)
        if packed:
            steps = [("dp", 2, 0), ("dp", 1, 1)] + [("dp", 2 * stride, 0) for stride in strides(seq)[1:]]
            now["dn"] = Scatter(order, place, *downs, steps)
        else:
            now["dn"] = scatter_down_whole(*downs)

    def joined_step(layer):
        nonlocal upstream
        now = work[layer]
        (normed_chips, stream_in, stream_other, query, key, value, before, attended, attended_other,
         den, one, pre, two, vec_one, vec_two, unused) = saved[layer]
        sends = [(1,) + d_shape[1:]] * chips if layer == 0 else [d_shape]
        upstream, now["d_mine"], now["bias_qkv"], *d_sends = call(
            functools.partial(joined_back_kernel, sequences, len(now["after"])),
            (groups,),
            [wide, wide, wide, wide, wide, trig_spec,
             qkv_spec(layer, 0), qkv_spec(layer, 1), qkv_spec(layer, 2), full]
            + [state_spec] * len(now["after"]),
            [full, whole(d_shape), whole((1, 3 * width))] + [whole(shape) for shape in sends],
            [shaped(rows), shaped(d_shape), shaped((1, 3 * width))] + [shaped(shape) for shape in sends],
            6 * count * width * width,
            scratch=[acc, pltpu.VMEM((count, 3 * width), F32)],
            prefetch=1,
            name="joined_back",
        )(place, *now["inner"], key, value, trig, w_qkv, w_qkv, w_qkv, now["d_one"], *now["after"])
        now["d_other"] = [swap(part, "seq", 1) for part in d_sends]

    def attention_weights_step(layer):
        now = work[layer]
        (normed_chips, stream_in, stream_other, query, key, value, before, attended, attended_other,
         den, one, pre, two, vec_one, vec_two, unused) = saved[layer]
        upper = uppers[layer]
        y_shape = (chips // 2, dp, upper, lanes)
        x_shape = (chips, dp // 2, size - upper, lanes)
        shapes = ([y_shape] * 2 if upper else []) + ([x_shape] * 2 if upper < size else [])
        found = call(
            functools.partial(attention_weights_kernel, upper, len(now["d_other"])),
            (1,),
            [full] * 4 + [whole(d_shape)] + [whole(part.shape) for part in now["d_other"]],
            [whole(shape) for shape in shapes],
            [shaped(shape) for shape in shapes],
            8 * count * width * width,
            prefetch=1,
            name="attention_weights",
        )(place, stream_in, stream_other, attended, attended_other, now["d_mine"], *now["d_other"])
        if upper:
            now["by"] = Scatter(
                order, place, *found[:2],
                [(*step, 0) for step in above] + [(*step, 1) for step in x_and_z],
            )
        if upper < size:
            now["bx"] = Scatter(
                order, place, *found[-2:],
                [(*x_and_z[0], 1)] + [(*step, 0) for step in above] + [(*step, 1) for step in x_and_z[1:]],
            )

    def move(layer, name):
        now = work[layer]
        if name == "ud" and UP_FIRST[layer] == 0 and packed:
            name = "up"
        if name in ("ud", "bb"):
            first, second = (now.get(part) for part in {"ud": ("up", "dn"), "bb": ("by", "bx")}[name])
            both = isinstance(first, Scatter) and isinstance(second, Scatter)
            if both and not first.done() and first.fits(second):
                first.advance(second)
                del now["dn" if name == "ud" else "bx"]
            else:
                move(layer, "up" if name == "ud" else "by")
                move(layer, "dn" if name == "ud" else "bx")
            return
        scatter = now.get(name)
        if name == "sx":
            order.ready = now["after"][-1:]
        elif name == "dx":
            order.ready = [now["down"]] if "down" in now else []
        elif name == "ba":
            joint = now.get("by") or now["bx"]
            if joint.done() and joint.recv is not None and not ("by" in now and "bx" in now):
                joint.keep, joint.recv = add(order, *joint.last()), None
        elif name == "dt":
            if packed and "down" not in now:
                held = (now.get("dn") or now["up"]).last()
                now["down"] = transpose_down(add(order, *held, at=held[0].shape[0] - 1))
        elif isinstance(scatter, Scatter) and not scatter.done():
            scatter.advance()

    steps = {
        "sn": norm_step, "fb": feed_step, "sb": state_step, "sc": scan_step, "ib": inner_step,
        "ga": gate_step, "fw": feed_weights_step, "jb": joined_step, "aw": attention_weights_step,
    }
    hops = [("dp", stride) for stride in strides(dp)[1:]] + [("seq", stride) for stride in strides(seq)]
    hops.append(("dp", 1))
    summed = moving = None
    for word in PLAN:
        word, unused, wait = word.partition("+")
        name, layer = word[:2], int(word[2:]) - 1
        order.wait = float(wait or 0)
        if name == "ve":
            if summed is None:
                pieces = []
                for now in work:
                    pieces += [now["bias_qkv"], now["bias_up"], now["sums_one"], now["sums_two"]]
                shape = (layers * VECTOR, width)
                summed = call(
                    functools.partial(vector_kernel, layers), (1,), [whole(p.shape) for p in pieces],
                    [whole(shape)], [shaped(shape)], 1, name="vectors",
                )(*pieces)[0]
            elif moving is not None:
                summed, moving = add(order, summed, moving), None
            if hops:
                moving = swap(summed, *hops.pop(0))
        elif name in steps:
            steps[name](layer)
        else:
            move(layer, name)
    while hops or moving is not None:
        summed = add(order, summed, moving)
        moving = swap(summed, *hops.pop(0)) if hops else None
    for _ in range(2 * len(x_and_z) + len(above)):
        for layer in reversed(range(layers)):
            for name in ("up", "dn", "by", "bx"):
                move(layer, name)
    given, counts = [], []
    for layer in range(layers):
        move(layer, "dt")
        now = work[layer]
        counts.append([])
        for name in ("by", "bx", "up"):
            parts = now[name].last() if name in now else []
            given += parts
            counts[-1] += [len(parts)] if parts else []
        given.append(now["down"] if packed else now["dn"])
    part = 3 * lanes // 4
    out_shapes = [
        shaped((layers, size, part)),
        shaped((layers, size, lanes - part)),
        shaped((layers, size, slot)),
        shaped((layers, hidden // dp, width // seq)),
        shaped((layers, 3 * width)),
        shaped((layers, hidden)),
        shaped((layers, 2 * width)),
        shaped((layers, 4 * width)),
    ]
    given.append(summed)
    outs = call(
        functools.partial(finish_kernel, counts),
        (1,),
        [whole(g.shape) for g in given],
        [whole(o.shape) for o in out_shapes],
        out_shapes,
        1,
        name="finish",
    )(*given)
    return (mixed, upstream.reshape(tokens.shape), *outs)


def solution(mesh):
    in_specs = (
        P("dp", "seq", None),
        P("dp"),
        P(),
        P(),
        P(),
        P(),
        P(),
        P(),
        P(),
        P(),
        P("dp", "seq", None),
    )
    out_specs = (
        P("dp", "seq", None),
        P("dp", "seq", None),
        P(None, "dp", "seq"),
        P(None, "dp", "seq"),
        P(None, "dp", "seq"),
        P(None, "dp", "seq"),
        P(),
        P(),
        P(),
        P(),
    )
    return jax.shard_map(
        on_device, mesh=mesh, in_specs=in_specs, out_specs=out_specs, check_vma=False
    )
```

```python
import functools
import math

import jax
import jax.numpy as jnp
from jax import lax
from jax.experimental import pallas as pl
from jax.experimental.pallas import tpu as pltpu
from jax.sharding import PartitionSpec as P

HEAD = 64
PAIR = 128
WIDE = 256
STATE = 136
VECTOR = 16
EPS = 1e-05
COST = 0.28
TIMES = {
    "key_value": 3.5, "query": 6.0, "attend": 4.0, "feed_forward": 8.0, "second_norm": 1.0, "feed_back": 8.0,
    "state_back": 4.0, "inner_back": 7.0, "feed_weights": 13.0, "joined_back": 8.0, "attention_weights": 5.0,
}
UP_FIRST = (1, 1)
BY_Y = (1.0, 1.0)
PLAN = (
    "sn2", "fb2", "sb2", "ib2", "ga2+5", "sc2", "fw2", "jb2", "sn1", "fb1",
    "sb1", "up2", "dn2", "ib1", "sc1", "ga1+8", "ud2", "sx1", "aw2", "jb1",
    "ve1", "fw1", "ve1", "aw1+2", "dt2+4", "by2", "up1+8", "dn1+8", "dx2", "ve1+6",
    "bb2+5", "ud1+6", "by1+4", "bb2", "ve1+10", "dt1+12", "ba2", "dx1", "bb1+15", "bb1+15",
    "ve1",
)
F32 = jnp.float32
BF16 = jnp.bfloat16

NN = (((1,), (0,)), ((), ()))
NT = (((1,), (1,)), ((), ()))
TN = (((0,), (0,)), ((), ()))


def dot(a, b, dims=NN):
    return lax.dot_general(a, b, dims, preferred_element_type=F32)


def split(a):
    high = a.astype(BF16)
    return high, (a - high.astype(F32)).astype(BF16)


def dot3(a, b, dims=NN):
    return dot(a[0], b[0], dims) + (dot(a[0], b[1], dims) + dot(a[1], b[0], dims))


def dot2(a, b, dims=NN):
    return dot(a, b[0], dims) + dot(a, b[1], dims)


def cut(parts, rows):
    return tuple(part[rows] for part in parts)


def softplus(v):
    return jnp.maximum(v, 0.0) + jnp.log1p(jnp.exp(-jnp.abs(v)))


def sigmoid(v):
    return 1.0 / (1.0 + jnp.exp(-v))


def lanes_of_first(shape):
    lane = lax.broadcasted_iota(jnp.int32, shape, len(shape) - 1)
    return (lane & HEAD) == 0


def causal(tokens, sequences):
    row = lax.broadcasted_iota(jnp.int32, (tokens, tokens), 0)
    column = lax.broadcasted_iota(jnp.int32, (tokens, tokens), 1)
    keep = column <= row
    segment = tokens // sequences
    for later in range(1, sequences):
        keep = keep & ((row < later * segment) | (column >= later * segment))
    return keep


def two_maps(feature, cosine, sine):
    return jnp.concatenate([feature * cosine, feature * sine], axis=1)


def pack_state(full, sums):
    first = lanes_of_first((HEAD, PAIR))
    top = jnp.where(first, full[0:HEAD], full[HEAD : 2 * HEAD])
    low = jnp.where(first, full[2 * HEAD : 3 * HEAD], full[3 * HEAD :])
    rest = jnp.zeros((STATE - 2 * HEAD - 2, PAIR), F32)
    return jnp.concatenate([top, low, sums[:, :PAIR], sums[:, PAIR:], rest], axis=0)


def unpack_state(packed):
    first = lanes_of_first((HEAD, PAIR))
    top, low = packed[0:HEAD], packed[HEAD : 2 * HEAD]
    full = jnp.concatenate(
        [
            jnp.where(first, top, 0.0),
            jnp.where(first, 0.0, top),
            jnp.where(first, low, 0.0),
            jnp.where(first, 0.0, low),
        ],
        axis=0,
    )
    return full, packed[2 * HEAD : 2 * HEAD + 1], packed[2 * HEAD + 1 : 2 * HEAD + 2]


def head_sum(values):
    row = lax.broadcasted_iota(jnp.int32, (PAIR, PAIR), 0)
    column = lax.broadcasted_iota(jnp.int32, (PAIR, PAIR), 1)
    same = jnp.where((row & HEAD) == (column & HEAD), 1.0, 0.0).astype(BF16)
    high, low = split(values)
    return dot(high, same) + dot(low, same)


def norm_parts(residual):
    centre = residual - jnp.mean(residual, axis=-1, keepdims=True)
    rstd = lax.rsqrt(jnp.mean(centre * centre, axis=-1, keepdims=True) + EPS)
    return centre * rstd, rstd


def norm_back(residual, gain, upstream):
    xhat, rstd = norm_parts(residual)
    scaled = gain * upstream
    mean = jnp.mean(scaled, axis=-1, keepdims=True)
    along = jnp.mean(scaled * xhat, axis=-1, keepdims=True)
    grad = rstd * (scaled - mean - xhat * along)
    sums = jnp.concatenate(
        [
            jnp.sum(upstream * xhat, axis=0, keepdims=True),
            jnp.sum(upstream, axis=0, keepdims=True),
            jnp.sum(grad, axis=0, keepdims=True),
            jnp.zeros((5, residual.shape[1]), F32),
        ],
        axis=0,
    )
    return grad, sums


GELU_A = math.sqrt(2.0 / math.pi)
GELU_B = 0.044715


def gelu_terms(v):
    square = v * v
    bent = jnp.tanh(GELU_A * (v + GELU_B * (square * v)))
    return square, bent


def gelu(v):
    unused, bent = gelu_terms(v)
    return 0.5 * v * (1.0 + bent)


def gelu_both(v):
    square, bent = gelu_terms(v)
    slope = 0.5 * (1.0 + bent) + (0.5 * GELU_A) * v * (1.0 - bent * bent) * (
        1.0 + (3.0 * GELU_B) * square
    )
    return 0.5 * v * (1.0 + bent), slope


def spec(block, index):
    return pl.BlockSpec(block, index)


def whole(shape):
    return pl.BlockSpec(shape, lambda *at: (0,) * len(shape))


def shaped(shape, dtype=F32):
    return jax.ShapeDtypeStruct(shape, dtype)


class Order:
    def __init__(self):
        self.last = None
        self.ready = []
        self.wait = 0.0

    def call(self, body, grid, ins, outs, shapes, flops, scratch=(), vmem=40, prefetch=0, name=None, carry=(), after=()):
        after = list(after) + self.ready + ([] if self.last is None else [self.last])
        self.ready = []
        skipped = len(after) + len(carry)
        made = len(shapes)
        anywhere = pl.BlockSpec(memory_space=pl.ANY)

        def kernel(*refs):
            given, rest = refs[:prefetch], refs[prefetch + skipped :]
            body(*given, *rest[: len(ins) + made], *rest[len(ins) + made + len(carry) :])

        run = pl.pallas_call(
            kernel,
            grid_spec=pltpu.PrefetchScalarGridSpec(
                num_scalar_prefetch=prefetch,
                grid=grid,
                in_specs=[anywhere] * skipped + list(ins),
                out_specs=list(outs) + [anywhere] * len(carry),
                scratch_shapes=list(scratch),
            ),
            out_shape=list(shapes) + [shaped(c.shape, c.dtype) for c in carry],
            input_output_aliases={
                prefetch + skipped - len(carry) + at: made + at for at in range(len(carry))
            },
            compiler_params=pltpu.CompilerParams(
                dimension_semantics=("arbitrary",) * len(grid), vmem_limit_bytes=vmem << 20
            ),
            cost_estimate=pl.CostEstimate(
                flops=int((TIMES.get(name, 1.0) + 0.7 + self.wait) * COST * 1.15e9),
                bytes_accessed=0,
                transcendentals=0,
            ),
            name=name,
        )

        def apply(*given):
            found = run(*given[:prefetch], *after, *carry, *given[prefetch:])
            self.last = found[0]
            return found

        return apply


def key_value_kernel(
    sequences, x_ref, wk_ref, wv_ref, bk_ref, bv_ref, trig_ref, jk_ref, jv_ref, state_ref
):
    x = x_ref[...].astype(BF16)
    key = dot(x, wk_ref[...]) + bk_ref[...]
    value = dot(x, wv_ref[...]) + bv_ref[...]
    jk_ref[...] = key
    jv_ref[...] = value
    cosine, sine, inside = trig_ref[0], trig_ref[1], trig_ref[2]
    segment = x.shape[0] // sequences
    for pair in range(WIDE // PAIR):
        lanes = slice(pair * PAIR, (pair + 1) * PAIR)
        maps = two_maps(softplus(key[:, lanes]) * inside, cosine, sine)
        maps_s, value_s = split(maps), split(value[:, lanes])
        for number in range(sequences):
            rows = slice(number * segment, (number + 1) * segment)
            state_ref[number, pair] = pack_state(
                dot3(cut(maps_s, rows), cut(value_s, rows), TN),
                jnp.sum(maps[rows], axis=0, keepdims=True),
            )


def query_kernel(
    sequences, x_ref, wq_ref, bq_ref, jk_ref, jv_ref, trig_ref, jq_ref, numer_ref, denom_ref
):
    x = x_ref[...].astype(BF16)
    query = dot(x, wq_ref[...]) + bq_ref[...]
    jq_ref[...] = query
    cosine, sine, inside = trig_ref[0], trig_ref[1], trig_ref[2]
    tokens = x.shape[0]
    keep = causal(tokens, sequences)
    first_two = lanes_of_first((tokens, 2 * PAIR))
    first = lanes_of_first((tokens, PAIR))
    for pair in range(WIDE // PAIR):
        lanes = slice(pair * PAIR, (pair + 1) * PAIR)
        query_maps = two_maps(softplus(query[:, lanes]), cosine, sine)
        key_maps = two_maps(softplus(jk_ref[:, lanes]) * inside, cosine, sine).astype(BF16)
        value = jv_ref[:, lanes]
        both = []
        for head in range(2):
            masked = jnp.where(first_two, query_maps, 0.0) if head == 0 else jnp.where(first_two, 0.0, query_maps)
            scores = jnp.where(keep, dot(masked.astype(BF16), key_maps, NT), 0.0)
            ones = jnp.where(first, value, 1.0) if head == 0 else jnp.where(first, 1.0, value)
            both.append(dot2(scores.astype(BF16), split(ones)))
        numer_ref[:, lanes] = jnp.where(first, both[0], both[1])
        denom_ref[:, lanes] = pltpu.roll(jnp.where(first, both[1], both[0]), HEAD, 1)


def attend_kernel(
    sequences, steps, at_ref, jq_ref, numer_ref, denom_ref, trig_ref, w_ref, res_ref, vec_ref, *rest
):
    state_refs, (att_ref, den_ref, one_ref, normed_ref, acc_ref) = rest[:steps], rest[steps:]
    step = pl.program_id(0)
    cosine, sine = trig_ref[0], trig_ref[1]
    segment = jq_ref.shape[0] // sequences
    for pair in range(WIDE // PAIR):
        lanes = slice(pair * PAIR, (pair + 1) * PAIR)
        for number in range(sequences):
            rows = slice(number * segment, (number + 1) * segment)
            feature = softplus(jq_ref[rows, lanes])
            maps = jnp.concatenate([feature * cosine[rows], feature * sine[rows]], axis=1).astype(BF16)
            full, sum_cos, sum_sin = unpack_state(add_states(at_ref, state_refs, number, pair, False))
            numer = numer_ref[rows, lanes] + dot2(maps, split(full))
            query_cos, query_sin = maps[:, :PAIR].astype(F32), maps[:, PAIR:].astype(F32)
            denom = denom_ref[rows, lanes] + head_sum(query_cos * sum_cos + query_sin * sum_sin)
            den_ref[rows, lanes] = denom
            att_ref[rows, lanes] = numer / denom
    part = dot(att_ref[...].astype(BF16), w_ref[...])

    @pl.when(step == 0)
    def _():
        acc_ref[...] = part

    @pl.when(step > 0)
    def _():
        acc_ref[...] += part

    @pl.when(step == pl.num_programs(0) - 1)
    def _():
        residual = res_ref[...].astype(F32) + acc_ref[...] + vec_ref[0:1]
        one_ref[...] = residual
        xhat, unused = norm_parts(residual)
        normed_ref[...] = xhat * vec_ref[1:2] + vec_ref[2:3]


def feed_forward_kernel(
    normed_ref, up_ref, bias_ref, down_ref, vec_ref, pre_ref, two_ref, stream_ref, low_ref, acc_ref
):
    step = pl.program_id(0)
    pre = dot(normed_ref[...].astype(BF16), up_ref[...]) + bias_ref[...]
    pre_ref[...] = pre
    part = dot(gelu(pre).astype(BF16), down_ref[...])

    @pl.when(step == 0)
    def _():
        acc_ref[...] = part

    @pl.when(step > 0)
    def _():
        acc_ref[...] += part

    @pl.when(step == pl.num_programs(0) - 1)
    def _():
        residual = normed_ref[...] + acc_ref[...] + vec_ref[0:1]
        two_ref[...] = residual
        xhat, unused = norm_parts(residual)
        stream = xhat * vec_ref[1:2] + vec_ref[2:3]
        stream_ref[...] = stream
        low_ref[...] = stream.astype(BF16)


def second_norm_kernel(up_ref, two_ref, vec_ref, d_ref, sums_ref):
    grad, sums = norm_back(two_ref[...], vec_ref[1:2], up_ref[...].astype(F32))
    d_ref[...] = grad
    sums_ref[...] = sums


def feed_back_kernel(
    d_two_ref, down_ref, up_ref, pre_ref, one_ref, vec_ref,
    d_one_ref, sums_ref, bias_ref, acc_ref,
):
    step = pl.program_id(0)
    d_act = dot(d_two_ref[...].astype(BF16), down_ref[...], NT)
    unused, slope = gelu_both(pre_ref[...])
    d_pre = slope * d_act
    bias_ref[...] = jnp.sum(d_pre, axis=0, keepdims=True)
    part = dot(d_pre.astype(BF16), up_ref[...], NT)

    @pl.when(step == 0)
    def _():
        acc_ref[...] = part

    @pl.when(step > 0)
    def _():
        acc_ref[...] += part

    @pl.when(step == pl.num_programs(0) - 1)
    def _():
        grad, sums = norm_back(one_ref[...], vec_ref[1:2], d_two_ref[...] + acc_ref[...])
        d_one_ref[...] = grad
        sums_ref[...] = sums


def state_back_kernel(
    sequences, d_one_ref, w_ref, jq_ref, trig_ref, att_ref, den_ref, num_ref, dden_ref, state_ref
):
    d_att = dot(d_one_ref[...].astype(BF16), w_ref[...], NT)
    cosine, sine = trig_ref[0], trig_ref[1]
    segment = jq_ref.shape[0] // sequences
    for pair in range(WIDE // PAIR):
        lanes = slice(pair * PAIR, (pair + 1) * PAIR)
        feature = softplus(jq_ref[:, lanes])
        query_cos, query_sin = feature * cosine, feature * sine
        d_num = d_att[:, lanes] / den_ref[:, lanes]
        d_den = -head_sum(d_num * att_ref[:, lanes])
        num_ref[:, lanes] = d_num
        dden_ref[:, lanes] = d_den
        maps_s = split(jnp.concatenate([query_cos, query_sin], axis=1))
        num_s = split(d_num)
        sum_cos, sum_sin = query_cos * d_den, query_sin * d_den
        for number in range(sequences):
            rows = slice(number * segment, (number + 1) * segment)
            sums = jnp.concatenate(
                [
                    jnp.sum(sum_cos[rows], axis=0, keepdims=True),
                    jnp.sum(sum_sin[rows], axis=0, keepdims=True),
                ],
                axis=1,
            )
            state_ref[number, pair] = pack_state(
                dot3(cut(maps_s, rows), cut(num_s, rows), TN), sums
            )


def inner_back_kernel(
    sequences, at_ref, jq_ref, jk_ref, jv_ref, trig_ref, num_ref, dden_ref, *rest
):
    *state_refs, dq_ref, dk_ref, dv_ref = rest
    cosine, sine, inside = trig_ref[0], trig_ref[1], trig_ref[2]
    tokens = jq_ref.shape[0]
    segment = tokens // sequences
    keep = causal(tokens, sequences)
    first_two = lanes_of_first((tokens, 2 * PAIR))
    first = lanes_of_first((tokens, PAIR))
    for pair in range(WIDE // PAIR):
        lanes = slice(pair * PAIR, (pair + 1) * PAIR)
        query = jq_ref[:, lanes]
        query_maps = two_maps(softplus(query), cosine, sine)
        query_low = query_maps.astype(BF16)
        key_low = two_maps(softplus(jk_ref[:, lanes]) * inside, cosine, sine).astype(BF16)
        value = jv_ref[:, lanes]
        d_num, d_den = num_ref[:, lanes], dden_ref[:, lanes]
        num_s = split(d_num)
        moved = pltpu.roll(d_den, HEAD, 1) * (1.0 / HEAD)
        d_query, d_key, d_value = [], [], []
        for head in range(2):
            if head == 0:
                masked = jnp.where(first_two, query_maps, 0.0)
                ones = jnp.where(first, value, 1.0)
                joint = jnp.where(first, d_num, moved)
            else:
                masked = jnp.where(first_two, 0.0, query_maps)
                ones = jnp.where(first, 1.0, value)
                joint = jnp.where(first, moved, d_num)
            scores = jnp.where(keep, dot(masked.astype(BF16), key_low, NT), 0.0).astype(BF16)
            grads = jnp.where(keep, dot3(split(joint), split(ones), NT), 0.0).astype(BF16)
            d_query.append(dot(grads, key_low))
            d_key.append(dot(grads, query_low, TN))
            d_value.append(dot(scores, num_s[0], TN))
        d_query_maps = jnp.where(first_two, d_query[0], d_query[1])
        d_key_maps = jnp.where(first_two, d_key[0], d_key[1])
        from_state = []
        for number in range(sequences):
            rows = slice(number * segment, (number + 1) * segment)
            full, sum_cos, sum_sin = unpack_state(add_states(at_ref, state_refs, number, pair, False))
            more = dot3(cut(num_s, rows), split(full), NT)
            part = d_den[rows]
            from_state.append(
                more + jnp.concatenate([part * sum_cos, part * sum_sin], axis=1)
            )
        d_query_maps = d_query_maps + (
            from_state[0] if sequences == 1 else jnp.concatenate(from_state, axis=0)
        )
        dq_ref[:, lanes] = sigmoid(query) * (
            d_query_maps[:, :PAIR] * cosine + d_query_maps[:, PAIR:] * sine
        )
        dk_ref[:, lanes] = d_key_maps[:, :PAIR] * cosine + d_key_maps[:, PAIR:] * sine
        dv_ref[:, lanes] = jnp.where(first, d_value[0], d_value[1])


def joined_back_kernel(
    sequences, scan, at_ref, dq_ref, dk_ref, dv_ref, jk_ref, jv_ref, trig_ref,
    wq_ref, wk_ref, wv_ref, d_one_ref, *rest,
):
    state_refs, (up_ref, mine_ref, sum_ref, *other_refs, acc_ref, join_ref) = rest[:scan], rest[scan:]
    step = pl.program_id(0)
    steps = 3
    cosine, sine, inside = trig_ref[0], trig_ref[1], trig_ref[2]
    segment = jk_ref.shape[0] // sequences
    keys, values = [], []
    for pair in range(WIDE // PAIR):
        lanes = slice(pair * PAIR, (pair + 1) * PAIR)
        key = jk_ref[:, lanes]
        maps_s = split(two_maps(softplus(key) * inside, cosine, sine))
        value_s = split(jv_ref[:, lanes])
        d_key, d_value = [], []
        for number in range(sequences):
            rows = slice(number * segment, (number + 1) * segment)
            full, sum_cos, sum_sin = unpack_state(add_states(at_ref, state_refs, number, pair, True))
            full_s = split(full)
            back = dot3(cut(value_s, rows), full_s, NT)
            d_key.append(
                (back[:, :PAIR] + sum_cos) * cosine[rows] + (back[:, PAIR:] + sum_sin) * sine[rows]
            )
            d_value.append(dot3(cut(maps_s, rows), full_s))
        d_key = d_key[0] if sequences == 1 else jnp.concatenate(d_key, axis=0)
        d_value = d_value[0] if sequences == 1 else jnp.concatenate(d_value, axis=0)
        keys.append(inside * sigmoid(key) * (dk_ref[:, lanes] + d_key))
        values.append(dv_ref[:, lanes] + d_value)
    three = (dq_ref[...], jnp.concatenate(keys, axis=1), jnp.concatenate(values, axis=1))
    part = (
        dot(three[0].astype(BF16), wq_ref[...], NT)
        + dot(three[1].astype(BF16), wk_ref[...], NT)
        + dot(three[2].astype(BF16), wv_ref[...], NT)
    )
    for at in range(steps):

        @pl.when(step == at)
        def _(at=at):
            for group, block in enumerate(three):
                begin = (group * steps + at) * WIDE
                join_ref[:, begin : begin + WIDE] = block

    @pl.when(step == 0)
    def _():
        acc_ref[...] = d_one_ref[...] + part

    @pl.when(step > 0)
    def _():
        acc_ref[...] += part

    @pl.when(step == steps - 1)
    def _():
        up_ref[...] = acc_ref[...]
        sum_ref[...] = jnp.sum(join_ref[...], axis=0, keepdims=True)
        chips = mine_ref.shape[0]
        part, part_one = join_ref.shape[1] // (2 * chips), d_one_ref.shape[1] // (2 * chips)
        for core in range(2):

            @pl.when(at_ref[place_of("seq", 1)] == core)
            def _(core=core):
                for block in range(2 * chips):
                    others = other_refs[0] if len(other_refs) == 1 else other_refs[block // 2]
                    ref = mine_ref if block % 2 == core else others
                    ref[block // 2 % ref.shape[0]] = jnp.concatenate(
                        [
                            join_ref[:, block * part : (block + 1) * part],
                            d_one_ref[:, block * part_one : (block + 1) * part_one],
                        ],
                        axis=1,
                    )


def feed_weights_kernel(chips, packed, first, at_ref, *refs):
    mine, theirs, rest = refs[: 2 * chips], refs[2 * chips : 4 * chips], refs[4 * chips :]
    up_ref, bias_ref, down_ref, up_keep_ref, up_send_ref, *down_refs = rest
    pairs = list(zip(mine[:chips], mine[chips:])) + list(zip(theirs[:chips], theirs[chips:]))
    up, down, bias = up_ref[...], down_ref[...], bias_ref[...]
    normed, errors, ups, acts = [], [], [], []
    for n_ref, e_ref in pairs:
        n, e = n_ref[...].astype(BF16), e_ref[...].astype(BF16)
        act, slope = gelu_both(dot(n, up) + bias)
        normed.append(n)
        errors.append(e)
        ups.append((slope * dot(e, down, NT)).astype(BF16))
        acts.append(act.astype(BF16))
    normed, errors, ups, acts = (jnp.concatenate(parts, axis=0) for parts in (normed, errors, ups, acts))
    d_up = dot(normed, ups, TN)
    d_down = dot(acts, errors, TN)

    def down_piece(x, z, rows):
        groups = blocks // 2
        lanes = d_down.shape[1] // groups
        top, begin = x * groups * rows, z * lanes
        columns = d_down[:, begin : begin + lanes]
        return jnp.concatenate([columns[top + at * rows : top + (at + 1) * rows] for at in range(groups)], axis=1)

    if first == 0:
        halves, unused, rows, unused = up_keep_ref.shape
        blocks = 2 * halves
        for mine in range(2):

            @pl.when(at_ref[place_of("dp", 1)] == mine)
            def _(mine=mine):
                for block in range(blocks):
                    ref = up_keep_ref if block % 2 == mine else up_send_ref
                    ref[block // 2, 0] = d_up[block * rows : (block + 1) * rows]
                    ref[block // 2, 1] = down_piece(block % 2, block // 2, rows)

        return
    halves, rows, unused = up_keep_ref.shape
    blocks = 2 * halves
    for mine in range(2):

        @pl.when(at_ref[place_of("dp", first)] == mine)
        def _(mine=mine):
            for block in range(blocks):
                ref = up_keep_ref if block // first % 2 == mine else up_send_ref
                ref[block // (2 * first) * first + block % first] = d_up[block * rows : (block + 1) * rows]

    if not packed:
        down_refs[0][...] = d_down
        return
    keep_ref, send_ref = down_refs
    others, unused, rows, unused = keep_ref.shape
    for z in range(2):

        @pl.when(at_ref[place_of("dp", 2)] == z)
        def _(z=z):
            for low, ref in ((z, keep_ref), (1 - z, send_ref)):
                for x in range(2):
                    for high in range(others):
                        ref[high, x] = down_piece(x, 2 * high + low, rows)


def attention_weights_kernel(
    rows, many, at_ref, x_ref, x_other_ref, a_ref, a_other_ref, d_ref, *outs
):
    others, outs = outs[:many], outs[many:]
    chips = d_ref.shape[0]
    part = 3 * d_ref.shape[2] // 4
    both = (x_ref, x_other_ref), (a_ref, a_other_ref)
    inputs = [jnp.concatenate([r[...].astype(BF16) for r in refs], axis=0) for refs in both]
    grads = []
    for chip in range(chips):
        other = others[0][chip] if many == 1 else others[chip][0]
        errors = jnp.concatenate([d_ref[chip].astype(BF16), other.astype(BF16)], axis=0)
        grads.append(
            jnp.concatenate(
                [dot(inputs[0], errors[:, :part], TN), dot(inputs[1], errors[:, part:], TN)], axis=1
            )
        )
    by_y, by_x = outs[:2] if rows else (), outs[-2:] if len(outs) == 4 or not rows else ()
    high, blocks = by_y[0].shape[:2] if by_y else (chips // 2, 2 * by_x[0].shape[1])
    more = by_x[0].shape[2] if by_x else 0
    size = rows + more
    for y in range(2 if by_y else 0):

        @pl.when(at_ref[place_of("seq", 2)] == y)
        def _(y=y):
            for low, ref in ((y, by_y[0]), (1 - y, by_y[1])):
                for upper in range(high):
                    for block in range(blocks):
                        ref[upper, block] = grads[2 * upper + low][block * size : block * size + rows]

    for x in range(2 if by_x else 0):

        @pl.when(at_ref[place_of("dp", 1)] == x)
        def _(x=x):
            for parity, ref in ((x, by_x[0]), (1 - x, by_x[1])):
                for chip in range(chips):
                    for block in range(blocks // 2):
                        begin = (2 * block + parity) * size + rows
                        ref[chip, block] = grads[chip][begin : begin + more]


def gate_kernel(out_ref):
    out_ref[...] = jnp.zeros_like(out_ref)


def swap(value, axis, stride):
    return lax.ppermute(value, axis, [(i, i ^ stride) for i in range(lax.axis_size(axis))])


def strides(count):
    found, stride = [], 1
    while stride < count:
        found.append(stride)
        stride *= 2
    return found


def bit(axis, stride):
    return (lax.axis_index(axis) // stride) % 2


def places():
    found = [lax.axis_index("seq")]
    for axis in ("seq", "dp"):
        found += [bit(axis, stride) for stride in strides(lax.axis_size(axis))]
    return jnp.stack(found).astype(jnp.int32)


def place_of(axis, stride):
    spot = 1 + strides(lax.axis_size(axis)).index(stride)
    return spot if axis == "seq" else spot + len(strides(lax.axis_size("seq")))


def scan_states(total, order=None):
    steps = strides(lax.axis_size("seq"))
    others = []
    for stride in steps:
        others.append(swap(total, "seq", stride))
        if stride < steps[-1]:
            total = total + others[-1] if order is None else add(order, total, others[-1])
    return others


def add_states(at_ref, refs, number, pair, backward):
    total = None
    for step, ref in enumerate(refs):
        part = ref[number, pair]
        part = jnp.where((at_ref[1 + step] == 0) == backward, part, jnp.zeros_like(part))
        total = part if total is None else total + part
    return total


def gather_chips(value):
    held = [value]
    for stride in reversed(strides(lax.axis_size("seq"))[1:]):
        held = held + [swap(part, "seq", stride) for part in held]
    return held


def gather_cores(held):
    return held + [swap(part, "seq", 1) for part in held]


def halve_kernel(at_ref, *refs):
    kept_ref, sent_ref = refs[-2:]
    for at in range(kept_ref.shape[1]):
        keep_mine, recv_mine, keep_other, recv_other = refs[4 * at : 4 * at + 4]
        kept_ref[:, at] = keep_mine[...] + recv_mine[...]
        sent_ref[:, at] = keep_other[...] + recv_other[...]


def add_kernel(one_ref, two_ref, out_ref):
    out_ref[...] = one_ref[...] + two_ref[...]


class Scatter:
    def __init__(self, order, place, keep, send, steps):
        self.order, self.place, self.keep, self.steps = order, place, keep, list(steps)
        self.recv = self.swap(send)

    def swap(self, send):
        axis, stride, self.at = self.steps.pop(0)
        return swap(send, axis, stride)

    def done(self):
        return not self.steps

    def fits(self, other):
        return self.keep.shape == other.keep.shape and self.steps == other.steps

    def advance(self, *others):
        axis, stride, at = self.steps[0]
        shape = self.keep.shape
        rows, lanes = shape[-2:]
        outer = math.prod(shape[:at]) * shape[at] // 2
        inner = math.prod(shape[at + 1 : -2])
        flat = (outer, 2, inner, rows, lanes)
        parts = (self,) + others
        pieces = 2 if rows % 16 == 0 and outer < 4 else 1
        block = (None, None, inner, rows // pieces, lanes)
        spot = place_of(axis, stride)
        mine = spec(block, lambda a, r, at: (a, at[spot], 0, r, 0))
        other = spec(block, lambda a, r, at: (a, 1 - at[spot], 0, r, 0))
        out = spec((None, inner, len(parts), rows // pieces, lanes), lambda a, r, at: (a, 0, 0, r, 0))
        given = []
        for part in parts:
            given += [part.keep.reshape(flat), part.recv.reshape(flat)] * 2
        kept, sent = self.order.call(
            halve_kernel,
            (outer, pieces),
            [mine, mine, other, other] * len(parts),
            [out, out],
            [shaped((outer, inner, len(parts), rows, lanes))] * 2,
            1,
            prefetch=1,
            name="halve",
        )(self.place, *given)
        left = shape[:at] + (shape[at] // 2,) + shape[at + 1 : -2] + (len(parts), rows, lanes)
        if len(parts) == 1:
            left = left[:-3] + left[-2:]
        self.keep = kept.reshape(left)
        self.recv = self.swap(sent.reshape(left))
        for part in others:
            part.steps = []

    def last(self):
        rows, lanes = self.keep.shape[-2:]
        shape = (-1, rows, lanes)
        return [part.reshape(shape) for part in (self.keep, self.recv) if part is not None]


def add(order, one, two, at=None):
    if at is None:
        given = out = whole(one.shape)
        shape = one.shape
    else:
        shape = one.shape[1:]
        given = spec((None,) + shape, lambda g: (at,) + (0,) * len(shape))
        out = whole(shape)
    return order.call(add_kernel, (1,), [given] * 2, [out], [shaped(shape)], 1, name="add")(one, two)[0]


def vector_kernel(layers, *refs):
    out_ref = refs[-1]
    out_ref[...] = jnp.zeros_like(out_ref)
    width = out_ref.shape[1]
    for layer in range(layers):
        qkv_ref, up_ref, one_ref, two_ref = refs[4 * layer : 4 * layer + 4]
        rows = []
        for ref in (qkv_ref, up_ref):
            rows += [ref[0:1, at : at + width] for at in range(0, ref.shape[1], width)]
        rows += [one_ref[0:1], two_ref[0:1], one_ref[2:3], one_ref[1:2], two_ref[2:3], two_ref[1:2]]
        for at, row in enumerate(rows):
            out_ref[layer * VECTOR + at : layer * VECTOR + at + 1] = row


def finish_kernel(counts, *refs):
    vector_ref, qkv_ref, out_ref, up_ref, down_ref, *vector_refs = refs[-9:]
    width = vector_ref.shape[1]
    begin = 0
    for ref in vector_refs:
        many = ref.shape[1] // width
        for layer in range(len(counts)):
            for at in range(many):
                row = layer * VECTOR + begin + at
                ref[layer : layer + 1, at * width : (at + 1) * width] = vector_ref[row : row + 1]
        begin += many
    part = qkv_ref.shape[2]
    given = list(refs)
    for layer, many in enumerate(counts):
        sums = []
        for number in many:
            sums.append(given[:number])
            given = given[number:]
        down, given = given[0], given[1:]
        begin = 0
        for parts in sums[:-1]:
            for piece in range(parts[0].shape[0]):
                total = sum(part[piece] for part in parts[1:]) + parts[0][piece]
                rows = total.shape[0]
                qkv_ref[layer, begin : begin + rows] = total[:, :part]
                out_ref[layer, begin : begin + rows] = total[:, part:]
                begin += rows
        up_ref[layer] = sum(part[0] for part in sums[-1][1:]) + sums[-1][0][0]
        rows, lanes = down.shape
        across = down_ref.shape[2]
        for at in range(lanes // across):
            down_ref[layer, at * rows : (at + 1) * rows] = down[:, at * across : (at + 1) * across]


def scatter_down_whole(value):
    seq, dp = lax.axis_size("seq"), lax.axis_size("dp")
    value = lax.all_to_all(value, "seq", split_axis=1, concat_axis=0, tiled=True)
    value = value.reshape(dp, value.shape[0] // dp, value.shape[1])
    for stride in strides(dp):
        mine = bit("dp", stride)
        pairs = value.reshape((value.shape[0] // 2, 2) + value.shape[1:])
        keep = lax.dynamic_index_in_dim(pairs, mine, 1, keepdims=False)
        send = lax.dynamic_index_in_dim(pairs, 1 - mine, 1, keepdims=False)
        value = keep + swap(send, "dp", stride)
    return value[0]


def transpose_down(value):
    seq, dp = lax.axis_size("seq"), lax.axis_size("dp")
    pairs = []
    for z in range(seq):
        for x in range(2):
            for s in range(seq):
                pairs.append((s * dp + 2 * z + x, z * dp + 2 * s + x))
    return lax.ppermute(value, ("seq", "dp"), pairs)


def on_device(
    tokens, lengths, w_qkv, b_qkv, output_weight, w_up, b_up, w_down, gains, shifts, cotangent
):
    sequences, segment, width = tokens.shape
    layers, hidden = b_up.shape
    seq = lax.axis_size("seq")
    count = sequences * segment
    groups = width // WIDE
    pairs = width // PAIR
    position = lax.axis_index("seq") * segment + jnp.arange(segment, dtype=jnp.int32)
    length_col = lengths[:, None]
    inside = (position[None, :] < length_col).astype(F32)
    phases = (
        math.pi
        / 2
        * jnp.minimum(position[None, :], length_col - 1).astype(F32)
        / length_col.astype(F32)
    )
    trig = jnp.stack([jnp.cos(phases), jnp.sin(phases), inside]).reshape(3, count, 1)
    trig = jnp.broadcast_to(trig, (3, count, PAIR))
    b_qkv = b_qkv[:, None, :]
    b_up = b_up[:, None, :]

    rows = (count, width)
    wide = spec((count, WIDE), lambda g, *_: (0, g))
    state_spec = spec((sequences, WIDE // PAIR, STATE, PAIR), lambda g, *_: (0, g, 0, 0))
    state_shape = shaped((sequences, pairs, STATE, PAIR))
    trig_spec = whole((3, count, PAIR))
    full = whole(rows)
    vec_spec = whole((8, width))
    acc = pltpu.VMEM(rows, F32)
    attention_flops = 2 * count * count * 256 * 12

    def qkv_spec(layer, part):
        return spec((None, width, WIDE), lambda g, *_: (layer, 0, part * groups + g))

    def bias_spec(layer, part):
        return spec((None, 1, WIDE), lambda g, *_: (layer, 0, part * groups + g))

    def rows_of(*vectors):
        stacked = jnp.stack(vectors)
        return jnp.concatenate([stacked, jnp.zeros((8 - len(vectors), width), F32)])

    stream, stream_low = tokens.reshape(rows), tokens.reshape(rows)
    saved = []
    block = min(768, hidden)
    order = Order()
    call = order.call
    place = places()
    waiting = []
    for layer in range(layers):
        shift, gain = shifts[layer], gains[layer]
        vec_one = rows_of(shift[:width], gain[:width], shift[width : 2 * width])
        vec_two = rows_of(shift[2 * width : 3 * width], gain[width:], shift[3 * width :])
        key, value, total = call(
            functools.partial(key_value_kernel, sequences),
            (groups,),
            [full, qkv_spec(layer, 1), qkv_spec(layer, 2), bias_spec(layer, 1), bias_spec(layer, 2), trig_spec],
            [wide, wide, state_spec],
            [shaped(rows), shaped(rows), state_shape],
            4 * count * width * width,
            name="key_value",
            after=waiting,
        )(stream_low, w_qkv, w_qkv, b_qkv, b_qkv, trig)
        before = scan_states(total, order)
        stream_other = swap(stream.astype(F32), "seq", 1)
        crossing = saved[-1][0][1:] if saved else []
        query, numer, denom, *crossing = call(
            functools.partial(query_kernel, sequences),
            (groups,),
            [full, qkv_spec(layer, 0), bias_spec(layer, 0), wide, wide, trig_spec],
            [wide, wide, wide],
            [shaped(rows), shaped(rows), shaped(rows)],
            2 * count * width * width + 5 * attention_flops,
            name="query",
            carry=crossing,
        )(stream_low, w_qkv, b_qkv, key, value, trig)
        if saved:
            saved[-1][0][1:] = crossing
            saved[-1][-1].extend(swap(part, "seq", 1) for part in crossing)
        attended, den, one, normed = call(
            functools.partial(attend_kernel, sequences, len(before)),
            (groups,),
            [wide, wide, wide, trig_spec,
             spec((None, WIDE, width), lambda g, at, layer=layer: (layer, g, 0)), full, vec_spec]
            + [state_spec] * len(before),
            [wide, wide, full, full],
            [shaped(rows)] * 4,
            4 * count * width * width,
            scratch=[acc],
            prefetch=1,
            name="attend",
        )(place, query, numer, denom, trig, output_weight, stream, vec_one, *before)
        stream_in = stream
        attended_other = swap(attended, "seq", 1)
        normed_chips = gather_chips(normed)
        pre, two, stream, stream_low = call(
            feed_forward_kernel,
            (hidden // block,),
            [full, spec((None, width, block), lambda g, layer=layer: (layer, 0, g)),
             spec((None, 1, block), lambda g, layer=layer: (layer, 0, g)),
             spec((None, block, width), lambda g, layer=layer: (layer, g, 0)), vec_spec],
            [spec((count, block), lambda g: (0, g)), full, full, full],
            [shaped((count, hidden)), shaped(rows), shaped(rows), shaped(rows, BF16)],
            4 * count * width * hidden,
            scratch=[acc],
            name="feed_forward",
            after=[stream_other],
        )(normed, w_up, b_up, w_down, vec_two)
        normed_cores = [swap(normed, "seq", 1)]
        waiting = [attended_other, normed_cores[0]]
        saved.append(
            (normed_chips, stream_in, stream_other, query, key, value, before, attended, attended_other,
             den, one, pre, two, vec_one, vec_two, normed_cores)
        )
    mixed = stream_low.reshape(tokens.shape)

    upstream = cotangent.reshape(rows)
    chips, dp = seq // 2, lax.axis_size("dp")
    lanes = 4 * width // seq
    slot = hidden // seq
    size = width // dp
    uppers = [int(size * part) // 8 * 8 for part in BY_Y]
    packed = dp == 2 * seq
    down_shape = (seq // 2, 2, slot // (2 * seq), width) if packed else (slot, width)
    down_count = 2 if packed else 1
    up_shape = (dp // 2, size, slot)
    d_shape = (chips, count, lanes)
    x_and_z = [("dp", stride) for stride in strides(dp)]
    above = [("seq", stride) for stride in strides(seq)[1:]]
    work = [dict() for _ in range(layers)]

    def norm_step(layer):
        now = work[layer]
        normed_chips, *unused, two, vec_one, vec_two, normed_cores = saved[layer]
        now["d_two"], now["sums_two"] = call(
            second_norm_kernel,
            (1,),
            [full, full, vec_spec],
            [full, vec_spec],
            [shaped(rows), shaped((8, width))],
            count * width * 20,
            name="second_norm",
            after=waiting + saved[layer - 1][-1][1:] if layer == layers - 1 else (),
        )(upstream, two, vec_two)
        now["errors"] = gather_chips(now["d_two"])
        now["error_core"] = swap(now["d_two"], "seq", 1)

    def feed_step(layer):
        now = work[layer]
        (normed_chips, stream_in, stream_other, query, key, value, before, attended, attended_other,
         den, one, pre, two, vec_one, vec_two, unused) = saved[layer]
        now["d_one"], now["sums_one"], now["bias_up"] = call(
            feed_back_kernel,
            (hidden // block,),
            [full, spec((None, block, width), lambda g: (layer, g, 0)),
             spec((None, width, block), lambda g: (layer, 0, g)),
             spec((count, block), lambda g: (0, g)), full, vec_spec],
            [full, vec_spec, spec((1, block), lambda g: (0, g))],
            [shaped(rows), shaped((8, width)), shaped((1, hidden))],
            4 * count * width * hidden,
            scratch=[acc],
            name="feed_back",
        )(now["d_two"], w_down, w_up, pre, one, vec_one)

    def state_step(layer):
        now = work[layer]
        (normed_chips, stream_in, stream_other, query, key, value, before, attended, attended_other,
         den, one, pre, two, vec_one, vec_two, unused) = saved[layer]
        now["d_num"], now["d_den"], now["d_state"] = call(
            functools.partial(state_back_kernel, sequences),
            (groups,),
            [full, spec((None, WIDE, width), lambda g: (layer, g, 0)),
             wide, trig_spec, wide, wide],
            [wide, wide, state_spec],
            [shaped(rows), shaped(rows), state_shape],
            4 * count * width * width,
            name="state_back",
        )(now["d_one"], output_weight, query, trig, attended, den)

    def scan_step(layer):
        work[layer]["after"] = scan_states(work[layer]["d_state"], order)

    def inner_step(layer):
        now = work[layer]
        (normed_chips, stream_in, stream_other, query, key, value, before, attended, attended_other,
         den, one, pre, two, vec_one, vec_two, unused) = saved[layer]
        now["inner"] = call(
            functools.partial(inner_back_kernel, sequences),
            (groups,),
            [wide, wide, wide, trig_spec, wide, wide] + [state_spec] * len(before),
            [wide, wide, wide],
            [shaped(rows)] * 3,
            15 * attention_flops,
            prefetch=1,
            name="inner_back",
            after=saved[layer][0][1:] if layer == layers - 1 else (),
        )(place, query, key, value, trig, now["d_num"], now["d_den"], *before)

    def gate(held):
        unused, *held = call(
            gate_kernel, (1,), [], [whole((8, PAIR))], [shaped((8, PAIR))], 0, name="gate", carry=held
        )()
        return unused, held

    def gate_step(layer):
        now = work[layer]
        normed_chips, *unused, normed_cores = saved[layer]
        held = now["errors"][1:]
        if layer == layers - 1:
            held = normed_chips[1:] + held
        unused, held = gate(held)
        if layer == layers - 1:
            normed_chips[1:] = held[: chips - 1]
            normed_cores.extend(swap(part, "seq", 1) for part in normed_chips[1:])
        now["errors"][1:] = held[1 - chips :]
        now["error_cores"] = [swap(part, "seq", 1) for part in now["errors"][1:]]

    def feed_weights_step(layer):
        now = work[layer]
        first = UP_FIRST[layer] if packed else 1
        mine = saved[layer][0] + now["errors"]
        theirs = saved[layer][-1] + [now["error_core"]] + now["error_cores"]
        shapes = [(dp // 2, 2, size, width)] * 2 if first == 0 else [up_shape] * 2 + [down_shape] * down_count
        up_keep, up_send, *downs = call(
            functools.partial(feed_weights_kernel, chips, packed, first),
            (1,),
            [full] * (4 * chips)
            + [spec((None, width, slot), lambda g, at: (layer, 0, at[0])),
               spec((None, 1, slot), lambda g, at: (layer, 0, at[0])),
               spec((None, slot, width), lambda g, at: (layer, at[0], 0))],
            [whole(shape) for shape in shapes],
            [shaped(shape) for shape in shapes],
            8 * count * width * hidden,
            prefetch=1,
            vmem=56,
            name="feed_weights",
        )(place, *mine, *theirs, w_up, b_up, w_down)
        if first == 0:
            now["up"] = Scatter(order, place, up_keep, up_send, [("dp", stride, 0) for stride in strides(dp)])
            return
        parts = (dp // (2 * first), first) + up_shape[1:]
        steps = [("dp", first, 0)] + [("dp", stride, 1) for stride in strides(first)]
        steps += [("dp", stride, 0) for stride in strides(dp) if stride > first]
        now["up"] = Scatter(order, place, up_keep.reshape(parts), up_send.reshape(parts), steps)
        if packed:
            steps = [("dp", 2, 0), ("dp", 1, 1)] + [("dp", 2 * stride, 0) for stride in strides(seq)[1:]]
            now["dn"] = Scatter(order, place, *downs, steps)
        else:
            now["dn"] = scatter_down_whole(*downs)

    def joined_step(layer):
        nonlocal upstream
        now = work[layer]
        (normed_chips, stream_in, stream_other, query, key, value, before, attended, attended_other,
         den, one, pre, two, vec_one, vec_two, unused) = saved[layer]
        sends = [(1,) + d_shape[1:]] * chips if layer == 0 else [d_shape]
        upstream, now["d_mine"], now["bias_qkv"], *d_sends = call(
            functools.partial(joined_back_kernel, sequences, len(now["after"])),
            (groups,),
            [wide, wide, wide, wide, wide, trig_spec,
             qkv_spec(layer, 0), qkv_spec(layer, 1), qkv_spec(layer, 2), full]
            + [state_spec] * len(now["after"]),
            [full, whole(d_shape), whole((1, 3 * width))] + [whole(shape) for shape in sends],
            [shaped(rows), shaped(d_shape), shaped((1, 3 * width))] + [shaped(shape) for shape in sends],
            6 * count * width * width,
            scratch=[acc, pltpu.VMEM((count, 3 * width), F32)],
            prefetch=1,
            name="joined_back",
        )(place, *now["inner"], key, value, trig, w_qkv, w_qkv, w_qkv, now["d_one"], *now["after"])
        now["d_other"] = [swap(part, "seq", 1) for part in d_sends]

    def attention_weights_step(layer):
        now = work[layer]
        (normed_chips, stream_in, stream_other, query, key, value, before, attended, attended_other,
         den, one, pre, two, vec_one, vec_two, unused) = saved[layer]
        upper = uppers[layer]
        y_shape = (chips // 2, dp, upper, lanes)
        x_shape = (chips, dp // 2, size - upper, lanes)
        shapes = ([y_shape] * 2 if upper else []) + ([x_shape] * 2 if upper < size else [])
        found = call(
            functools.partial(attention_weights_kernel, upper, len(now["d_other"])),
            (1,),
            [full] * 4 + [whole(d_shape)] + [whole(part.shape) for part in now["d_other"]],
            [whole(shape) for shape in shapes],
            [shaped(shape) for shape in shapes],
            8 * count * width * width,
            prefetch=1,
            name="attention_weights",
        )(place, stream_in, stream_other, attended, attended_other, now["d_mine"], *now["d_other"])
        if upper:
            now["by"] = Scatter(
                order, place, *found[:2],
                [(*step, 0) for step in above] + [(*step, 1) for step in x_and_z],
            )
        if upper < size:
            now["bx"] = Scatter(
                order, place, *found[-2:],
                [(*x_and_z[0], 1)] + [(*step, 0) for step in above] + [(*step, 1) for step in x_and_z[1:]],
            )

    def move(layer, name):
        now = work[layer]
        if name == "ud" and UP_FIRST[layer] == 0 and packed:
            name = "up"
        if name in ("ud", "bb"):
            first, second = (now.get(part) for part in {"ud": ("up", "dn"), "bb": ("by", "bx")}[name])
            both = isinstance(first, Scatter) and isinstance(second, Scatter)
            if both and not first.done() and first.fits(second):
                first.advance(second)
                del now["dn" if name == "ud" else "bx"]
            else:
                move(layer, "up" if name == "ud" else "by")
                move(layer, "dn" if name == "ud" else "bx")
            return
        scatter = now.get(name)
        if name == "sx":
            order.ready = now["after"][-1:]
        elif name == "dx":
            order.ready = [now["down"]] if "down" in now else []
        elif name == "ba":
            joint = now.get("by") or now["bx"]
            if joint.done() and joint.recv is not None and not ("by" in now and "bx" in now):
                joint.keep, joint.recv = add(order, *joint.last()), None
        elif name == "dt":
            if packed and "down" not in now:
                held = (now.get("dn") or now["up"]).last()
                now["down"] = transpose_down(add(order, *held, at=held[0].shape[0] - 1))
        elif isinstance(scatter, Scatter) and not scatter.done():
            scatter.advance()

    steps = {
        "sn": norm_step, "fb": feed_step, "sb": state_step, "sc": scan_step, "ib": inner_step,
        "ga": gate_step, "fw": feed_weights_step, "jb": joined_step, "aw": attention_weights_step,
    }
    hops = [("dp", stride) for stride in strides(dp)[1:]] + [("seq", stride) for stride in strides(seq)]
    hops.append(("dp", 1))
    summed = moving = None
    for word in PLAN:
        word, unused, wait = word.partition("+")
        name, layer = word[:2], int(word[2:]) - 1
        order.wait = float(wait or 0)
        if name == "ve":
            if summed is None:
                pieces = []
                for now in work:
                    pieces += [now["bias_qkv"], now["bias_up"], now["sums_one"], now["sums_two"]]
                shape = (layers * VECTOR, width)
                summed = call(
                    functools.partial(vector_kernel, layers), (1,), [whole(p.shape) for p in pieces],
                    [whole(shape)], [shaped(shape)], 1, name="vectors",
                )(*pieces)[0]
            elif moving is not None:
                summed, moving = add(order, summed, moving), None
            if hops:
                moving = swap(summed, *hops.pop(0))
        elif name in steps:
            steps[name](layer)
        else:
            move(layer, name)
    while hops or moving is not None:
        summed = add(order, summed, moving)
        moving = swap(summed, *hops.pop(0)) if hops else None
    for _ in range(2 * len(x_and_z) + len(above)):
        for layer in reversed(range(layers)):
            for name in ("up", "dn", "by", "bx"):
                move(layer, name)
    given, counts = [], []
    for layer in range(layers):
        move(layer, "dt")
        now = work[layer]
        counts.append([])
        for name in ("by", "bx", "up"):
            parts = now[name].last() if name in now else []
            given += parts
            counts[-1] += [len(parts)] if parts else []
        given.append(now["down"] if packed else now["dn"])
    part = 3 * lanes // 4
    out_shapes = [
        shaped((layers, size, part)),
        shaped((layers, size, lanes - part)),
        shaped((layers, size, slot)),
        shaped((layers, hidden // dp, width // seq)),
        shaped((layers, 3 * width)),
        shaped((layers, hidden)),
        shaped((layers, 2 * width)),
        shaped((layers, 4 * width)),
    ]
    given.append(summed)
    outs = call(
        functools.partial(finish_kernel, counts),
        (1,),
        [whole(g.shape) for g in given],
        [whole(o.shape) for o in out_shapes],
        out_shapes,
        1,
        name="finish",
    )(*given)
    return (mixed, upstream.reshape(tokens.shape), *outs)


def solution(mesh):
    in_specs = (
        P("dp", "seq", None),
        P("dp"),
        P(),
        P(),
        P(),
        P(),
        P(),
        P(),
        P(),
        P(),
        P("dp", "seq", None),
    )
    out_specs = (
        P("dp", "seq", None),
        P("dp", "seq", None),
        P(None, "dp", "seq"),
        P(None, "dp", "seq"),
        P(None, "dp", "seq"),
        P(None, "dp", "seq"),
        P(),
        P(),
        P(),
        P(),
    )
    return jax.shard_map(
        on_device, mesh=mesh, in_specs=in_specs, out_specs=out_specs, check_vma=False
    )
```

```python
import functools
import math

import jax
import jax.numpy as jnp
from jax import lax
from jax.experimental import pallas as pl
from jax.experimental.pallas import tpu as pltpu
from jax.sharding import PartitionSpec as P

HEAD = 64
PAIR = 128
WIDE = 256
STATE = 136
VECTOR = 16
EPS = 1e-05
COST = 0.28
TIMES = {
    "key_value": 3.5, "query": 6.0, "attend": 4.0, "feed_forward": 8.0, "second_norm": 1.0, "feed_back": 8.0,
    "state_back": 4.0, "inner_back": 7.0, "feed_weights": 13.0, "joined_back": 8.0, "attention_weights": 5.0,
}
UP_FIRST = (1, 1)
BY_Y = (1.0, 1.0)
PLAN = (
    "sn2", "fb2", "sb2", "ib2", "ga2+5", "sc2", "fw2", "jb2", "sn1", "fb1",
    "sb1", "up2", "dn2", "ib1", "sc1", "ga1+8", "ud2", "sx1", "aw2", "jb1",
    "ve1", "fw1", "ve1", "aw1+2", "dt2+4", "by2", "up1+8", "dn1+8", "dx2", "ve1+6",
    "bb2+5", "ud1+6", "by1+4", "ve1+12", "dt1", "bb2+12", "ba2", "dx1", "bb1+15", "bb1+15",
    "ve1",
)
F32 = jnp.float32
BF16 = jnp.bfloat16

NN = (((1,), (0,)), ((), ()))
NT = (((1,), (1,)), ((), ()))
TN = (((0,), (0,)), ((), ()))


def dot(a, b, dims=NN):
    return lax.dot_general(a, b, dims, preferred_element_type=F32)


def split(a):
    high = a.astype(BF16)
    return high, (a - high.astype(F32)).astype(BF16)


def dot3(a, b, dims=NN):
    return dot(a[0], b[0], dims) + (dot(a[0], b[1], dims) + dot(a[1], b[0], dims))


def dot2(a, b, dims=NN):
    return dot(a, b[0], dims) + dot(a, b[1], dims)


def cut(parts, rows):
    return tuple(part[rows] for part in parts)


def softplus(v):
    return jnp.maximum(v, 0.0) + jnp.log1p(jnp.exp(-jnp.abs(v)))


def sigmoid(v):
    return 1.0 / (1.0 + jnp.exp(-v))


def lanes_of_first(shape):
    lane = lax.broadcasted_iota(jnp.int32, shape, len(shape) - 1)
    return (lane & HEAD) == 0


def causal(tokens, sequences):
    row = lax.broadcasted_iota(jnp.int32, (tokens, tokens), 0)
    column = lax.broadcasted_iota(jnp.int32, (tokens, tokens), 1)
    keep = column <= row
    segment = tokens // sequences
    for later in range(1, sequences):
        keep = keep & ((row < later * segment) | (column >= later * segment))
    return keep


def two_maps(feature, cosine, sine):
    return jnp.concatenate([feature * cosine, feature * sine], axis=1)


def pack_state(full, sums):
    first = lanes_of_first((HEAD, PAIR))
    top = jnp.where(first, full[0:HEAD], full[HEAD : 2 * HEAD])
    low = jnp.where(first, full[2 * HEAD : 3 * HEAD], full[3 * HEAD :])
    rest = jnp.zeros((STATE - 2 * HEAD - 2, PAIR), F32)
    return jnp.concatenate([top, low, sums[:, :PAIR], sums[:, PAIR:], rest], axis=0)


def unpack_state(packed):
    first = lanes_of_first((HEAD, PAIR))
    top, low = packed[0:HEAD], packed[HEAD : 2 * HEAD]
    full = jnp.concatenate(
        [
            jnp.where(first, top, 0.0),
            jnp.where(first, 0.0, top),
            jnp.where(first, low, 0.0),
            jnp.where(first, 0.0, low),
        ],
        axis=0,
    )
    return full, packed[2 * HEAD : 2 * HEAD + 1], packed[2 * HEAD + 1 : 2 * HEAD + 2]


def head_sum(values):
    row = lax.broadcasted_iota(jnp.int32, (PAIR, PAIR), 0)
    column = lax.broadcasted_iota(jnp.int32, (PAIR, PAIR), 1)
    same = jnp.where((row & HEAD) == (column & HEAD), 1.0, 0.0).astype(BF16)
    high, low = split(values)
    return dot(high, same) + dot(low, same)


def norm_parts(residual):
    centre = residual - jnp.mean(residual, axis=-1, keepdims=True)
    rstd = lax.rsqrt(jnp.mean(centre * centre, axis=-1, keepdims=True) + EPS)
    return centre * rstd, rstd


def norm_back(residual, gain, upstream):
    xhat, rstd = norm_parts(residual)
    scaled = gain * upstream
    mean = jnp.mean(scaled, axis=-1, keepdims=True)
    along = jnp.mean(scaled * xhat, axis=-1, keepdims=True)
    grad = rstd * (scaled - mean - xhat * along)
    sums = jnp.concatenate(
        [
            jnp.sum(upstream * xhat, axis=0, keepdims=True),
            jnp.sum(upstream, axis=0, keepdims=True),
            jnp.sum(grad, axis=0, keepdims=True),
            jnp.zeros((5, residual.shape[1]), F32),
        ],
        axis=0,
    )
    return grad, sums


GELU_A = math.sqrt(2.0 / math.pi)
GELU_B = 0.044715


def gelu_terms(v):
    square = v * v
    bent = jnp.tanh(GELU_A * (v + GELU_B * (square * v)))
    return square, bent


def gelu(v):
    unused, bent = gelu_terms(v)
    return 0.5 * v * (1.0 + bent)


def gelu_both(v):
    square, bent = gelu_terms(v)
    slope = 0.5 * (1.0 + bent) + (0.5 * GELU_A) * v * (1.0 - bent * bent) * (
        1.0 + (3.0 * GELU_B) * square
    )
    return 0.5 * v * (1.0 + bent), slope


def spec(block, index):
    return pl.BlockSpec(block, index)


def whole(shape):
    return pl.BlockSpec(shape, lambda *at: (0,) * len(shape))


def shaped(shape, dtype=F32):
    return jax.ShapeDtypeStruct(shape, dtype)


class Order:
    def __init__(self):
        self.last = None
        self.ready = []
        self.wait = 0.0

    def call(self, body, grid, ins, outs, shapes, flops, scratch=(), vmem=40, prefetch=0, name=None, carry=(), after=()):
        after = list(after) + self.ready + ([] if self.last is None else [self.last])
        self.ready = []
        skipped = len(after) + len(carry)
        made = len(shapes)
        anywhere = pl.BlockSpec(memory_space=pl.ANY)

        def kernel(*refs):
            given, rest = refs[:prefetch], refs[prefetch + skipped :]
            body(*given, *rest[: len(ins) + made], *rest[len(ins) + made + len(carry) :])

        run = pl.pallas_call(
            kernel,
            grid_spec=pltpu.PrefetchScalarGridSpec(
                num_scalar_prefetch=prefetch,
                grid=grid,
                in_specs=[anywhere] * skipped + list(ins),
                out_specs=list(outs) + [anywhere] * len(carry),
                scratch_shapes=list(scratch),
            ),
            out_shape=list(shapes) + [shaped(c.shape, c.dtype) for c in carry],
            input_output_aliases={
                prefetch + skipped - len(carry) + at: made + at for at in range(len(carry))
            },
            compiler_params=pltpu.CompilerParams(
                dimension_semantics=("arbitrary",) * len(grid), vmem_limit_bytes=vmem << 20
            ),
            cost_estimate=pl.CostEstimate(
                flops=int((TIMES.get(name, 1.0) + 0.7 + self.wait) * COST * 1.15e9),
                bytes_accessed=0,
                transcendentals=0,
            ),
            name=name,
        )

        def apply(*given):
            found = run(*given[:prefetch], *after, *carry, *given[prefetch:])
            self.last = found[0]
            return found

        return apply


def key_value_kernel(
    sequences, x_ref, wk_ref, wv_ref, bk_ref, bv_ref, trig_ref, jk_ref, jv_ref, state_ref
):
    x = x_ref[...].astype(BF16)
    key = dot(x, wk_ref[...]) + bk_ref[...]
    value = dot(x, wv_ref[...]) + bv_ref[...]
    jk_ref[...] = key
    jv_ref[...] = value
    cosine, sine, inside = trig_ref[0], trig_ref[1], trig_ref[2]
    segment = x.shape[0] // sequences
    for pair in range(WIDE // PAIR):
        lanes = slice(pair * PAIR, (pair + 1) * PAIR)
        maps = two_maps(softplus(key[:, lanes]) * inside, cosine, sine)
        maps_s, value_s = split(maps), split(value[:, lanes])
        for number in range(sequences):
            rows = slice(number * segment, (number + 1) * segment)
            state_ref[number, pair] = pack_state(
                dot3(cut(maps_s, rows), cut(value_s, rows), TN),
                jnp.sum(maps[rows], axis=0, keepdims=True),
            )


def query_kernel(
    sequences, x_ref, wq_ref, bq_ref, jk_ref, jv_ref, trig_ref, jq_ref, numer_ref, denom_ref
):
    x = x_ref[...].astype(BF16)
    query = dot(x, wq_ref[...]) + bq_ref[...]
    jq_ref[...] = query
    cosine, sine, inside = trig_ref[0], trig_ref[1], trig_ref[2]
    tokens = x.shape[0]
    keep = causal(tokens, sequences)
    first_two = lanes_of_first((tokens, 2 * PAIR))
    first = lanes_of_first((tokens, PAIR))
    for pair in range(WIDE // PAIR):
        lanes = slice(pair * PAIR, (pair + 1) * PAIR)
        query_maps = two_maps(softplus(query[:, lanes]), cosine, sine)
        key_maps = two_maps(softplus(jk_ref[:, lanes]) * inside, cosine, sine).astype(BF16)
        value = jv_ref[:, lanes]
        both = []
        for head in range(2):
            masked = jnp.where(first_two, query_maps, 0.0) if head == 0 else jnp.where(first_two, 0.0, query_maps)
            scores = jnp.where(keep, dot(masked.astype(BF16), key_maps, NT), 0.0)
            ones = jnp.where(first, value, 1.0) if head == 0 else jnp.where(first, 1.0, value)
            both.append(dot2(scores.astype(BF16), split(ones)))
        numer_ref[:, lanes] = jnp.where(first, both[0], both[1])
        denom_ref[:, lanes] = pltpu.roll(jnp.where(first, both[1], both[0]), HEAD, 1)


def attend_kernel(
    sequences, steps, at_ref, jq_ref, numer_ref, denom_ref, trig_ref, w_ref, res_ref, vec_ref, *rest
):
    state_refs, (att_ref, den_ref, one_ref, normed_ref, acc_ref) = rest[:steps], rest[steps:]
    step = pl.program_id(0)
    cosine, sine = trig_ref[0], trig_ref[1]
    segment = jq_ref.shape[0] // sequences
    for pair in range(WIDE // PAIR):
        lanes = slice(pair * PAIR, (pair + 1) * PAIR)
        for number in range(sequences):
            rows = slice(number * segment, (number + 1) * segment)
            feature = softplus(jq_ref[rows, lanes])
            maps = jnp.concatenate([feature * cosine[rows], feature * sine[rows]], axis=1).astype(BF16)
            full, sum_cos, sum_sin = unpack_state(add_states(at_ref, state_refs, number, pair, False))
            numer = numer_ref[rows, lanes] + dot2(maps, split(full))
            query_cos, query_sin = maps[:, :PAIR].astype(F32), maps[:, PAIR:].astype(F32)
            denom = denom_ref[rows, lanes] + head_sum(query_cos * sum_cos + query_sin * sum_sin)
            den_ref[rows, lanes] = denom
            att_ref[rows, lanes] = numer / denom
    part = dot(att_ref[...].astype(BF16), w_ref[...])

    @pl.when(step == 0)
    def _():
        acc_ref[...] = part

    @pl.when(step > 0)
    def _():
        acc_ref[...] += part

    @pl.when(step == pl.num_programs(0) - 1)
    def _():
        residual = res_ref[...].astype(F32) + acc_ref[...] + vec_ref[0:1]
        one_ref[...] = residual
        xhat, unused = norm_parts(residual)
        normed_ref[...] = xhat * vec_ref[1:2] + vec_ref[2:3]


def feed_forward_kernel(
    normed_ref, up_ref, bias_ref, down_ref, vec_ref, pre_ref, two_ref, stream_ref, low_ref, acc_ref
):
    step = pl.program_id(0)
    pre = dot(normed_ref[...].astype(BF16), up_ref[...]) + bias_ref[...]
    pre_ref[...] = pre
    part = dot(gelu(pre).astype(BF16), down_ref[...])

    @pl.when(step == 0)
    def _():
        acc_ref[...] = part

    @pl.when(step > 0)
    def _():
        acc_ref[...] += part

    @pl.when(step == pl.num_programs(0) - 1)
    def _():
        residual = normed_ref[...] + acc_ref[...] + vec_ref[0:1]
        two_ref[...] = residual
        xhat, unused = norm_parts(residual)
        stream = xhat * vec_ref[1:2] + vec_ref[2:3]
        stream_ref[...] = stream
        low_ref[...] = stream.astype(BF16)


def second_norm_kernel(up_ref, two_ref, vec_ref, d_ref, sums_ref):
    grad, sums = norm_back(two_ref[...], vec_ref[1:2], up_ref[...].astype(F32))
    d_ref[...] = grad
    sums_ref[...] = sums


def feed_back_kernel(
    d_two_ref, down_ref, up_ref, pre_ref, one_ref, vec_ref,
    d_one_ref, sums_ref, bias_ref, acc_ref,
):
    step = pl.program_id(0)
    d_act = dot(d_two_ref[...].astype(BF16), down_ref[...], NT)
    unused, slope = gelu_both(pre_ref[...])
    d_pre = slope * d_act
    bias_ref[...] = jnp.sum(d_pre, axis=0, keepdims=True)
    part = dot(d_pre.astype(BF16), up_ref[...], NT)

    @pl.when(step == 0)
    def _():
        acc_ref[...] = part

    @pl.when(step > 0)
    def _():
        acc_ref[...] += part

    @pl.when(step == pl.num_programs(0) - 1)
    def _():
        grad, sums = norm_back(one_ref[...], vec_ref[1:2], d_two_ref[...] + acc_ref[...])
        d_one_ref[...] = grad
        sums_ref[...] = sums


def state_back_kernel(
    sequences, d_one_ref, w_ref, jq_ref, trig_ref, att_ref, den_ref, num_ref, dden_ref, state_ref
):
    d_att = dot(d_one_ref[...].astype(BF16), w_ref[...], NT)
    cosine, sine = trig_ref[0], trig_ref[1]
    segment = jq_ref.shape[0] // sequences
    for pair in range(WIDE // PAIR):
        lanes = slice(pair * PAIR, (pair + 1) * PAIR)
        feature = softplus(jq_ref[:, lanes])
        query_cos, query_sin = feature * cosine, feature * sine
        d_num = d_att[:, lanes] / den_ref[:, lanes]
        d_den = -head_sum(d_num * att_ref[:, lanes])
        num_ref[:, lanes] = d_num
        dden_ref[:, lanes] = d_den
        maps_s = split(jnp.concatenate([query_cos, query_sin], axis=1))
        num_s = split(d_num)
        sum_cos, sum_sin = query_cos * d_den, query_sin * d_den
        for number in range(sequences):
            rows = slice(number * segment, (number + 1) * segment)
            sums = jnp.concatenate(
                [
                    jnp.sum(sum_cos[rows], axis=0, keepdims=True),
                    jnp.sum(sum_sin[rows], axis=0, keepdims=True),
                ],
                axis=1,
            )
            state_ref[number, pair] = pack_state(
                dot3(cut(maps_s, rows), cut(num_s, rows), TN), sums
            )


def inner_back_kernel(
    sequences, at_ref, jq_ref, jk_ref, jv_ref, trig_ref, num_ref, dden_ref, *rest
):
    *state_refs, dq_ref, dk_ref, dv_ref = rest
    cosine, sine, inside = trig_ref[0], trig_ref[1], trig_ref[2]
    tokens = jq_ref.shape[0]
    segment = tokens // sequences
    keep = causal(tokens, sequences)
    first_two = lanes_of_first((tokens, 2 * PAIR))
    first = lanes_of_first((tokens, PAIR))
    for pair in range(WIDE // PAIR):
        lanes = slice(pair * PAIR, (pair + 1) * PAIR)
        query = jq_ref[:, lanes]
        query_maps = two_maps(softplus(query), cosine, sine)
        query_low = query_maps.astype(BF16)
        key_low = two_maps(softplus(jk_ref[:, lanes]) * inside, cosine, sine).astype(BF16)
        value = jv_ref[:, lanes]
        d_num, d_den = num_ref[:, lanes], dden_ref[:, lanes]
        num_s = split(d_num)
        moved = pltpu.roll(d_den, HEAD, 1) * (1.0 / HEAD)
        d_query, d_key, d_value = [], [], []
        for head in range(2):
            if head == 0:
                masked = jnp.where(first_two, query_maps, 0.0)
                ones = jnp.where(first, value, 1.0)
                joint = jnp.where(first, d_num, moved)
            else:
                masked = jnp.where(first_two, 0.0, query_maps)
                ones = jnp.where(first, 1.0, value)
                joint = jnp.where(first, moved, d_num)
            scores = jnp.where(keep, dot(masked.astype(BF16), key_low, NT), 0.0).astype(BF16)
            grads = jnp.where(keep, dot3(split(joint), split(ones), NT), 0.0).astype(BF16)
            d_query.append(dot(grads, key_low))
            d_key.append(dot(grads, query_low, TN))
            d_value.append(dot(scores, num_s[0], TN))
        d_query_maps = jnp.where(first_two, d_query[0], d_query[1])
        d_key_maps = jnp.where(first_two, d_key[0], d_key[1])
        from_state = []
        for number in range(sequences):
            rows = slice(number * segment, (number + 1) * segment)
            full, sum_cos, sum_sin = unpack_state(add_states(at_ref, state_refs, number, pair, False))
            more = dot3(cut(num_s, rows), split(full), NT)
            part = d_den[rows]
            from_state.append(
                more + jnp.concatenate([part * sum_cos, part * sum_sin], axis=1)
            )
        d_query_maps = d_query_maps + (
            from_state[0] if sequences == 1 else jnp.concatenate(from_state, axis=0)
        )
        dq_ref[:, lanes] = sigmoid(query) * (
            d_query_maps[:, :PAIR] * cosine + d_query_maps[:, PAIR:] * sine
        )
        dk_ref[:, lanes] = d_key_maps[:, :PAIR] * cosine + d_key_maps[:, PAIR:] * sine
        dv_ref[:, lanes] = jnp.where(first, d_value[0], d_value[1])


def joined_back_kernel(
    sequences, scan, at_ref, dq_ref, dk_ref, dv_ref, jk_ref, jv_ref, trig_ref,
    wq_ref, wk_ref, wv_ref, d_one_ref, *rest,
):
    state_refs, (up_ref, mine_ref, sum_ref, *other_refs, acc_ref, join_ref) = rest[:scan], rest[scan:]
    step = pl.program_id(0)
    steps = 3
    cosine, sine, inside = trig_ref[0], trig_ref[1], trig_ref[2]
    segment = jk_ref.shape[0] // sequences
    keys, values = [], []
    for pair in range(WIDE // PAIR):
        lanes = slice(pair * PAIR, (pair + 1) * PAIR)
        key = jk_ref[:, lanes]
        maps_s = split(two_maps(softplus(key) * inside, cosine, sine))
        value_s = split(jv_ref[:, lanes])
        d_key, d_value = [], []
        for number in range(sequences):
            rows = slice(number * segment, (number + 1) * segment)
            full, sum_cos, sum_sin = unpack_state(add_states(at_ref, state_refs, number, pair, True))
            full_s = split(full)
            back = dot3(cut(value_s, rows), full_s, NT)
            d_key.append(
                (back[:, :PAIR] + sum_cos) * cosine[rows] + (back[:, PAIR:] + sum_sin) * sine[rows]
            )
            d_value.append(dot3(cut(maps_s, rows), full_s))
        d_key = d_key[0] if sequences == 1 else jnp.concatenate(d_key, axis=0)
        d_value = d_value[0] if sequences == 1 else jnp.concatenate(d_value, axis=0)
        keys.append(inside * sigmoid(key) * (dk_ref[:, lanes] + d_key))
        values.append(dv_ref[:, lanes] + d_value)
    three = (dq_ref[...], jnp.concatenate(keys, axis=1), jnp.concatenate(values, axis=1))
    part = (
        dot(three[0].astype(BF16), wq_ref[...], NT)
        + dot(three[1].astype(BF16), wk_ref[...], NT)
        + dot(three[2].astype(BF16), wv_ref[...], NT)
    )
    for at in range(steps):

        @pl.when(step == at)
        def _(at=at):
            for group, block in enumerate(three):
                begin = (group * steps + at) * WIDE
                join_ref[:, begin : begin + WIDE] = block

    @pl.when(step == 0)
    def _():
        acc_ref[...] = d_one_ref[...] + part

    @pl.when(step > 0)
    def _():
        acc_ref[...] += part

    @pl.when(step == steps - 1)
    def _():
        up_ref[...] = acc_ref[...]
        sum_ref[...] = jnp.sum(join_ref[...], axis=0, keepdims=True)
        chips = mine_ref.shape[0]
        part, part_one = join_ref.shape[1] // (2 * chips), d_one_ref.shape[1] // (2 * chips)
        for core in range(2):

            @pl.when(at_ref[place_of("seq", 1)] == core)
            def _(core=core):
                for block in range(2 * chips):
                    others = other_refs[0] if len(other_refs) == 1 else other_refs[block // 2]
                    ref = mine_ref if block % 2 == core else others
                    ref[block // 2 % ref.shape[0]] = jnp.concatenate(
                        [
                            join_ref[:, block * part : (block + 1) * part],
                            d_one_ref[:, block * part_one : (block + 1) * part_one],
                        ],
                        axis=1,
                    )


def feed_weights_kernel(chips, packed, first, at_ref, *refs):
    mine, theirs, rest = refs[: 2 * chips], refs[2 * chips : 4 * chips], refs[4 * chips :]
    up_ref, bias_ref, down_ref, up_keep_ref, up_send_ref, *down_refs = rest
    pairs = list(zip(mine[:chips], mine[chips:])) + list(zip(theirs[:chips], theirs[chips:]))
    up, down, bias = up_ref[...], down_ref[...], bias_ref[...]
    normed, errors, ups, acts = [], [], [], []
    for n_ref, e_ref in pairs:
        n, e = n_ref[...].astype(BF16), e_ref[...].astype(BF16)
        act, slope = gelu_both(dot(n, up) + bias)
        normed.append(n)
        errors.append(e)
        ups.append((slope * dot(e, down, NT)).astype(BF16))
        acts.append(act.astype(BF16))
    normed, errors, ups, acts = (jnp.concatenate(parts, axis=0) for parts in (normed, errors, ups, acts))
    d_up = dot(normed, ups, TN)
    d_down = dot(acts, errors, TN)

    def down_piece(x, z, rows):
        groups = blocks // 2
        lanes = d_down.shape[1] // groups
        top, begin = x * groups * rows, z * lanes
        columns = d_down[:, begin : begin + lanes]
        return jnp.concatenate([columns[top + at * rows : top + (at + 1) * rows] for at in range(groups)], axis=1)

    if first == 0:
        halves, unused, rows, unused = up_keep_ref.shape
        blocks = 2 * halves
        for mine in range(2):

            @pl.when(at_ref[place_of("dp", 1)] == mine)
            def _(mine=mine):
                for block in range(blocks):
                    ref = up_keep_ref if block % 2 == mine else up_send_ref
                    ref[block // 2, 0] = d_up[block * rows : (block + 1) * rows]
                    ref[block // 2, 1] = down_piece(block % 2, block // 2, rows)

        return
    halves, rows, unused = up_keep_ref.shape
    blocks = 2 * halves
    for mine in range(2):

        @pl.when(at_ref[place_of("dp", first)] == mine)
        def _(mine=mine):
            for block in range(blocks):
                ref = up_keep_ref if block // first % 2 == mine else up_send_ref
                ref[block // (2 * first) * first + block % first] = d_up[block * rows : (block + 1) * rows]

    if not packed:
        down_refs[0][...] = d_down
        return
    keep_ref, send_ref = down_refs
    others, unused, rows, unused = keep_ref.shape
    for z in range(2):

        @pl.when(at_ref[place_of("dp", 2)] == z)
        def _(z=z):
            for low, ref in ((z, keep_ref), (1 - z, send_ref)):
                for x in range(2):
                    for high in range(others):
                        ref[high, x] = down_piece(x, 2 * high + low, rows)


def attention_weights_kernel(
    rows, many, at_ref, x_ref, x_other_ref, a_ref, a_other_ref, d_ref, *outs
):
    others, outs = outs[:many], outs[many:]
    chips = d_ref.shape[0]
    part = 3 * d_ref.shape[2] // 4
    both = (x_ref, x_other_ref), (a_ref, a_other_ref)
    inputs = [jnp.concatenate([r[...].astype(BF16) for r in refs], axis=0) for refs in both]
    grads = []
    for chip in range(chips):
        other = others[0][chip] if many == 1 else others[chip][0]
        errors = jnp.concatenate([d_ref[chip].astype(BF16), other.astype(BF16)], axis=0)
        grads.append(
            jnp.concatenate(
                [dot(inputs[0], errors[:, :part], TN), dot(inputs[1], errors[:, part:], TN)], axis=1
            )
        )
    by_y, by_x = outs[:2] if rows else (), outs[-2:] if len(outs) == 4 or not rows else ()
    high, blocks = by_y[0].shape[:2] if by_y else (chips // 2, 2 * by_x[0].shape[1])
    more = by_x[0].shape[2] if by_x else 0
    size = rows + more
    for y in range(2 if by_y else 0):

        @pl.when(at_ref[place_of("seq", 2)] == y)
        def _(y=y):
            for low, ref in ((y, by_y[0]), (1 - y, by_y[1])):
                for upper in range(high):
                    for block in range(blocks):
                        ref[upper, block] = grads[2 * upper + low][block * size : block * size + rows]

    for x in range(2 if by_x else 0):

        @pl.when(at_ref[place_of("dp", 1)] == x)
        def _(x=x):
            for parity, ref in ((x, by_x[0]), (1 - x, by_x[1])):
                for chip in range(chips):
                    for block in range(blocks // 2):
                        begin = (2 * block + parity) * size + rows
                        ref[chip, block] = grads[chip][begin : begin + more]


def gate_kernel(out_ref):
    out_ref[...] = jnp.zeros_like(out_ref)


def swap(value, axis, stride):
    return lax.ppermute(value, axis, [(i, i ^ stride) for i in range(lax.axis_size(axis))])


def strides(count):
    found, stride = [], 1
    while stride < count:
        found.append(stride)
        stride *= 2
    return found


def bit(axis, stride):
    return (lax.axis_index(axis) // stride) % 2


def places():
    found = [lax.axis_index("seq")]
    for axis in ("seq", "dp"):
        found += [bit(axis, stride) for stride in strides(lax.axis_size(axis))]
    return jnp.stack(found).astype(jnp.int32)


def place_of(axis, stride):
    spot = 1 + strides(lax.axis_size(axis)).index(stride)
    return spot if axis == "seq" else spot + len(strides(lax.axis_size("seq")))


def scan_states(total, order=None):
    steps = strides(lax.axis_size("seq"))
    others = []
    for stride in steps:
        others.append(swap(total, "seq", stride))
        if stride < steps[-1]:
            total = total + others[-1] if order is None else add(order, total, others[-1])
    return others


def add_states(at_ref, refs, number, pair, backward):
    total = None
    for step, ref in enumerate(refs):
        part = ref[number, pair]
        part = jnp.where((at_ref[1 + step] == 0) == backward, part, jnp.zeros_like(part))
        total = part if total is None else total + part
    return total


def gather_chips(value):
    held = [value]
    for stride in reversed(strides(lax.axis_size("seq"))[1:]):
        held = held + [swap(part, "seq", stride) for part in held]
    return held


def gather_cores(held):
    return held + [swap(part, "seq", 1) for part in held]


def halve_kernel(at_ref, *refs):
    kept_ref, sent_ref = refs[-2:]
    for at in range(kept_ref.shape[1]):
        keep_mine, recv_mine, keep_other, recv_other = refs[4 * at : 4 * at + 4]
        kept_ref[:, at] = keep_mine[...] + recv_mine[...]
        sent_ref[:, at] = keep_other[...] + recv_other[...]


def add_kernel(one_ref, two_ref, out_ref):
    out_ref[...] = one_ref[...] + two_ref[...]


class Scatter:
    def __init__(self, order, place, keep, send, steps):
        self.order, self.place, self.keep, self.steps = order, place, keep, list(steps)
        self.recv = self.swap(send)

    def swap(self, send):
        axis, stride, self.at = self.steps.pop(0)
        return swap(send, axis, stride)

    def done(self):
        return not self.steps

    def fits(self, other):
        return self.keep.shape == other.keep.shape and self.steps == other.steps

    def advance(self, *others):
        axis, stride, at = self.steps[0]
        shape = self.keep.shape
        rows, lanes = shape[-2:]
        outer = math.prod(shape[:at]) * shape[at] // 2
        inner = math.prod(shape[at + 1 : -2])
        flat = (outer, 2, inner, rows, lanes)
        parts = (self,) + others
        pieces = 2 if rows % 16 == 0 and outer < 4 else 1
        block = (None, None, inner, rows // pieces, lanes)
        spot = place_of(axis, stride)
        mine = spec(block, lambda a, r, at: (a, at[spot], 0, r, 0))
        other = spec(block, lambda a, r, at: (a, 1 - at[spot], 0, r, 0))
        out = spec((None, inner, len(parts), rows // pieces, lanes), lambda a, r, at: (a, 0, 0, r, 0))
        given = []
        for part in parts:
            given += [part.keep.reshape(flat), part.recv.reshape(flat)] * 2
        kept, sent = self.order.call(
            halve_kernel,
            (outer, pieces),
            [mine, mine, other, other] * len(parts),
            [out, out],
            [shaped((outer, inner, len(parts), rows, lanes))] * 2,
            1,
            prefetch=1,
            name="halve",
        )(self.place, *given)
        left = shape[:at] + (shape[at] // 2,) + shape[at + 1 : -2] + (len(parts), rows, lanes)
        if len(parts) == 1:
            left = left[:-3] + left[-2:]
        self.keep = kept.reshape(left)
        self.recv = self.swap(sent.reshape(left))
        for part in others:
            part.steps = []

    def last(self):
        rows, lanes = self.keep.shape[-2:]
        shape = (-1, rows, lanes)
        return [part.reshape(shape) for part in (self.keep, self.recv) if part is not None]


def add(order, one, two, at=None):
    if at is None:
        given = out = whole(one.shape)
        shape = one.shape
    else:
        shape = one.shape[1:]
        given = spec((None,) + shape, lambda g: (at,) + (0,) * len(shape))
        out = whole(shape)
    return order.call(add_kernel, (1,), [given] * 2, [out], [shaped(shape)], 1, name="add")(one, two)[0]


def vector_kernel(layers, *refs):
    out_ref = refs[-1]
    out_ref[...] = jnp.zeros_like(out_ref)
    width = out_ref.shape[1]
    for layer in range(layers):
        qkv_ref, up_ref, one_ref, two_ref = refs[4 * layer : 4 * layer + 4]
        rows = []
        for ref in (qkv_ref, up_ref):
            rows += [ref[0:1, at : at + width] for at in range(0, ref.shape[1], width)]
        rows += [one_ref[0:1], two_ref[0:1], one_ref[2:3], one_ref[1:2], two_ref[2:3], two_ref[1:2]]
        for at, row in enumerate(rows):
            out_ref[layer * VECTOR + at : layer * VECTOR + at + 1] = row


def finish_kernel(counts, *refs):
    vector_ref, qkv_ref, out_ref, up_ref, down_ref, *vector_refs = refs[-9:]
    width = vector_ref.shape[1]
    begin = 0
    for ref in vector_refs:
        many = ref.shape[1] // width
        for layer in range(len(counts)):
            for at in range(many):
                row = layer * VECTOR + begin + at
                ref[layer : layer + 1, at * width : (at + 1) * width] = vector_ref[row : row + 1]
        begin += many
    part = qkv_ref.shape[2]
    given = list(refs)
    for layer, many in enumerate(counts):
        sums = []
        for number in many:
            sums.append(given[:number])
            given = given[number:]
        down, given = given[0], given[1:]
        begin = 0
        for parts in sums[:-1]:
            for piece in range(parts[0].shape[0]):
                total = sum(part[piece] for part in parts[1:]) + parts[0][piece]
                rows = total.shape[0]
                qkv_ref[layer, begin : begin + rows] = total[:, :part]
                out_ref[layer, begin : begin + rows] = total[:, part:]
                begin += rows
        up_ref[layer] = sum(part[0] for part in sums[-1][1:]) + sums[-1][0][0]
        rows, lanes = down.shape
        across = down_ref.shape[2]
        for at in range(lanes // across):
            down_ref[layer, at * rows : (at + 1) * rows] = down[:, at * across : (at + 1) * across]


def scatter_down_whole(value):
    seq, dp = lax.axis_size("seq"), lax.axis_size("dp")
    value = lax.all_to_all(value, "seq", split_axis=1, concat_axis=0, tiled=True)
    value = value.reshape(dp, value.shape[0] // dp, value.shape[1])
    for stride in strides(dp):
        mine = bit("dp", stride)
        pairs = value.reshape((value.shape[0] // 2, 2) + value.shape[1:])
        keep = lax.dynamic_index_in_dim(pairs, mine, 1, keepdims=False)
        send = lax.dynamic_index_in_dim(pairs, 1 - mine, 1, keepdims=False)
        value = keep + swap(send, "dp", stride)
    return value[0]


def transpose_down(value):
    seq, dp = lax.axis_size("seq"), lax.axis_size("dp")
    pairs = []
    for z in range(seq):
        for x in range(2):
            for s in range(seq):
                pairs.append((s * dp + 2 * z + x, z * dp + 2 * s + x))
    return lax.ppermute(value, ("seq", "dp"), pairs)


def on_device(
    tokens, lengths, w_qkv, b_qkv, output_weight, w_up, b_up, w_down, gains, shifts, cotangent
):
    sequences, segment, width = tokens.shape
    layers, hidden = b_up.shape
    seq = lax.axis_size("seq")
    count = sequences * segment
    groups = width // WIDE
    pairs = width // PAIR
    position = lax.axis_index("seq") * segment + jnp.arange(segment, dtype=jnp.int32)
    length_col = lengths[:, None]
    inside = (position[None, :] < length_col).astype(F32)
    phases = (
        math.pi
        / 2
        * jnp.minimum(position[None, :], length_col - 1).astype(F32)
        / length_col.astype(F32)
    )
    trig = jnp.stack([jnp.cos(phases), jnp.sin(phases), inside]).reshape(3, count, 1)
    trig = jnp.broadcast_to(trig, (3, count, PAIR))
    b_qkv = b_qkv[:, None, :]
    b_up = b_up[:, None, :]

    rows = (count, width)
    wide = spec((count, WIDE), lambda g, *_: (0, g))
    state_spec = spec((sequences, WIDE // PAIR, STATE, PAIR), lambda g, *_: (0, g, 0, 0))
    state_shape = shaped((sequences, pairs, STATE, PAIR))
    trig_spec = whole((3, count, PAIR))
    full = whole(rows)
    vec_spec = whole((8, width))
    acc = pltpu.VMEM(rows, F32)
    attention_flops = 2 * count * count * 256 * 12

    def qkv_spec(layer, part):
        return spec((None, width, WIDE), lambda g, *_: (layer, 0, part * groups + g))

    def bias_spec(layer, part):
        return spec((None, 1, WIDE), lambda g, *_: (layer, 0, part * groups + g))

    def rows_of(*vectors):
        stacked = jnp.stack(vectors)
        return jnp.concatenate([stacked, jnp.zeros((8 - len(vectors), width), F32)])

    stream, stream_low = tokens.reshape(rows), tokens.reshape(rows)
    saved = []
    block = min(768, hidden)
    order = Order()
    call = order.call
    place = places()
    waiting = []
    for layer in range(layers):
        shift, gain = shifts[layer], gains[layer]
        vec_one = rows_of(shift[:width], gain[:width], shift[width : 2 * width])
        vec_two = rows_of(shift[2 * width : 3 * width], gain[width:], shift[3 * width :])
        key, value, total = call(
            functools.partial(key_value_kernel, sequences),
            (groups,),
            [full, qkv_spec(layer, 1), qkv_spec(layer, 2), bias_spec(layer, 1), bias_spec(layer, 2), trig_spec],
            [wide, wide, state_spec],
            [shaped(rows), shaped(rows), state_shape],
            4 * count * width * width,
            name="key_value",
            after=waiting,
        )(stream_low, w_qkv, w_qkv, b_qkv, b_qkv, trig)
        before = scan_states(total, order)
        stream_other = swap(stream.astype(F32), "seq", 1)
        crossing = saved[-1][0][1:] if saved else []
        query, numer, denom, *crossing = call(
            functools.partial(query_kernel, sequences),
            (groups,),
            [full, qkv_spec(layer, 0), bias_spec(layer, 0), wide, wide, trig_spec],
            [wide, wide, wide],
            [shaped(rows), shaped(rows), shaped(rows)],
            2 * count * width * width + 5 * attention_flops,
            name="query",
            carry=crossing,
        )(stream_low, w_qkv, b_qkv, key, value, trig)
        if saved:
            saved[-1][0][1:] = crossing
            saved[-1][-1].extend(swap(part, "seq", 1) for part in crossing)
        attended, den, one, normed = call(
            functools.partial(attend_kernel, sequences, len(before)),
            (groups,),
            [wide, wide, wide, trig_spec,
             spec((None, WIDE, width), lambda g, at, layer=layer: (layer, g, 0)), full, vec_spec]
            + [state_spec] * len(before),
            [wide, wide, full, full],
            [shaped(rows)] * 4,
            4 * count * width * width,
            scratch=[acc],
            prefetch=1,
            name="attend",
        )(place, query, numer, denom, trig, output_weight, stream, vec_one, *before)
        stream_in = stream
        attended_other = swap(attended, "seq", 1)
        normed_chips = gather_chips(normed)
        pre, two, stream, stream_low = call(
            feed_forward_kernel,
            (hidden // block,),
            [full, spec((None, width, block), lambda g, layer=layer: (layer, 0, g)),
             spec((None, 1, block), lambda g, layer=layer: (layer, 0, g)),
             spec((None, block, width), lambda g, layer=layer: (layer, g, 0)), vec_spec],
            [spec((count, block), lambda g: (0, g)), full, full, full],
            [shaped((count, hidden)), shaped(rows), shaped(rows), shaped(rows, BF16)],
            4 * count * width * hidden,
            scratch=[acc],
            name="feed_forward",
            after=[stream_other],
        )(normed, w_up, b_up, w_down, vec_two)
        normed_cores = [swap(normed, "seq", 1)]
        waiting = [attended_other, normed_cores[0]]
        saved.append(
            (normed_chips, stream_in, stream_other, query, key, value, before, attended, attended_other,
             den, one, pre, two, vec_one, vec_two, normed_cores)
        )
    mixed = stream_low.reshape(tokens.shape)

    upstream = cotangent.reshape(rows)
    chips, dp = seq // 2, lax.axis_size("dp")
    lanes = 4 * width // seq
    slot = hidden // seq
    size = width // dp
    uppers = [int(size * part) // 8 * 8 for part in BY_Y]
    packed = dp == 2 * seq
    down_shape = (seq // 2, 2, slot // (2 * seq), width) if packed else (slot, width)
    down_count = 2 if packed else 1
    up_shape = (dp // 2, size, slot)
    d_shape = (chips, count, lanes)
    x_and_z = [("dp", stride) for stride in strides(dp)]
    above = [("seq", stride) for stride in strides(seq)[1:]]
    work = [dict() for _ in range(layers)]

    def norm_step(layer):
        now = work[layer]
        normed_chips, *unused, two, vec_one, vec_two, normed_cores = saved[layer]
        now["d_two"], now["sums_two"] = call(
            second_norm_kernel,
            (1,),
            [full, full, vec_spec],
            [full, vec_spec],
            [shaped(rows), shaped((8, width))],
            count * width * 20,
            name="second_norm",
            after=waiting + saved[layer - 1][-1][1:] if layer == layers - 1 else (),
        )(upstream, two, vec_two)
        now["errors"] = gather_chips(now["d_two"])
        now["error_core"] = swap(now["d_two"], "seq", 1)

    def feed_step(layer):
        now = work[layer]
        (normed_chips, stream_in, stream_other, query, key, value, before, attended, attended_other,
         den, one, pre, two, vec_one, vec_two, unused) = saved[layer]
        now["d_one"], now["sums_one"], now["bias_up"] = call(
            feed_back_kernel,
            (hidden // block,),
            [full, spec((None, block, width), lambda g: (layer, g, 0)),
             spec((None, width, block), lambda g: (layer, 0, g)),
             spec((count, block), lambda g: (0, g)), full, vec_spec],
            [full, vec_spec, spec((1, block), lambda g: (0, g))],
            [shaped(rows), shaped((8, width)), shaped((1, hidden))],
            4 * count * width * hidden,
            scratch=[acc],
            name="feed_back",
        )(now["d_two"], w_down, w_up, pre, one, vec_one)

    def state_step(layer):
        now = work[layer]
        (normed_chips, stream_in, stream_other, query, key, value, before, attended, attended_other,
         den, one, pre, two, vec_one, vec_two, unused) = saved[layer]
        now["d_num"], now["d_den"], now["d_state"] = call(
            functools.partial(state_back_kernel, sequences),
            (groups,),
            [full, spec((None, WIDE, width), lambda g: (layer, g, 0)),
             wide, trig_spec, wide, wide],
            [wide, wide, state_spec],
            [shaped(rows), shaped(rows), state_shape],
            4 * count * width * width,
            name="state_back",
        )(now["d_one"], output_weight, query, trig, attended, den)

    def scan_step(layer):
        work[layer]["after"] = scan_states(work[layer]["d_state"], order)

    def inner_step(layer):
        now = work[layer]
        (normed_chips, stream_in, stream_other, query, key, value, before, attended, attended_other,
         den, one, pre, two, vec_one, vec_two, unused) = saved[layer]
        now["inner"] = call(
            functools.partial(inner_back_kernel, sequences),
            (groups,),
            [wide, wide, wide, trig_spec, wide, wide] + [state_spec] * len(before),
            [wide, wide, wide],
            [shaped(rows)] * 3,
            15 * attention_flops,
            prefetch=1,
            name="inner_back",
            after=saved[layer][0][1:] if layer == layers - 1 else (),
        )(place, query, key, value, trig, now["d_num"], now["d_den"], *before)

    def gate(held):
        unused, *held = call(
            gate_kernel, (1,), [], [whole((8, PAIR))], [shaped((8, PAIR))], 0, name="gate", carry=held
        )()
        return unused, held

    def gate_step(layer):
        now = work[layer]
        normed_chips, *unused, normed_cores = saved[layer]
        held = now["errors"][1:]
        if layer == layers - 1:
            held = normed_chips[1:] + held
        unused, held = gate(held)
        if layer == layers - 1:
            normed_chips[1:] = held[: chips - 1]
            normed_cores.extend(swap(part, "seq", 1) for part in normed_chips[1:])
        now["errors"][1:] = held[1 - chips :]
        now["error_cores"] = [swap(part, "seq", 1) for part in now["errors"][1:]]

    def feed_weights_step(layer):
        now = work[layer]
        first = UP_FIRST[layer] if packed else 1
        mine = saved[layer][0] + now["errors"]
        theirs = saved[layer][-1] + [now["error_core"]] + now["error_cores"]
        shapes = [(dp // 2, 2, size, width)] * 2 if first == 0 else [up_shape] * 2 + [down_shape] * down_count
        up_keep, up_send, *downs = call(
            functools.partial(feed_weights_kernel, chips, packed, first),
            (1,),
            [full] * (4 * chips)
            + [spec((None, width, slot), lambda g, at: (layer, 0, at[0])),
               spec((None, 1, slot), lambda g, at: (layer, 0, at[0])),
               spec((None, slot, width), lambda g, at: (layer, at[0], 0))],
            [whole(shape) for shape in shapes],
            [shaped(shape) for shape in shapes],
            8 * count * width * hidden,
            prefetch=1,
            vmem=56,
            name="feed_weights",
        )(place, *mine, *theirs, w_up, b_up, w_down)
        if first == 0:
            now["up"] = Scatter(order, place, up_keep, up_send, [("dp", stride, 0) for stride in strides(dp)])
            return
        parts = (dp // (2 * first), first) + up_shape[1:]
        steps = [("dp", first, 0)] + [("dp", stride, 1) for stride in strides(first)]
        steps += [("dp", stride, 0) for stride in strides(dp) if stride > first]
        now["up"] = Scatter(order, place, up_keep.reshape(parts), up_send.reshape(parts), steps)
        if packed:
            steps = [("dp", 2, 0), ("dp", 1, 1)] + [("dp", 2 * stride, 0) for stride in strides(seq)[1:]]
            now["dn"] = Scatter(order, place, *downs, steps)
        else:
            now["dn"] = scatter_down_whole(*downs)

    def joined_step(layer):
        nonlocal upstream
        now = work[layer]
        (normed_chips, stream_in, stream_other, query, key, value, before, attended, attended_other,
         den, one, pre, two, vec_one, vec_two, unused) = saved[layer]
        sends = [(1,) + d_shape[1:]] * chips if layer == 0 else [d_shape]
        upstream, now["d_mine"], now["bias_qkv"], *d_sends = call(
            functools.partial(joined_back_kernel, sequences, len(now["after"])),
            (groups,),
            [wide, wide, wide, wide, wide, trig_spec,
             qkv_spec(layer, 0), qkv_spec(layer, 1), qkv_spec(layer, 2), full]
            + [state_spec] * len(now["after"]),
            [full, whole(d_shape), whole((1, 3 * width))] + [whole(shape) for shape in sends],
            [shaped(rows), shaped(d_shape), shaped((1, 3 * width))] + [shaped(shape) for shape in sends],
            6 * count * width * width,
            scratch=[acc, pltpu.VMEM((count, 3 * width), F32)],
            prefetch=1,
            name="joined_back",
        )(place, *now["inner"], key, value, trig, w_qkv, w_qkv, w_qkv, now["d_one"], *now["after"])
        now["d_other"] = [swap(part, "seq", 1) for part in d_sends]

    def attention_weights_step(layer):
        now = work[layer]
        (normed_chips, stream_in, stream_other, query, key, value, before, attended, attended_other,
         den, one, pre, two, vec_one, vec_two, unused) = saved[layer]
        upper = uppers[layer]
        y_shape = (chips // 2, dp, upper, lanes)
        x_shape = (chips, dp // 2, size - upper, lanes)
        shapes = ([y_shape] * 2 if upper else []) + ([x_shape] * 2 if upper < size else [])
        found = call(
            functools.partial(attention_weights_kernel, upper, len(now["d_other"])),
            (1,),
            [full] * 4 + [whole(d_shape)] + [whole(part.shape) for part in now["d_other"]],
            [whole(shape) for shape in shapes],
            [shaped(shape) for shape in shapes],
            8 * count * width * width,
            prefetch=1,
            name="attention_weights",
        )(place, stream_in, stream_other, attended, attended_other, now["d_mine"], *now["d_other"])
        if upper:
            now["by"] = Scatter(
                order, place, *found[:2],
                [(*step, 0) for step in above] + [(*step, 1) for step in x_and_z],
            )
        if upper < size:
            now["bx"] = Scatter(
                order, place, *found[-2:],
                [(*x_and_z[0], 1)] + [(*step, 0) for step in above] + [(*step, 1) for step in x_and_z[1:]],
            )

    def move(layer, name):
        now = work[layer]
        if name == "ud" and UP_FIRST[layer] == 0 and packed:
            name = "up"
        if name in ("ud", "bb"):
            first, second = (now.get(part) for part in {"ud": ("up", "dn"), "bb": ("by", "bx")}[name])
            both = isinstance(first, Scatter) and isinstance(second, Scatter)
            if both and not first.done() and first.fits(second):
                first.advance(second)
                del now["dn" if name == "ud" else "bx"]
            else:
                move(layer, "up" if name == "ud" else "by")
                move(layer, "dn" if name == "ud" else "bx")
            return
        scatter = now.get(name)
        if name == "sx":
            order.ready = now["after"][-1:]
        elif name == "dx":
            order.ready = [now["down"]] if "down" in now else []
        elif name == "ba":
            joint = now.get("by") or now["bx"]
            if joint.done() and joint.recv is not None and not ("by" in now and "bx" in now):
                joint.keep, joint.recv = add(order, *joint.last()), None
        elif name == "dt":
            if packed and "down" not in now:
                held = (now.get("dn") or now["up"]).last()
                now["down"] = transpose_down(add(order, *held, at=held[0].shape[0] - 1))
        elif isinstance(scatter, Scatter) and not scatter.done():
            scatter.advance()

    steps = {
        "sn": norm_step, "fb": feed_step, "sb": state_step, "sc": scan_step, "ib": inner_step,
        "ga": gate_step, "fw": feed_weights_step, "jb": joined_step, "aw": attention_weights_step,
    }
    hops = [("dp", stride) for stride in strides(dp)[1:]] + [("seq", stride) for stride in strides(seq)]
    hops.append(("dp", 1))
    summed = moving = None
    for word in PLAN:
        word, unused, wait = word.partition("+")
        name, layer = word[:2], int(word[2:]) - 1
        order.wait = float(wait or 0)
        if name == "ve":
            if summed is None:
                pieces = []
                for now in work:
                    pieces += [now["bias_qkv"], now["bias_up"], now["sums_one"], now["sums_two"]]
                shape = (layers * VECTOR, width)
                summed = call(
                    functools.partial(vector_kernel, layers), (1,), [whole(p.shape) for p in pieces],
                    [whole(shape)], [shaped(shape)], 1, name="vectors",
                )(*pieces)[0]
            elif moving is not None:
                summed, moving = add(order, summed, moving), None
            if hops:
                moving = swap(summed, *hops.pop(0))
        elif name in steps:
            steps[name](layer)
        else:
            move(layer, name)
    while hops or moving is not None:
        summed = add(order, summed, moving)
        moving = swap(summed, *hops.pop(0)) if hops else None
    for _ in range(2 * len(x_and_z) + len(above)):
        for layer in reversed(range(layers)):
            for name in ("up", "dn", "by", "bx"):
                move(layer, name)
    given, counts = [], []
    for layer in range(layers):
        move(layer, "dt")
        now = work[layer]
        counts.append([])
        for name in ("by", "bx", "up"):
            parts = now[name].last() if name in now else []
            given += parts
            counts[-1] += [len(parts)] if parts else []
        given.append(now["down"] if packed else now["dn"])
    part = 3 * lanes // 4
    out_shapes = [
        shaped((layers, size, part)),
        shaped((layers, size, lanes - part)),
        shaped((layers, size, slot)),
        shaped((layers, hidden // dp, width // seq)),
        shaped((layers, 3 * width)),
        shaped((layers, hidden)),
        shaped((layers, 2 * width)),
        shaped((layers, 4 * width)),
    ]
    given.append(summed)
    outs = call(
        functools.partial(finish_kernel, counts),
        (1,),
        [whole(g.shape) for g in given],
        [whole(o.shape) for o in out_shapes],
        out_shapes,
        1,
        name="finish",
    )(*given)
    return (mixed, upstream.reshape(tokens.shape), *outs)


def solution(mesh):
    in_specs = (
        P("dp", "seq", None),
        P("dp"),
        P(),
        P(),
        P(),
        P(),
        P(),
        P(),
        P(),
        P(),
        P("dp", "seq", None),
    )
    out_specs = (
        P("dp", "seq", None),
        P("dp", "seq", None),
        P(None, "dp", "seq"),
        P(None, "dp", "seq"),
        P(None, "dp", "seq"),
        P(None, "dp", "seq"),
        P(),
        P(),
        P(),
        P(),
    )
    return jax.shard_map(
        on_device, mesh=mesh, in_specs=in_specs, out_specs=out_specs, check_vma=False
    )
```
